128 devices in a mesh: fsdp: 4 (over y), context: 4 (over z_lo, core), tensor: 8 (over x, z_hi).
Axes of the slice: x: 4, y: 4, z: 4 (z_hi: 2, z_lo: 2; z = z_hi * 2 + z_lo), core: 2. Of those that a mesh axis runs over, the one named last changes fastest.
Arguments:
- tokens: bfloat16 [4, 2048, 2048], P('fsdp', 'context'), may hold values from -6 to 6
- segments: int32 [4, 2048], P('fsdp'), may hold values from 0 to 18, as said below
- positions: int32 [4, 2048], P('fsdp'), may hold values from 0 to 2045, as said below
- cotangent: bfloat16 [4, 2048, 2048], P('fsdp', 'context'), may hold values from -6 to 6
- w_query: bfloat16 [2048, 2048], P('fsdp', 'tensor'), may hold values from -0.125 to 0.125
- w_key: bfloat16 [2048, 2048], P('fsdp', 'tensor'), may hold values from -0.125 to 0.125
- w_value: bfloat16 [2048, 2048], P('fsdp', 'tensor'), may hold values from -0.125 to 0.125
- w_output: bfloat16 [2048, 2048], P('tensor', 'fsdp'), may hold values from -0.125 to 0.125
- w_gate: bfloat16 [2048, 8192], P('fsdp', 'tensor'), may hold values from -0.125 to 0.125
- w_up: bfloat16 [2048, 8192], P('fsdp', 'tensor'), may hold values from -0.125 to 0.125
- w_down: bfloat16 [8192, 2048], P('tensor', 'fsdp'), may hold values from -0.0625 to 0.0625
- query_gain: float32 [2048], P('tensor'), may hold values from 0.1 to 1.9
- key_gain: float32 [2048], P('tensor'), may hold values from 0.1 to 1.9
- attn_gain: float32 [2048], replicated, may hold values from 0.5 to 1.5
- mlp_gain: float32 [2048], replicated, may hold values from 0.5 to 1.5
Outputs:
- layer_out: bfloat16 [4, 2048, 2048], P('fsdp', 'context')
- input_grad: float32 [4, 2048, 2048], P('fsdp', 'context')
- grad_query: float32 [2048, 2048], P('fsdp', 'tensor')
- grad_key: float32 [2048, 2048], P('fsdp', 'tensor')
- grad_value: float32 [2048, 2048], P('fsdp', 'tensor')
- grad_output: float32 [2048, 2048], P('tensor', 'fsdp')
- grad_gate: float32 [2048, 8192], P('fsdp', 'tensor')
- grad_up: float32 [2048, 8192], P('fsdp', 'tensor')
- grad_down: float32 [8192, 2048], P('tensor', 'fsdp')
- grad_query_gain: float32 [2048], P('tensor')
- grad_key_gain: float32 [2048], P('tensor')
- grad_attn_gain: float32 [2048], replicated
- grad_mlp_gain: float32 [2048], replicated
The draws below stay inside these ranges and needn't reach their ends.
Inputs may be any that keep to these rules, and one draw needn't show every extreme that they name: `segments`: within each sequence the document numbers start at 0 and rise by 0 or 1 from one token to the next; one document of each sequence begins within its first 512 tokens and ends within its last 512. `positions`: A token's position is 0 at a sequence's start and where the document number rises, else one more than the position of the token before it.
All inputs are finite; a program needn't handle non-finite values.
Results may differ from the reference program's by a relative error of at most 0.025.
Values may be sent and summed in bfloat16 or wider, within the bound.
A program may use at most 192 MiB of HBM per device.

```python
import jax
import jax.numpy as jnp
from jax import lax

D = 2048
HEADS = 16
HEAD_DIM = 128
FF = 8192
TOK_DEV = 512
LENGTH = 2048
NSEQ = 4


def doc_layout(key):
    head_key, tail_key, front_key, back_key = jax.random.split(key, 4)
    where = jnp.arange(LENGTH, dtype=jnp.int32)[None, :]
    which = jnp.arange(NSEQ, dtype=jnp.int32)[:, None]
    reach = TOK_DEV - 1
    shortest = max(2, LENGTH * 60 // 2048)
    longest = max(shortest + 1, LENGTH * 800 // 2048)
    count = LENGTH // shortest + 1
    last_seq = which == NSEQ - 1
    head = jax.random.randint(head_key, (NSEQ, 1), 1, reach + 1)
    head = jnp.where(which == 0, 1, head)
    head = jnp.where(last_seq, reach, head)
    cut = jax.random.randint(tail_key, (NSEQ, 1), 1, reach + 1)
    cut = jnp.where(which == 0, 1, cut)
    cut = jnp.where(last_seq, reach, cut)
    tail = LENGTH - cut
    front_sizes = jax.random.randint(front_key, (NSEQ, count), shortest, longest + 1)
    front_sizes = jnp.where(last_seq, shortest, front_sizes)
    back_sizes = jax.random.randint(back_key, (NSEQ, count), shortest, longest + 1)
    back_sizes = jnp.where(last_seq, shortest, back_sizes)
    front = jnp.cumsum(front_sizes, axis=1) - front_sizes
    back = tail + jnp.cumsum(back_sizes, axis=1) - back_sizes
    spots = where[:, :, None]
    hits_front = jnp.any(spots == front[:, None, :], axis=2) & (where < head)
    hits_back = jnp.any(spots == back[:, None, :], axis=2)
    begins = (where == 0) | (where == head) | (where == tail) | hits_front | hits_back
    numbers = jnp.cumsum(begins.astype(jnp.int32), axis=1) - 1
    first_place = lax.cummax(jnp.where(begins, where, 0), axis=1)
    return (numbers.astype(jnp.int32), (where - first_place).astype(jnp.int32))


def draw_segments(key, part):
    return doc_layout(key)[0]


def draw_positions(key, part):
    return doc_layout(key)[1]


def level_of(own_key, dims, pieces, least, high):
    def one(position, blocks):
        steps = jax.random.uniform(jax.random.fold_in(jax.random.fold_in(own_key, 6), position), (blocks,), jnp.float32, least / len(pieces), high / len(pieces))
        return jnp.repeat(jnp.exp(steps), dims[position] // blocks).reshape((-1,) + (1,) * (len(dims) - position - 1))

    gain = one(*pieces[0])
    for cut in pieces[1:]:
        gain = gain * one(*cut)
    return gain


def centred(key, extent, spread, most, cuts=(), kind=jnp.bfloat16):
    entries = jax.random.normal(key, extent, jnp.float32) * spread
    if len(cuts) > 0:
        entries = level_of(key, extent, cuts, -0.22, 0.18) * entries
    return jnp.clip(entries, min=-most, max=most).astype(kind)


def setup_inputs(seed: int = 0) -> dict:
    key_list = jax.random.split(jax.random.key(seed), 16)
    return {
        "tokens": centred(key_list[0], (NSEQ, LENGTH, D), 1.0, 6.0, ((0, 4), (1, 4))),
        "segments": draw_segments(jax.random.fold_in(key_list[15], 71), 0),
        "positions": draw_positions(jax.random.fold_in(key_list[15], 71), 0),
        "cotangent": centred(key_list[3], (NSEQ, LENGTH, D), 1.0, 6.0, ((0, 4), (1, 4))),
        "w_query": centred(key_list[4], (D, D), D ** -0.5, 0.125, ((0, 4), (1, 8))),
        "w_key": centred(key_list[5], (D, D), D ** -0.5, 0.125, ((0, 4), (1, 8))),
        "w_value": centred(key_list[6], (D, D), D ** -0.5, 0.125, ((0, 4), (1, 8))),
        "w_output": centred(key_list[7], (D, D), D ** -0.5, 0.125, ((0, 8), (1, 4))),
        "w_gate": centred(key_list[8], (D, FF), D ** -0.5, 0.125, ((0, 4), (1, 8))),
        "w_up": centred(key_list[9], (D, FF), D ** -0.5, 0.125, ((0, 4), (1, 8))),
        "w_down": centred(key_list[10], (FF, D), FF ** -0.5, 0.0625, ((0, 8), (1, 4))),
        "query_gain": jnp.clip(1.0 + 0.18 * jax.random.normal(key_list[11], (D,), jnp.float32), 0.1, 1.9),
        "key_gain": jnp.clip(1.0 + 0.18 * jax.random.normal(key_list[12], (D,), jnp.float32), 0.1, 1.9),
        "attn_gain": jnp.clip(1.0 + 0.1 * jax.random.normal(key_list[13], (D,), jnp.float32), 0.5, 1.5),
        "mlp_gain": jnp.clip(1.0 + 0.1 * jax.random.normal(key_list[14], (D,), jnp.float32), 0.5, 1.5),
    }


@jax.custom_vjp
def low(v):
    return lax.optimization_barrier(v.astype(jnp.bfloat16)).astype(jnp.float32)

@jax.custom_vjp
def low_back(v):
    return v

def low_keep(v):
    return (low(v), None)

def low_pass(kept, grad):
    return (grad,)

def back_keep(v):
    return (v, None)

def back_low(kept, grad):
    return (low(grad),)
low.defvjp(low_keep, low_pass)
low_back.defvjp(back_keep, back_low)
eps_norm = 1e-06
rope_base = 500000.0
blocked = -1000000000.0

def mult(left, right):
    return jnp.dot(left, right, precision=lax.Precision.HIGHEST, preferred_element_type=jnp.float32)

def rms_scale(value):
    return lax.rsqrt(lax.optimization_barrier(jnp.mean(value * value, axis=-1, keepdims=True)) + eps_norm)

def rotary(value, places):
    half = value.shape[-1] // 2
    freqs = rope_base ** (-jnp.arange(half, dtype=jnp.float32) * 2.0 / value.shape[-1])
    angle = places.astype(jnp.float32)[:, None] * freqs[None, :]
    cosine = jnp.cos(angle)[:, None, :]
    sine = jnp.sin(angle)[:, None, :]
    first = value[..., :half]
    second = value[..., half:]
    return jnp.concatenate([first * cosine - second * sine, second * cosine + first * sine], axis=-1)

def layer(params, inputs, docs, places):
    wq, wk, wv, wo, wg, wu, wd, qgain, kgain, again, mgain = params
    count_rows = inputs.shape[0]
    q_raw = low_back(mult(inputs, wq))
    k_raw = low_back(mult(inputs, wk))
    v_raw = low_back(mult(inputs, wv))
    q_norm = q_raw * rms_scale(q_raw) * qgain
    k_norm = k_raw * rms_scale(k_raw) * kgain
    q_rot = low(rotary(q_norm.reshape(count_rows, HEADS, HEAD_DIM), places))
    k_rot = low(rotary(k_norm.reshape(count_rows, HEADS, HEAD_DIM), places))
    v_low = low(v_raw).reshape(count_rows, HEADS, HEAD_DIM)
    block = min(count_rows, 512)
    count = count_rows // block
    index = jnp.arange(count_rows, dtype=jnp.int32)
    scale = HEAD_DIM ** (-0.5)

    def attend(item):
        q_block, doc_block, index_block = item
        raw = jnp.einsum('qhd,khd->hqk', q_block, k_rot, precision=lax.Precision.HIGHEST)
        scores = low_back(raw * scale)
        allowed = (doc_block[:, None] == docs[None, :]) & (index[None, :] <= index_block[:, None])
        masked = jnp.where(allowed[None], scores, blocked)
        shifted = masked - lax.optimization_barrier(jnp.max(masked, axis=-1, keepdims=True))
        expo = jnp.exp(shifted)
        probs = low(expo / lax.optimization_barrier(jnp.sum(expo, axis=-1, keepdims=True)))
        return low_back(jnp.einsum('hqk,khd->qhd', probs, v_low, precision=lax.Precision.HIGHEST))
    attended = lax.map(jax.checkpoint(attend), (q_rot.reshape(count, block, HEADS, HEAD_DIM), docs.reshape(count, block), index.reshape(count, block)))
    attended = low(attended.reshape(count_rows, D))
    o_sum = low_back(mult(attended, wo))
    hidden = inputs + o_sum * rms_scale(o_sum) * again
    hidden_low = low(hidden)
    gate = low_back(mult(hidden_low, wg))
    upper = low_back(mult(hidden_low, wu))
    mixed = low(gate * jax.nn.sigmoid(gate) * upper)
    m_sum = low_back(mult(mixed, wd))
    return hidden + m_sum * rms_scale(m_sum) * mgain

def reference(tokens, segments, positions, cotangent, w_query, w_key, w_value, w_output, w_gate, w_up, w_down, query_gain, key_gain, attn_gain, mlp_gain):
    params = tuple((w.astype(jnp.float32) for w in (w_query, w_key, w_value, w_output, w_gate, w_up, w_down, query_gain, key_gain, attn_gain, mlp_gain)))

    def per_sequence(totals, item):
        inputs, docs, places, grads_out = item

        def forward(weights, values):
            return layer(weights, values, docs, places)
        result, pull = jax.vjp(forward, params, inputs.astype(jnp.float32))
        grad_params, grad_inputs = pull(grads_out.astype(jnp.float32))
        totals = jax.tree.map(jnp.add, totals, grad_params)
        return (totals, (result.astype(jnp.bfloat16), grad_inputs))
    zeros = jax.tree.map(jnp.zeros_like, params)
    totals, (outputs, input_grads) = lax.scan(per_sequence, zeros, (tokens, segments, positions, cotangent))
    return (outputs, input_grads, totals[0], totals[1], totals[2], totals[3], totals[4], totals[5], totals[6], totals[7], totals[8], totals[9], totals[10])
```

```python
import jax
import jax.numpy as jnp
import numpy as np
from jax import lax
from jax.experimental import pallas as pl
from jax.experimental.pallas import tpu as pltpu
from jax.sharding import PartitionSpec as P

MESH = pl.DeviceIdType.MESH
BF = jnp.bfloat16
F32 = jnp.float32
HEAD = 128
WIDTH = 2048
ROWS = 512
COLS = 256
BLOCK = 256
CHUNK = 64
HALF = 32
EPS = 1e-06
ROPE_BASE = 500000.0
BLOCKED = -1000000000.0
SCALE = HEAD ** (-0.5)
HIGHEST = lax.Precision.HIGHEST
MIB = 2**20


def mm(a, b):
    return lax.dot_general(a, b, (((1,), (0,)), ((), ())), preferred_element_type=F32)


def mm_nt(a, b):
    return lax.dot_general(a, b, (((1,), (1,)), ((), ())), preferred_element_type=F32)


def mm_tn(a, b):
    return lax.dot_general(a, b, (((0,), (0,)), ((), ())), preferred_element_type=F32)


class Place:
    def __init__(self):
        self.f = lax.axis_index("fsdp")
        self.c = lax.axis_index("context")
        self.t = lax.axis_index("tensor")
        self.x = self.t // 2
        self.zh = self.t % 2
        self.zl = self.c // 2
        self.core = self.c % 2

    def x_at(self, k):
        return (self.x + k + 4) % 4

    def to_x(self, k):
        return {"tensor": self.x_at(k) * 2 + self.zh}

    def to_zh(self):
        return {"tensor": self.x * 2 + 1 - self.zh}

    def to_t(self, k):
        return {"tensor": (self.t + k) % 8}

    def to_y(self, k):
        return {"fsdp": (self.f + k) % 4}

    def to_core(self):
        return {"context": self.zl * 2 + 1 - self.core}

    def to_zl(self):
        return {"context": (1 - self.zl) * 2 + self.core}

    def barrier(self):
        bar = pltpu.get_barrier_semaphore()
        peers = [self.to_t(k) for k in range(1, 8)] + [self.to_y(k) for k in range(1, 4)]
        peers += [self.to_core(), self.to_zl()]
        for peer in peers:
            pl.semaphore_signal(bar, inc=1, device_id=peer, device_id_type=MESH)
        pl.semaphore_wait(bar, len(peers))


class Net:
    def __init__(self, send, recv, local):
        self.send, self.recv, self.loc = send, recv, local
        self.n = 0
        self.k = 0
        self.sent = []

    def put(self, src, dst, peer):
        i = self.n
        self.n += 1
        copy = pltpu.make_async_remote_copy(
            src_ref=src,
            dst_ref=dst,
            send_sem=self.send.at[i],
            recv_sem=self.recv.at[i],
            device_id=peer,
            device_id_type=MESH,
        )
        copy.start()
        self.sent.append(copy)
        return copy

    def local(self, src, dst):
        copy = pltpu.make_async_copy(src, dst, self.loc.at[self.k])
        self.k += 1
        copy.start()
        return copy

    def finish(self):
        for copy in self.sent:
            copy.wait_send()
        self.sent = []


def rows_of(start, size, unit):
    return pl.ds(pl.multiple_of(start, unit), size)


class Reduce:
    def __init__(self, net, me, part, ra, rb, zs, zr, b):
        self.net, self.me, self.part = net, me, part
        self.ra, self.rb, self.zs, self.zr, self.b = ra, rb, zs, zr, b

    def at(self, k, lower=False, size=HALF):
        start = self.b * BLOCK + self.me.x_at(k) * CHUNK + (HALF if lower else 0)
        return rows_of(start, size, HALF)

    def start(self):
        net, me, part, b = self.net, self.me, self.part, self.b
        self.a0 = net.put(part.at[self.at(2)], self.ra.at[b, 0], me.to_x(1))
        self.a1 = net.put(part.at[self.at(2, True)], self.ra.at[b, 1], me.to_x(-1))
        self.b0 = net.put(
            part.at[self.at(1, True)], self.rb.at[b, 0, pl.ds(HALF, HALF)], me.to_x(1)
        )
        self.b1 = net.put(part.at[self.at(-1)], self.rb.at[b, 1, pl.ds(0, HALF)], me.to_x(-1))

    def mid(self):
        net, me, part, b = self.net, self.me, self.part, self.b
        self.a0.wait_recv()
        s = self.at(1)
        part[s] = (part[s].astype(F32) + self.ra[b, 0].astype(F32)).astype(BF)
        self.c0 = net.put(part.at[s], self.rb.at[b, 0, pl.ds(0, HALF)], me.to_x(1))
        self.a1.wait_recv()
        s = self.at(-1, True)
        part[s] = (part[s].astype(F32) + self.ra[b, 1].astype(F32)).astype(BF)
        self.c1 = net.put(part.at[s], self.rb.at[b, 1, pl.ds(HALF, HALF)], me.to_x(-1))

    def cross(self):
        b = self.b
        for copy in (self.b0, self.b1, self.c0, self.c1):
            copy.wait_recv()
        own = self.part[self.at(0, size=CHUNK)].astype(F32)
        total = own + self.rb[b, 0].astype(F32) + self.rb[b, 1].astype(F32)
        self.zs[b] = total.astype(BF)
        self.z = self.net.put(self.zs.at[b], self.zr.at[b], self.me.to_zh())

    def result(self):
        self.z.wait_recv()
        return self.zs[self.b].astype(F32) + self.zr[self.b].astype(F32)


class Gather:
    def __init__(self, net, me, full, b):
        self.net, self.me, self.full, self.b = net, me, full, b

    def at(self, k, lower=False, size=HALF):
        start = self.b * BLOCK + self.me.x_at(k) * CHUNK + (HALF if lower else 0)
        return rows_of(start, size, HALF)

    def send(self, s, k):
        return self.net.put(self.full.at[s], self.full.at[s], self.me.to_x(k))

    def start(self, chunk):
        self.full[self.at(0, size=CHUNK)] = chunk
        self.p0 = self.send(self.at(0), 1)
        self.m0 = self.send(self.at(0, True), -1)
        self.p1 = self.send(self.at(0, True), 1)
        self.m1 = self.send(self.at(0), -1)

    def mid(self):
        self.p0.wait_recv()
        self.f0 = self.send(self.at(-1), 1)
        self.m0.wait_recv()
        self.f1 = self.send(self.at(1, True), -1)

    def end(self):
        for copy in (self.p1, self.m1, self.f0, self.f1):
            copy.wait_recv()


class Weight:
    def __init__(self, net, me, shard, full):
        self.net, self.me = net, me
        self.full = full
        half = shard.shape[0] // 2
        self.s = rows_of(me.core * half, half, 128)
        self.own = net.local(shard, full.at[me.f])
        self.far = [
            net.put(shard.at[self.s], full.at[me.f, self.s], me.to_y(k)) for k in (1, 3, 2)
        ]

    def pass_on(self):
        self.near = []
        for copy, k in zip(self.far, (1, 3, 2), strict=True):
            copy.wait_recv()
            ref = self.full.at[(self.me.f - k + 4) % 4, self.s]
            self.near.append(self.net.put(ref, ref, self.me.to_core()))

    def wait(self):
        for copy in self.near:
            copy.wait_recv()
        self.own.wait()


def rms(value):
    return lax.rsqrt(jnp.mean(value * value, axis=-1, keepdims=True) + EPS)


def rotate(value, cosine, sine):
    return value * cosine + pltpu.roll(value, 64, axis=1) * sine


def rotate_back(value, cosine, sine):
    return value * cosine - pltpu.roll(value, 64, axis=1) * sine


def two_heads(fn, value, cosine, sine):
    return jnp.concatenate(
        [fn(value[:, :HEAD], cosine, sine), fn(value[:, HEAD:], cosine, sine)], axis=1
    )


def pair_of_sums(first, second):
    ones = jnp.ones((8, COLS), F32)

    def total(v):
        return lax.dot_general(
            ones, v, (((1,), (1,)), ((), ())), precision=HIGHEST, preferred_element_type=F32
        )

    row = lax.broadcasted_iota(jnp.int32, (8, ROWS), 0)
    return jnp.where(row < 4, total(first), total(second))


def k1_body(
    tok_h, pos, freqs, qgain, kgain, again,
    wq, wk, wv, wo, wg, wu, wd,
    hid_o, ochunk_o, att_o, qraw_o, kraw_o, sums_o, qrot_o, keys_o, vals_o, lse_o, cos_o, sin_o, low_o,
    wqkv_o, wo_o, wg_o, wu_o, wd_o,
    tok, stat, part, ra, rb, zs, zr, m_s, l_s, acc_s, send, recv, local,
):
    me = Place()
    net = Net(send, recv, local)
    tok_copy = net.local(tok_h, tok)
    me.barrier()
    thirds = [wqkv_o.at[:, :, pl.ds(i * COLS, COLS)] for i in range(3)]
    small = [
        Weight(net, me, w, o) for w, o in zip((wq, wk, wv, wo), thirds + [wo_o], strict=True)
    ]
    big = [Weight(net, me, w, o) for w, o in ((wg, wg_o), (wu, wu_o), (wd, wd_o))]

    here = pos[0:1, pl.ds(pl.multiple_of(me.c * ROWS, ROWS), ROWS)].astype(F32)
    places = jnp.broadcast_to(here, (HEAD, ROWS)).T
    angle = places * freqs[0:1, :]
    lane = lax.broadcasted_iota(jnp.int32, (ROWS, HEAD), 1)
    cos_o[...] = jnp.cos(angle)
    sin = jnp.sin(angle)
    sin_o[...] = jnp.where(lane < HEAD // 2, -sin, sin)
    index = me.c * ROWS + lax.broadcasted_iota(jnp.int32, (ROWS, HEAD), 0)
    low_o[...] = index - places.astype(jnp.int32)

    tok_copy.wait()
    for w in small[:3]:
        w.pass_on()
    for w in small[:3]:
        w.wait()
    qkv = mm(tok[...], wqkv_o[...].reshape(WIDTH, 3 * COLS))
    qraw_o[...] = qkv[:, :COLS]
    kraw_o[...] = qkv[:, COLS : 2 * COLS]
    vals_o[me.c] = qkv[:, 2 * COLS :].astype(BF)
    stat[me.t] = pair_of_sums(qraw_o[...] * qraw_o[...], kraw_o[...] * kraw_o[...])
    stats = [net.put(stat.at[me.t], stat.at[me.t], me.to_t(k)) for k in range(1, 8)]
    v_near = net.put(vals_o.at[me.c], vals_o.at[me.c], me.to_core())
    v_far = net.put(vals_o.at[me.c], vals_o.at[me.c], me.to_zl())
    for copy in stats:
        copy.wait_recv()
    sums_o[...] = jnp.sum(stat[...], axis=0).T
    sums = sums_o[...]
    scale_q = lax.rsqrt(sums[:, 0:1] / WIDTH + EPS)
    scale_k = lax.rsqrt(sums[:, 4:5] / WIDTH + EPS)
    keys_o[me.c] = two_heads(
        rotate, kraw_o[...] * scale_k * kgain[...], cos_o[...], sin_o[...]
    ).astype(BF)
    k_near = net.put(keys_o.at[me.c], keys_o.at[me.c], me.to_core())
    k_far = net.put(keys_o.at[me.c], keys_o.at[me.c], me.to_zl())
    qrot_o[...] = two_heads(
        rotate, qraw_o[...] * scale_q * qgain[...], cos_o[...], sin_o[...]
    ).astype(BF)
    other = (1 - me.zl) * 2 + me.core
    v_far.wait_recv()
    v_on = net.put(vals_o.at[other], vals_o.at[other], me.to_core())
    k_far.wait_recv()
    k_on = net.put(keys_o.at[other], keys_o.at[other], me.to_core())
    small[3].pass_on()
    for copy in (v_near, k_near, v_on, k_on):
        copy.wait_recv()

    sub = 256
    m_s[...] = jnp.full(m_s.shape, 2 * BLOCKED, F32)
    l_s[...] = jnp.zeros(l_s.shape, F32)
    acc_s[...] = jnp.zeros(acc_s.shape, F32)

    def step(i, _):
        j = me.c - i
        k_index = j * ROWS + lax.broadcasted_iota(jnp.int32, (sub, ROWS), 1)
        for r in range(0, ROWS, sub):
            rows = slice(r, r + sub)
            q_index = me.c * ROWS + r + lax.broadcasted_iota(jnp.int32, (sub, ROWS), 0)
            allowed = (k_index >= low_o[rows, 0:1]) & (k_index <= q_index)
            for h in range(2):
                cols = slice(h * HEAD, (h + 1) * HEAD)
                s = mm_nt(qrot_o[rows, cols], keys_o[j, :, cols]) * SCALE
                s = jnp.where(allowed, s, BLOCKED)
                m_old = m_s[h, rows]
                m_new = jnp.maximum(m_old, jnp.max(s, axis=1, keepdims=True))
                p = jnp.exp(s - m_new)
                fade = jnp.exp(m_old - m_new)
                m_s[h, rows] = m_new
                l_s[h, rows] = l_s[h, rows] * fade + jnp.sum(p, axis=1, keepdims=True)
                acc_s[rows, cols] = acc_s[rows, cols] * fade + mm(p.astype(BF), vals_o[j, :, cols])
        return 0

    lax.fori_loop(0, me.c + 1, step, 0)
    for h in range(2):
        cols = slice(h * HEAD, (h + 1) * HEAD)
        att_o[:, cols] = (acc_s[:, cols] / l_s[h]).astype(BF)
        lse_o[h] = m_s[h] + jnp.log(l_s[h])
    small[3].wait()
    sums = [Reduce(net, me, part, ra, rb, zs, zr, b) for b in range(2)]
    for b in range(2):
        rows = slice(b * BLOCK, (b + 1) * BLOCK)
        for f in range(4):
            part[rows, f * 512 : (f + 1) * 512] = mm(att_o[rows], wo_o[f]).astype(BF)
        sums[b].start()
    for s in sums:
        s.mid()
    for s in sums:
        s.cross()
    gathers = [Gather(net, me, hid_o, b) for b in range(2)]
    for b, (s, g) in enumerate(zip(sums, gathers, strict=True)):
        o_sum = s.result()
        ochunk_o[b] = o_sum
        hidden = tok[s.at(0, size=CHUNK)].astype(F32) + o_sum * rms(o_sum) * again[...]
        g.start(hidden.astype(BF))
    for g in gathers:
        g.mid()
    for w in big:
        w.pass_on()
    for g in gathers:
        g.end()
    for w in big:
        w.wait()
    net.finish()


def k1(tokens, positions, freqs, qgain, kgain, again, wq, wk, wv, wo, wg, wu, wd):
    def sds(*shape, dtype=BF):
        return jax.ShapeDtypeStruct(shape, dtype)

    vm, anyw = pl.BlockSpec(memory_space=pltpu.VMEM), pl.BlockSpec(memory_space=pl.ANY)
    outs = [
        (sds(ROWS, WIDTH), vm),
        (sds(2, CHUNK, WIDTH, dtype=F32), vm),
        (sds(ROWS, COLS), vm),
        (sds(ROWS, COLS, dtype=F32), vm),
        (sds(ROWS, COLS, dtype=F32), vm),
        (sds(ROWS, 8, dtype=F32), vm),
        (sds(ROWS, COLS), vm),
        (sds(4, ROWS, COLS), vm),
        (sds(4, ROWS, COLS), vm),
        (sds(2, ROWS, 1, dtype=F32), vm),
        (sds(ROWS, HEAD, dtype=F32), vm),
        (sds(ROWS, HEAD, dtype=F32), vm),
        (sds(ROWS, HEAD, dtype=jnp.int32), vm),
        (sds(4, 512, 3 * COLS), vm),
        (sds(4, COLS, 512), vm),
        (sds(4, 512, 1024), anyw),
        (sds(4, 512, 1024), anyw),
        (sds(4, 1024, 512), anyw),
    ]
    return pl.pallas_call(
        k1_body,
        name="forward_to_hidden",
        out_shape=[s for s, _ in outs],
        out_specs=[s for _, s in outs],
        in_specs=[anyw] + [vm] * 5 + [anyw] * 7,
        scratch_shapes=[
            pltpu.VMEM((ROWS, WIDTH), BF),
            pltpu.VMEM((8, 8, ROWS), F32),
            pltpu.VMEM((ROWS, WIDTH), BF),
            pltpu.VMEM((2, 2, HALF, WIDTH), BF),
            pltpu.VMEM((2, 2, CHUNK, WIDTH), BF),
            pltpu.VMEM((2, CHUNK, WIDTH), BF),
            pltpu.VMEM((2, CHUNK, WIDTH), BF),
            pltpu.VMEM((2, ROWS, 1), F32),
            pltpu.VMEM((2, ROWS, 1), F32),
            pltpu.VMEM((ROWS, COLS), F32),
            pltpu.SemaphoreType.DMA((96,)),
            pltpu.SemaphoreType.DMA((96,)),
            pltpu.SemaphoreType.DMA((16,)),
        ],
        compiler_params=pltpu.CompilerParams(
            collective_id=1, has_side_effects=True, vmem_limit_bytes=56 * MIB
        ),
    )(tokens, positions, freqs, qgain, kgain, again, wq, wk, wv, wo, wg, wu, wd)


class CoreSum:
    def __init__(self, net, me, grad, got):
        self.net, self.me, self.grad, self.got = net, me, grad, got
        self.half = grad.shape[1] // 2
        self.mine = rows_of(me.core * self.half, self.half, 128)

    def start(self):
        theirs = rows_of((1 - self.me.core) * self.half, self.half, 128)
        self.copy = self.net.put(self.grad.at[:, theirs], self.got, self.me.to_core())

    def add(self):
        self.copy.wait_recv()
        for f in range(4):
            here = self.grad[f, self.mine].astype(F32)
            self.grad[f, self.mine] = (here + self.got[f].astype(F32)).astype(BF)


class ShardSum:
    def __init__(self, net, me, halves, own, got, zs, zr, out):
        self.net, self.me, self.halves, self.own = net, me, halves, own
        self.got, self.zs, self.zr, self.out = got, zs, zr, out
        self.mine = rows_of(me.core * zs.shape[0], zs.shape[0], 128)

    def start(self):
        net, me = self.net, self.me
        self.far = [
            net.put(self.halves.at[(me.f + k) % 4], self.got.at[k - 1], me.to_y(k))
            for k in (1, 3, 2)
        ]

    def cross(self):
        for copy in self.far:
            copy.wait_recv()
        total = self.own().astype(F32)
        for k in range(3):
            total = total + self.got[k].astype(F32)
        self.zs[...] = total.astype(BF)
        self.z = self.net.put(self.zs, self.zr, self.me.to_zl())

    def near(self):
        self.z.wait_recv()
        total = self.zs[...].astype(F32) + self.zr[...].astype(F32)
        self.out[self.mine] = total.astype(BF)
        ref = self.out.at[self.mine]
        self.back = self.net.put(ref, ref, self.me.to_core())

    def end(self):
        self.back.wait_recv()


def norm_back(grad, value, factor, gain):
    scaled = grad * gain
    inner = jnp.mean(scaled * value, axis=-1, keepdims=True)
    return factor * scaled - value * (factor * factor * factor * inner)


def k2_body(
    hid_h, cot_h, ochunk, again, mgain, wg_h, wu_h, wd_h,
    out_o, do_o, dhid_o, gdown_o, ggate_h, gup_h, ga_o, gm_o,
    hid, cot, wg, wu, wd, gate, up, mixed, dgate, dup, part, part2, m_full, d_m,
    ra, rb, zs, zr, ra2, rb2, zs2, zr2, rc_d, rc_g, rc_u, ry, yzs, yzr, ga_s, send, recv, local,
):
    me = Place()
    net = Net(send, recv, local)
    pairs = ((hid_h, hid), (wg_h, wg), (wu_h, wu), (wd_h, wd), (cot_h, cot))
    loads = [net.local(a, b) for a, b in pairs]
    me.barrier()
    for copy in loads[:3]:
        copy.wait()
    wide = 256
    sums = [Reduce(net, me, part, ra, rb, zs, zr, b) for b in range(2)]
    for b in range(2):
        rows = slice(b * BLOCK, (b + 1) * BLOCK)
        for n in range(0, 1024, wide):
            cols = slice(n, n + wide)
            g = mm(hid[rows], wg[:, :, cols].reshape(WIDTH, wide))
            u = mm(hid[rows], wu[:, :, cols].reshape(WIDTH, wide))
            gate[rows, cols] = g
            up[rows, cols] = u
            mixed[rows, cols] = (g * jax.nn.sigmoid(g) * u).astype(BF)
        if b == 0:
            loads[3].wait()
        for f in range(4):
            part[rows, f * 512 : (f + 1) * 512] = mm(mixed[rows], wd[f]).astype(BF)
        sums[b].start()
    for s in sums:
        s.mid()
    for s in sums:
        s.cross()
    gathers = [Gather(net, me, m_full, b) for b in range(2)]
    for s, g in zip(sums, gathers, strict=True):
        g.start(s.result().astype(BF))
    loads[4].wait()
    for g in gathers:
        g.mid()

    gm_o[...] = jnp.zeros(gm_o.shape, F32)
    sums = [Reduce(net, me, part2, ra2, rb2, zs2, zr2, b) for b in range(2)]
    for b in range(2):
        rows = slice(b * BLOCK, (b + 1) * BLOCK)
        gathers[b].end()

        def norm_rows(i, _, b=b):
            some = rows_of(b * BLOCK + i * 64, 64, 64)
            m = m_full[some].astype(F32)
            g = cot[some].astype(F32)
            r = rms(m)
            mr = m * r
            out_o[some] = (hid[some].astype(F32) + mr * mgain[...]).astype(BF)
            d_m[some] = norm_back(g, m, r, mgain[...]).astype(BF)
            gm_o[...] += jnp.sum(g * mr, axis=0, keepdims=True)
            return 0

        lax.fori_loop(0, BLOCK // 64, norm_rows, 0)
        for n in range(0, 1024, wide):
            cols = slice(n, n + wide)
            d_mixed = mm_nt(d_m[rows, 0:512], wd[0, cols])
            for f in range(1, 4):
                d_mixed += mm_nt(d_m[rows, f * 512 : (f + 1) * 512], wd[f, cols])
            g = gate[rows, cols]
            sigma = jax.nn.sigmoid(g)
            dgate[rows, cols] = (
                d_mixed * up[rows, cols] * sigma * (1.0 + g * (1.0 - sigma))
            ).astype(BF)
            dup[rows, cols] = (d_mixed * (g * sigma)).astype(BF)
        for f in range(4):
            for n in range(0, 512, wide):
                d_hidden = mm_nt(dgate[rows], wg[f, n : n + wide])
                d_hidden += mm_nt(dup[rows], wu[f, n : n + wide])
                part2[rows, f * 512 + n : f * 512 + n + wide] = d_hidden.astype(BF)
        sums[b].start()

    down, gates, ups = (
        CoreSum(net, me, w, got) for w, got in ((wd, rc_d), (wg, rc_g), (wu, rc_u))
    )
    for f in range(4):
        wd[f] = mm_tn(mixed[...], d_m[:, f * 512 : (f + 1) * 512]).astype(BF)
    down.start()
    for s in sums:
        s.mid()
    down.add()
    shard = ShardSum(
        net, me, wd.at[:, down.mine], lambda: wd[me.f, down.mine], ry, yzs, yzr, gdown_o
    )
    shard.start()
    for f in range(4):
        wg[f] = mm_tn(hid[:, f * 512 : (f + 1) * 512], dgate[...]).astype(BF)
    gates.start()
    for s in sums:
        s.cross()
    for f in range(4):
        wu[f] = mm_tn(hid[:, f * 512 : (f + 1) * 512], dup[...]).astype(BF)
    ups.start()
    gathers = [Gather(net, me, do_o, b) for b in range(2)]
    ga = jnp.zeros((1, WIDTH), F32)
    for b, (s, g) in enumerate(zip(sums, gathers, strict=True)):
        d_hidden = cot[s.at(0, size=CHUNK)].astype(F32) + s.result()
        dhid_o[b] = d_hidden
        o_sum = ochunk[b]
        r = rms(o_sum)
        g.start(norm_back(d_hidden, o_sum, r, again[...]).astype(BF))
        ga += jnp.sum(d_hidden * (o_sum * r), axis=0, keepdims=True)
    ga_s[me.x] = jnp.broadcast_to(ga, (8, WIDTH))
    far = [net.put(ga_s.at[me.x], ga_s.at[me.x], me.to_x(k)) for k in (1, 3, 2)]
    gates.add()
    stores = [net.local(wg.at[:, gates.mine], ggate_h)]
    ups.add()
    stores.append(net.local(wu.at[:, ups.mine], gup_h))
    for g in gathers:
        g.mid()
    for copy in far:
        copy.wait_recv()
    ga_o[...] = jnp.sum(ga_s[...], axis=0)[0:1]
    shard.cross()
    for g in gathers:
        g.end()
    shard.near()
    for copy in stores:
        copy.wait()
    shard.end()
    net.finish()


def k2(hidden, cotangent, ochunk, again, mgain, wg, wu, wd):
    def sds(*shape, dtype=BF):
        return jax.ShapeDtypeStruct(shape, dtype)

    vm, anyw = pl.BlockSpec(memory_space=pltpu.VMEM), pl.BlockSpec(memory_space=pl.ANY)
    outs = [
        (sds(ROWS, WIDTH), vm),
        (sds(ROWS, WIDTH), vm),
        (sds(2, CHUNK, WIDTH, dtype=F32), vm),
        (sds(1024, 512), vm),
        (sds(4, 256, 1024), anyw),
        (sds(4, 256, 1024), anyw),
        (sds(1, WIDTH, dtype=F32), vm),
        (sds(1, WIDTH, dtype=F32), vm),
    ]
    reduce_bufs = [
        pltpu.VMEM((2, 2, HALF, WIDTH), BF),
        pltpu.VMEM((2, 2, CHUNK, WIDTH), BF),
        pltpu.VMEM((2, CHUNK, WIDTH), BF),
        pltpu.VMEM((2, CHUNK, WIDTH), BF),
    ]
    return pl.pallas_call(
        k2_body,
        name="feed_forward",
        out_shape=[s for s, _ in outs],
        out_specs=[s for _, s in outs],
        in_specs=[anyw, anyw, vm, vm, vm, anyw, anyw, anyw],
        scratch_shapes=[
            pltpu.VMEM((ROWS, WIDTH), BF),
            pltpu.VMEM((ROWS, WIDTH), BF),
            pltpu.VMEM((4, 512, 1024), BF),
            pltpu.VMEM((4, 512, 1024), BF),
            pltpu.VMEM((4, 1024, 512), BF),
            pltpu.VMEM((ROWS, 1024), F32),
            pltpu.VMEM((ROWS, 1024), F32),
            pltpu.VMEM((ROWS, 1024), BF),
            pltpu.VMEM((ROWS, 1024), BF),
            pltpu.VMEM((ROWS, 1024), BF),
            pltpu.VMEM((ROWS, WIDTH), BF),
            pltpu.VMEM((ROWS, WIDTH), BF),
            pltpu.VMEM((ROWS, WIDTH), BF),
            pltpu.VMEM((ROWS, WIDTH), BF),
            *reduce_bufs,
            *reduce_bufs,
            pltpu.VMEM((4, 512, 512), BF),
            pltpu.VMEM((4, 256, 1024), BF),
            pltpu.VMEM((4, 256, 1024), BF),
            pltpu.VMEM((3, 512, 512), BF),
            pltpu.VMEM((512, 512), BF),
            pltpu.VMEM((512, 512), BF),
            pltpu.VMEM((4, 8, WIDTH), F32),
            pltpu.SemaphoreType.DMA((64,)),
            pltpu.SemaphoreType.DMA((64,)),
            pltpu.SemaphoreType.DMA((8,)),
        ],
        compiler_params=pltpu.CompilerParams(
            collective_id=2, has_side_effects=True, vmem_limit_bytes=60 * MIB
        ),
    )(hidden, cotangent, ochunk, again, mgain, wg, wu, wd)


def k3_body(
    tok_h, do_h, wqkv, wo, att, qraw, kraw, sums, qrot, keys, vals, lse, cosine, sine, low,
    qgain, kgain, dhid, ga, gm, ggate_h, gup_h,
    ig_o, ggate_o, gup_o, gqkv_o, gout_o, gains_o,
    tok, d_o, d_att, dq, dk, dv, dkv, rkv, skv, rz, stat, dqkv, dn, part, ra, rb, zs, zr,
    own_g, own_u, ry_g, ry_u, zs_g, zr_g, zs_u, zr_u,
    g_out, rc_o, ry_o, zs_o, zr_o, g_qkv, rc_q, ry_q, zs_q, zr_q,
    gy, gz, gzr, gc, gcr, send, recv, local,
):
    me = Place()
    net = Net(send, recv, local)
    pairs = ((do_h, d_o), (tok_h, tok), (ggate_h.at[me.f], own_g), (gup_h.at[me.f], own_u))
    loads = [net.local(a, b) for a, b in pairs]
    me.barrier()
    gates = ShardSum(net, me, ggate_h, lambda: own_g[...], ry_g, zs_g, zr_g, ggate_o)
    ups = ShardSum(net, me, gup_h, lambda: own_u[...], ry_u, zs_u, zr_u, gup_o)
    gates.start()
    ups.start()
    loads[0].wait()
    d = mm_nt(d_o[:, 0:512], wo[0])
    for f in range(1, 4):
        d += mm_nt(d_o[:, f * 512 : (f + 1) * 512], wo[f])
    d_att[...] = d.astype(BF)

    sub = 256
    dq[...] = jnp.zeros(dq.shape, F32)
    dk[...] = jnp.zeros(dk.shape, F32)
    dv[...] = jnp.zeros(dv.shape, F32)

    def step(j, _):
        k_index = j * ROWS + lax.broadcasted_iota(jnp.int32, (sub, ROWS), 1)
        for r in range(0, ROWS, sub):
            rows = slice(r, r + sub)
            q_index = me.c * ROWS + r + lax.broadcasted_iota(jnp.int32, (sub, ROWS), 0)
            allowed = (k_index >= low[rows, 0:1]) & (k_index <= q_index)
            for h in range(2):
                cols = slice(h * HEAD, (h + 1) * HEAD)
                q, k, v = qrot[rows, cols], keys[j, :, cols], vals[j, :, cols]
                e = d_att[rows, cols]
                delta = jnp.sum(
                    e.astype(F32) * att[rows, cols].astype(F32), axis=1, keepdims=True
                )
                s = mm_nt(q, k) * SCALE - lse[h, rows]
                p = jnp.exp(jnp.where(allowed, s, BLOCKED))
                ds = (p * (mm_nt(e, v) - delta)).astype(BF)
                dq[rows, cols] += mm(ds, k)
                dk[j, :, cols] += mm_tn(ds, q)
                dv[j, :, cols] += mm_tn(p.astype(BF), e)
        return 0

    lax.fori_loop(0, me.c + 1, step, 0)
    for j in range(4):
        dkv[j, :, :COLS] = (dk[j] * SCALE).astype(BF)
        dkv[j, :, COLS:] = dv[j].astype(BF)
    swaps = [
        net.put(dkv.at[z * 2 + 1 - me.core], rkv.at[z], me.to_core()) for z in range(2)
    ]
    g_out_sum = CoreSum(net, me, g_out, rc_o)
    for f in range(4):
        g_out[f] = mm_tn(att[...], d_o[:, f * 512 : (f + 1) * 512]).astype(BF)
    g_out_sum.start()
    for copy in swaps:
        copy.wait_recv()
    away, home = 1 - me.zl, me.zl
    skv[...] = (
        dkv[away * 2 + me.core].astype(F32) + rkv[away].astype(F32)
    ).astype(BF)
    kv_far = net.put(skv, rz, me.to_zl())
    scale_q = lax.rsqrt(sums[:, 0:1] / WIDTH + EPS)
    scale_k = lax.rsqrt(sums[:, 4:5] / WIDTH + EPS)
    dn[0] = two_heads(rotate_back, dq[...] * SCALE, cosine[...], sine[...])
    g_out_sum.add()
    outs = ShardSum(
        net, me, g_out.at[:, g_out_sum.mine], lambda: g_out[me.f, g_out_sum.mine],
        ry_o, zs_o, zr_o, gout_o,
    )
    outs.start()
    kv_far.wait_recv()
    d_kv = dkv[home * 2 + me.core].astype(F32) + rkv[home].astype(F32) + rz[...].astype(F32)
    dn[1] = two_heads(rotate_back, d_kv[:, :COLS], cosine[...], sine[...])
    dqkv[:, 2 * COLS :] = d_kv[:, COLS:].astype(BF)
    scaled_q = dn[0] * qgain[...]
    scaled_k = dn[1] * kgain[...]
    stat[me.t] = pair_of_sums(scaled_q * qraw[...], scaled_k * kraw[...])
    stats = [net.put(stat.at[me.t], stat.at[me.t], me.to_t(k)) for k in range(1, 8)]
    gy[me.f] = jnp.zeros((8, WIDTH), F32)
    gy[me.f, 0:1] = ga[...]
    gy[me.f, 1:2] = gm[...]
    gy[me.f, 2:3, :COLS] = jnp.sum(dn[0] * (qraw[...] * scale_q), axis=0, keepdims=True)
    gy[me.f, 2:3, COLS : 2 * COLS] = jnp.sum(
        dn[1] * (kraw[...] * scale_k), axis=0, keepdims=True
    )
    gains = [net.put(gy.at[me.f], gy.at[me.f], me.to_y(k)) for k in (1, 3, 2)]
    for copy in stats:
        copy.wait_recv()
    dots = jnp.sum(stat[...], axis=0).T / WIDTH
    dqkv[:, :COLS] = (
        scale_q * scaled_q - qraw[...] * (scale_q * scale_q * scale_q * dots[:, 0:1])
    ).astype(BF)
    dqkv[:, COLS : 2 * COLS] = (
        scale_k * scaled_k - kraw[...] * (scale_k * scale_k * scale_k * dots[:, 4:5])
    ).astype(BF)

    wide = 256
    tot = [Reduce(net, me, part, ra, rb, zs, zr, b) for b in range(2)]
    for b in range(2):
        rows = slice(b * BLOCK, (b + 1) * BLOCK)
        for f in range(4):
            for n in range(0, 512, wide):
                part[rows, f * 512 + n : f * 512 + n + wide] = mm_nt(
                    dqkv[rows], wqkv[f, n : n + wide]
                ).astype(BF)
        tot[b].start()
    loads[1].wait()
    qkv_sum = CoreSum(net, me, g_qkv, rc_q)
    for f in range(4):
        g_qkv[f] = mm_tn(tok[:, f * 512 : (f + 1) * 512], dqkv[...]).astype(BF)
    qkv_sum.start()
    for s in tot:
        s.mid()
    qkv_sum.add()
    qkvs = ShardSum(
        net, me, g_qkv.at[:, qkv_sum.mine], lambda: g_qkv[me.f, qkv_sum.mine],
        ry_q, zs_q, zr_q, gqkv_o,
    )
    qkvs.start()
    for copy in gains:
        copy.wait_recv()
    gz[...] = gy[0] + gy[1] + gy[2] + gy[3]
    gain_z = net.put(gz, gzr, me.to_zl())
    for s in tot:
        s.cross()
    loads[2].wait()
    gates.cross()
    gain_z.wait_recv()
    gc[...] = gz[...] + gzr[...]
    gain_c = net.put(gc, gcr, me.to_core())
    gathers = [Gather(net, me, ig_o, b) for b in range(2)]
    for b, (s, g) in enumerate(zip(tot, gathers, strict=True)):
        g.start((dhid[b] + s.result()).astype(BF))
    loads[3].wait()
    ups.cross()
    outs.cross()
    for g in gathers:
        g.mid()
    gain_c.wait_recv()
    gains_o[...] = gc[...] + gcr[...]
    gates.near()
    qkvs.cross()
    ups.near()
    outs.near()
    for g in gathers:
        g.end()
    qkvs.near()
    for s in (gates, ups, outs, qkvs):
        s.end()
    net.finish()


def k3(*args):
    def sds(*shape, dtype=BF):
        return jax.ShapeDtypeStruct(shape, dtype)

    vm, anyw = pl.BlockSpec(memory_space=pltpu.VMEM), pl.BlockSpec(memory_space=pl.ANY)

    def buf(*shape, dtype=BF):
        return pltpu.VMEM(shape, dtype)

    def shard_bufs(rows, cols):
        return [buf(3, rows, cols), buf(rows, cols), buf(rows, cols)]

    return pl.pallas_call(
        k3_body,
        name="attention_backward",
        out_shape=[
            sds(ROWS, WIDTH),
            sds(512, 1024),
            sds(512, 1024),
            sds(512, 3 * COLS),
            sds(COLS, 512),
            sds(8, WIDTH, dtype=F32),
        ],
        out_specs=[vm] * 6,
        in_specs=[anyw, anyw] + [vm] * 18 + [anyw, anyw],
        scratch_shapes=[
            buf(ROWS, WIDTH),
            buf(ROWS, WIDTH),
            buf(ROWS, COLS),
            buf(ROWS, COLS, dtype=F32),
            buf(4, ROWS, COLS, dtype=F32),
            buf(4, ROWS, COLS, dtype=F32),
            buf(4, ROWS, 2 * COLS),
            buf(2, ROWS, 2 * COLS),
            buf(ROWS, 2 * COLS),
            buf(ROWS, 2 * COLS),
            buf(8, 8, ROWS, dtype=F32),
            buf(ROWS, 3 * COLS),
            buf(2, ROWS, COLS, dtype=F32),
            buf(ROWS, WIDTH),
            buf(2, 2, HALF, WIDTH),
            buf(2, 2, CHUNK, WIDTH),
            buf(2, CHUNK, WIDTH),
            buf(2, CHUNK, WIDTH),
            buf(256, 1024),
            buf(256, 1024),
            buf(3, 256, 1024),
            buf(3, 256, 1024),
            buf(256, 1024),
            buf(256, 1024),
            buf(256, 1024),
            buf(256, 1024),
            buf(4, COLS, 512),
            buf(4, 128, 512),
            *shard_bufs(128, 512),
            buf(4, 512, 3 * COLS),
            buf(4, 256, 3 * COLS),
            *shard_bufs(256, 3 * COLS),
            buf(4, 8, WIDTH, dtype=F32),
            *[buf(8, WIDTH, dtype=F32) for _ in range(4)],
            pltpu.SemaphoreType.DMA((80,)),
            pltpu.SemaphoreType.DMA((80,)),
            pltpu.SemaphoreType.DMA((8,)),
        ],
        compiler_params=pltpu.CompilerParams(
            collective_id=3, has_side_effects=True, vmem_limit_bytes=60 * MIB
        ),
    )(*args)


def body(
    tokens, segments, positions, cotangent,
    w_query, w_key, w_value, w_output, w_gate, w_up, w_down,
    query_gain, key_gain, attn_gain, mlp_gain,
):
    del segments
    inverse = ROPE_BASE ** (-np.arange(64, dtype=np.float64) * 2.0 / HEAD)
    freqs = jnp.asarray(np.concatenate([inverse, inverse])[None], F32)
    qgain, kgain, again, mgain = (
        g[None] for g in (query_gain, key_gain, attn_gain, mlp_gain)
    )
    (
        hidden, ochunk, att, qraw, kraw, sums, qrot, keys, vals, lse, cosine, sine, low,
        wqkv, wo, wg, wu, wd,
    ) = k1(
        tokens[0], positions, freqs, qgain, kgain, again,
        w_query, w_key, w_value, w_output, w_gate, w_up, w_down,
    )
    out, d_o, dhid, g_down, ggate, gup, ga, gm = k2(
        hidden, cotangent[0], ochunk, again, mgain, wg, wu, wd
    )
    d_in, g_gate, g_up, g_qkv, g_out, gains = k3(
        tokens[0], d_o, wqkv, wo, att, qraw, kraw, sums, qrot, keys, vals, lse, cosine, sine, low,
        qgain, kgain, dhid, ga, gm, ggate, gup,
    )
    g_qkv = g_qkv.astype(F32)
    return (
        out[None],
        d_in.astype(F32)[None],
        g_qkv[:, :COLS],
        g_qkv[:, COLS : 2 * COLS],
        g_qkv[:, 2 * COLS :],
        g_out.astype(F32),
        g_gate.astype(F32),
        g_up.astype(F32),
        g_down.astype(F32),
        gains[2, :COLS],
        gains[2, COLS : 2 * COLS],
        gains[0],
        gains[1],
    )


def solution(mesh):
    in_specs = (
        P("fsdp", "context", None),
        P("fsdp", None),
        P("fsdp", None),
        P("fsdp", "context", None),
        P("fsdp", "tensor"),
        P("fsdp", "tensor"),
        P("fsdp", "tensor"),
        P("tensor", "fsdp"),
        P("fsdp", "tensor"),
        P("fsdp", "tensor"),
        P("tensor", "fsdp"),
        P("tensor"),
        P("tensor"),
        P(),
        P(),
    )
    out_specs = (
        P("fsdp", "context", None),
        P("fsdp", "context", None),
        P("fsdp", "tensor"),
        P("fsdp", "tensor"),
        P("fsdp", "tensor"),
        P("tensor", "fsdp"),
        P("fsdp", "tensor"),
        P("fsdp", "tensor"),
        P("tensor", "fsdp"),
        P("tensor"),
        P("tensor"),
        P(),
        P(),
    )
    return jax.shard_map(body, mesh=mesh, in_specs=in_specs, out_specs=out_specs, check_vma=False)
```

```python
import jax
import jax.numpy as jnp
import numpy as np
from jax import lax
from jax.experimental import pallas as pl
from jax.experimental.pallas import tpu as pltpu
from jax.sharding import PartitionSpec as P

MESH = pl.DeviceIdType.MESH
BF = jnp.bfloat16
F32 = jnp.float32
HEAD = 128
WIDTH = 2048
ROWS = 512
COLS = 256
HIDDEN = 1024
BLOCK = 256
CHUNK = 64
HALF = 32
TILE = 256
EPS = 1e-06
ROPE_BASE = 500000.0
BLOCKED = -1000000000.0
LOG2E = 1.4426950408889634
SCALE = HEAD ** (-0.5)
HIGHEST = lax.Precision.HIGHEST
MIB = 2**20


def mm(a, b):
    return lax.dot_general(a, b, (((1,), (0,)), ((), ())), preferred_element_type=F32)


def mm_nt(a, b):
    return lax.dot_general(a, b, (((1,), (1,)), ((), ())), preferred_element_type=F32)


def mm_tn(a, b):
    return lax.dot_general(a, b, (((0,), (0,)), ((), ())), preferred_element_type=F32)


def rows_of(start, size, unit):
    return pl.ds(pl.multiple_of(start, unit), size)


class Place:
    def __init__(self):
        self.f = lax.axis_index("fsdp")
        self.c = lax.axis_index("context")
        self.t = lax.axis_index("tensor")
        self.x = self.t // 2
        self.zh = self.t % 2
        self.zl = self.c // 2
        self.core = self.c % 2

    def x_at(self, k):
        return (self.x + k + 4) % 4

    def to_x(self, k):
        return {"tensor": self.x_at(k) * 2 + self.zh}

    def to_zh(self):
        return {"tensor": self.x * 2 + 1 - self.zh}

    def to_t(self, k):
        return {"tensor": (self.t + k) % 8}

    def to_y(self, k):
        return {"fsdp": (self.f + k) % 4}

    def to_core(self):
        return {"context": self.zl * 2 + 1 - self.core}

    def to_zl(self):
        return {"context": (1 - self.zl) * 2 + self.core}

    def barrier(self):
        bar = pltpu.get_barrier_semaphore()
        peers = [self.to_t(k) for k in range(1, 8)] + [self.to_y(k) for k in range(1, 4)]
        peers += [self.to_core(), self.to_zl()]
        for peer in peers:
            pl.semaphore_signal(bar, inc=1, device_id=peer, device_id_type=MESH)
        pl.semaphore_wait(bar, len(peers))


class Net:
    def __init__(self, send, recv, local, credit):
        self.send, self.recv, self.loc, self.credit = send, recv, local, credit
        self.n = 0
        self.k = 0
        self.sent = []

    def put(self, src, dst, peer):
        i = self.n
        self.n += 1
        copy = pltpu.make_async_remote_copy(
            src_ref=src,
            dst_ref=dst,
            send_sem=self.send.at[i],
            recv_sem=self.recv.at[i],
            device_id=peer,
            device_id_type=MESH,
        )
        copy.start()
        self.sent.append(copy)
        return copy

    def left(self, *copies):
        for copy in copies:
            copy.wait_send()
            self.sent = [other for other in self.sent if other is not copy]

    def local(self, src, dst):
        copy = pltpu.make_async_copy(src, dst, self.loc.at[self.k])
        self.k += 1
        copy.start()
        return copy

    def finish(self):
        self.left(*list(self.sent))


class Reduce:
    def __init__(self, net, me, part, bufs, b):
        self.net, self.me, self.part, self.b = net, me, part, b
        self.ra, self.rb, self.zs, self.zr = bufs

    def at(self, k, lower=False, size=HALF):
        start = self.b * BLOCK + self.me.x_at(k) * CHUNK + (HALF if lower else 0)
        return rows_of(start, size, HALF)

    def start(self):
        net, me, part, b = self.net, self.me, self.part, self.b
        self.a0 = net.put(part.at[self.at(2)], self.ra.at[b, 0], me.to_x(1))
        self.a1 = net.put(part.at[self.at(2, True)], self.ra.at[b, 1], me.to_x(-1))
        self.b0 = net.put(
            part.at[self.at(1, True)], self.rb.at[b, 0, pl.ds(HALF, HALF)], me.to_x(1)
        )
        self.b1 = net.put(part.at[self.at(-1)], self.rb.at[b, 1, pl.ds(0, HALF)], me.to_x(-1))

    def mid(self):
        net, me, part, b = self.net, self.me, self.part, self.b
        self.a0.wait_recv()
        s = self.at(1)
        part[s] = (part[s].astype(F32) + self.ra[b, 0].astype(F32)).astype(BF)
        self.c0 = net.put(part.at[s], self.rb.at[b, 0, pl.ds(0, HALF)], me.to_x(1))
        self.a1.wait_recv()
        s = self.at(-1, True)
        part[s] = (part[s].astype(F32) + self.ra[b, 1].astype(F32)).astype(BF)
        self.c1 = net.put(part.at[s], self.rb.at[b, 1, pl.ds(HALF, HALF)], me.to_x(-1))

    def cross(self):
        b = self.b
        for copy in (self.b0, self.b1, self.c0, self.c1):
            copy.wait_recv()
        own = self.part[self.at(0, size=CHUNK)].astype(F32)
        total = own + self.rb[b, 0].astype(F32) + self.rb[b, 1].astype(F32)
        self.zs[b] = total.astype(BF)
        self.z = self.net.put(self.zs.at[b], self.zr.at[b], self.me.to_zh())

    def result(self):
        self.z.wait_recv()
        return self.zs[self.b].astype(F32) + self.zr[self.b].astype(F32)

    def left(self):
        self.net.left(self.a0, self.a1, self.b0, self.b1, self.c0, self.c1, self.z)


class Gather:
    def __init__(self, net, me, full, b):
        self.net, self.me, self.full, self.b = net, me, full, b

    def at(self, k, lower=False, size=HALF):
        start = self.b * BLOCK + self.me.x_at(k) * CHUNK + (HALF if lower else 0)
        return rows_of(start, size, HALF)

    def send(self, s, k):
        return self.net.put(self.full.at[s], self.full.at[s], self.me.to_x(k))

    def start(self, chunk):
        self.full[self.at(0, size=CHUNK)] = chunk
        self.p0 = self.send(self.at(0), 1)
        self.m0 = self.send(self.at(0, True), -1)
        self.p1 = self.send(self.at(0, True), 1)
        self.m1 = self.send(self.at(0), -1)

    def mid(self):
        self.p0.wait_recv()
        self.f0 = self.send(self.at(-1), 1)
        self.m0.wait_recv()
        self.f1 = self.send(self.at(1, True), -1)

    def end(self):
        for copy in (self.p1, self.m1, self.f0, self.f1):
            copy.wait_recv()

    def left(self):
        self.net.left(self.p0, self.m0, self.p1, self.m1, self.f0, self.f1)


class Weight:
    def __init__(self, net, me, shard, full):
        self.net, self.me, self.full = net, me, full
        half = shard.shape[0] // 2
        self.s = rows_of(me.core * half, half, 128)
        self.own = net.local(shard, full.at[me.f])
        self.far = [
            net.put(shard.at[self.s], full.at[me.f, self.s], me.to_y(k)) for k in (1, 3, 2)
        ]

    def pass_on(self):
        self.near = []
        for copy, k in zip(self.far, (1, 3, 2), strict=True):
            copy.wait_recv()
            ref = self.full.at[(self.me.f - k + 4) % 4, self.s]
            self.near.append(self.net.put(ref, ref, self.me.to_core()))

    def wait(self):
        for copy in self.near:
            copy.wait_recv()
        self.own.wait()
        self.net.left(*self.near)


class GradSum:
    def __init__(self, net, me, grad, got, credit, out):
        self.net, self.me, self.grad, self.got = net, me, grad, got
        self.credit, self.out = credit, out
        half = grad.shape[1] // 2
        self.mine = rows_of(me.core * half, half, 128)
        self.theirs = rows_of((1 - me.core) * half, half, 128)

    def start(self):
        self.near = [
            self.net.put(self.grad.at[f, self.theirs], self.got[f], self.me.to_core())
            for f in range(4)
        ]

    def add(self):
        net, me = self.net, self.me
        for f in range(4):
            self.near[f].wait_recv()
            here = self.grad[f, self.mine].astype(F32)
            self.grad[f, self.mine] = (here + self.got[f][...].astype(F32)).astype(BF)
        net.left(*self.near)
        for peer in [me.to_y(k) for k in (1, 3, 2)] + [me.to_zl()]:
            pl.semaphore_signal(self.credit, inc=1, device_id=peer, device_id_type=MESH)

    def spread(self):
        net, me = self.net, self.me
        pl.semaphore_wait(self.credit, 4)
        self.far = [
            net.put(
                self.grad.at[(me.f + k) % 4, self.mine],
                self.grad.at[k - 1, self.theirs],
                me.to_y(k),
            )
            for k in (1, 3, 2)
        ]

    def cross(self):
        for copy in self.far:
            copy.wait_recv()
        me = self.me
        total = self.grad[me.f, self.mine].astype(F32)
        for k in range(3):
            total = total + self.grad[k, self.theirs].astype(F32)
        self.grad[me.f, self.mine] = total.astype(BF)
        self.z = self.net.put(
            self.grad.at[me.f, self.mine], self.grad.at[3, self.theirs], me.to_zl()
        )

    def finish(self):
        self.z.wait_recv()
        me = self.me
        total = self.grad[me.f, self.mine].astype(F32) + self.grad[3, self.theirs].astype(F32)
        self.grad[0, self.theirs] = total.astype(BF)
        final = self.grad.at[0, self.theirs]
        self.store = self.net.local(final, self.out.at[self.mine])
        self.back = self.net.put(final, self.out.at[self.mine], me.to_core())

    def end(self):
        self.store.wait()
        self.back.wait_recv()


def rms(value):
    return lax.rsqrt(jnp.mean(value * value, axis=-1, keepdims=True) + EPS)


def norm_back(grad, value, factor, gain):
    scaled = grad * gain
    inner = jnp.mean(scaled * value, axis=-1, keepdims=True)
    return factor * scaled - value * (factor * factor * factor * inner)


def rotate(value, cosine, sine):
    return value * cosine + pltpu.roll(value, 64, axis=1) * sine


def rotate_back(value, cosine, sine):
    return value * cosine - pltpu.roll(value, 64, axis=1) * sine


def two_heads(fn, value, cosine, sine):
    return jnp.concatenate(
        [fn(value[:, :HEAD], cosine, sine), fn(value[:, HEAD:], cosine, sine)], axis=1
    )


def pair_of_sums(first, second):
    ones = jnp.ones((8, COLS), F32)

    def total(v):
        return lax.dot_general(
            ones, v, (((1,), (1,)), ((), ())), precision=HIGHEST, preferred_element_type=F32
        )

    row = lax.broadcasted_iota(jnp.int32, (8, ROWS), 0)
    return jnp.where(row < 4, total(first), total(second))


def layer_body(
    tok_h, cot_h, pos, freqs, qgain, kgain, again, mgain,
    wq_h, wk_h, wv_h, wo_h, wg_h, wu_h, wd_h,
    out_h, ig_h, gdown_h, ggate_h, gup_h, gqkv_h, gout_h, gains_o,
    tok, cot, wqkv, wo, wg, wu, wd, hid, gate, up, mixed, dgate, dup, part_a, part_b,
    m_full, d_m, do_full, ra0, rb0, zs0, zr0, ra1, rb1, zs1, zr1, ochunk,
    qraw, kraw, sums_s, qrot, keys, vals, att, lse, m_s, l_s, acc, cosine, sine, low,
    stat, stat2, skv, rz, dn, dqkv, d_att, ga_s, gm_s, gy, gz, gzr, gc, gcr,
    send, recv, local, credit, ready,
):
    me = Place()
    net = Net(send, recv, local, credit)
    bufs = ((ra0, rb0, zs0, zr0), (ra1, rb1, zs1, zr1))
    tok_copy = net.local(tok_h, tok)
    cot_copy = net.local(cot_h, cot)
    me.barrier()
    thirds = [wqkv.at[:, :, pl.ds(i * COLS, COLS)] for i in range(3)]
    w_q, w_k, w_v, w_o, w_g, w_u, w_d = (
        Weight(net, me, w, full)
        for w, full in zip(
            (wq_h, wk_h, wv_h, wo_h, wg_h, wu_h, wd_h), [*thirds, wo, wg, wu, wd], strict=True
        )
    )

    def block_rows(b):
        return slice(b * BLOCK, (b + 1) * BLOCK)

    here = pos[0:1, pl.ds(pl.multiple_of(me.c * ROWS, ROWS), ROWS)].astype(F32)
    places = jnp.broadcast_to(here, (HEAD, ROWS)).T
    angle = places * freqs[0:1, :]
    lane = lax.broadcasted_iota(jnp.int32, (ROWS, HEAD), 1)
    cosine[...] = jnp.cos(angle)
    sin = jnp.sin(angle)
    sine[...] = jnp.where(lane < HEAD // 2, -sin, sin)
    index = me.c * ROWS + lax.broadcasted_iota(jnp.int32, (ROWS, HEAD), 0)
    low[...] = index - places.astype(jnp.int32)
    tok_copy.wait()
    for w in (w_q, w_k, w_v):
        w.pass_on()
    for w in (w_q, w_k, w_v):
        w.wait()

    def project():
        qkv = mm(tok[...], wqkv[...].reshape(WIDTH, 3 * COLS))
        qraw[...] = qkv[:, :COLS]
        kraw[...] = qkv[:, COLS : 2 * COLS]
        vals[me.c] = qkv[:, 2 * COLS :].astype(BF)
        stat[me.t] = pair_of_sums(qraw[...] * qraw[...], kraw[...] * kraw[...])

    with jax.named_scope("project"):
        project()
    stats = [net.put(stat.at[me.t], stat.at[me.t], me.to_t(k)) for k in range(1, 8)]
    v_near = net.put(vals.at[me.c], vals.at[me.c], me.to_core())
    v_far = net.put(vals.at[me.c], vals.at[me.c], me.to_zl())
    with jax.named_scope("wait_stats"):
        for copy in stats:
            copy.wait_recv()
    with jax.named_scope("rotate"):
        sums_s[...] = jnp.sum(stat[...], axis=0).T
        scale_q = lax.rsqrt(sums_s[:, 0:1] / WIDTH + EPS)
        scale_k = lax.rsqrt(sums_s[:, 4:5] / WIDTH + EPS)
        keys[me.c] = two_heads(
            rotate, kraw[...] * scale_k * kgain[...], cosine[...], sine[...]
        ).astype(BF)
        k_near = net.put(keys.at[me.c], keys.at[me.c], me.to_core())
        k_far = net.put(keys.at[me.c], keys.at[me.c], me.to_zl())
        q_norm = qraw[...] * (scale_q * (SCALE * LOG2E)) * qgain[...]
        qrot[...] = two_heads(rotate, q_norm, cosine[...], sine[...]).astype(BF)
    other = (1 - me.zl) * 2 + me.core
    with jax.named_scope("wait_keys"):
        v_far.wait_recv()
        v_on = net.put(vals.at[other], vals.at[other], me.to_core())
        k_far.wait_recv()
        k_on = net.put(keys.at[other], keys.at[other], me.to_core())
        w_o.pass_on()
        for copy in (v_near, k_near, v_on, k_on):
            copy.wait_recv()

    m_s[...] = jnp.full(m_s.shape, 2 * BLOCKED, F32)
    l_s[...] = jnp.zeros(l_s.shape, F32)
    acc[...] = jnp.zeros(acc.shape, F32)

    def allowed_keys(j, rows):
        k_index = j * ROWS + lax.broadcasted_iota(jnp.int32, (BLOCK, ROWS), 1)
        first = me.c * ROWS + rows.start
        q_index = first + lax.broadcasted_iota(jnp.int32, (BLOCK, ROWS), 0)
        return (k_index >= low[rows, 0:1]) & (k_index <= q_index)

    def attend(i, _):
        j = me.c - i
        for b in range(2):
            rows = block_rows(b)
            allowed = allowed_keys(j, rows)
            for h in range(2):
                cols = slice(h * HEAD, (h + 1) * HEAD)
                s = jnp.where(allowed, mm_nt(qrot[rows, cols], keys[j, :, cols]), BLOCKED)
                m_old = m_s[h, rows]
                m_new = jnp.maximum(m_old, jnp.max(s, axis=1, keepdims=True))
                p = jnp.exp2(s - m_new)
                fade = jnp.exp2(m_old - m_new)
                m_s[h, rows] = m_new
                l_s[h, rows] = l_s[h, rows] * fade + jnp.sum(p, axis=1, keepdims=True)
                acc[rows, cols] = acc[rows, cols] * fade + mm(p.astype(BF), vals[j, :, cols])
        return 0

    with jax.named_scope("attend"):
        lax.fori_loop(0, me.c + 1, attend, 0)
    for h in range(2):
        cols = slice(h * HEAD, (h + 1) * HEAD)
        att[:, cols] = (acc[:, cols] / l_s[h]).astype(BF)
        lse[h] = m_s[h] + jnp.log2(l_s[h])

    w_o.wait()
    o_sum = [Reduce(net, me, part_a, bufs[0], b) for b in range(2)]
    to_hid = [Gather(net, me, hid, b) for b in range(2)]

    def output_projection(b):
        rows = block_rows(b)
        for f in range(4):
            part_a[rows, f * 512 : (f + 1) * 512] = mm(att[rows], wo[f]).astype(BF)

    def hidden(b):
        value = o_sum[b].result()
        ochunk[b] = value
        own = tok[o_sum[b].at(0, size=CHUNK)].astype(F32)
        to_hid[b].start((own + value * rms(value) * again[...]).astype(BF))

    output_projection(0)
    o_sum[0].start()
    output_projection(1)
    o_sum[0].mid()
    o_sum[1].start()
    w_g.pass_on()
    o_sum[0].cross()
    o_sum[1].mid()
    hidden(0)
    o_sum[1].cross()
    to_hid[0].mid()
    hidden(1)
    w_u.pass_on()
    to_hid[0].end()

    m_sum = [Reduce(net, me, part_b, bufs[1], b) for b in range(2)]
    to_m = [Gather(net, me, m_full, b) for b in range(2)]

    def gates(b, tiles):
        rows = block_rows(b)
        for n in tiles:
            cols = slice(n * TILE, (n + 1) * TILE)
            g = mm(hid[rows], wg[:, :, cols].reshape(WIDTH, TILE))
            u = mm(hid[rows], wu[:, :, cols].reshape(WIDTH, TILE))
            gate[rows, cols] = g
            up[rows, cols] = u
            mixed[rows, cols] = (g * jax.nn.sigmoid(g) * u).astype(BF)

    def down(b):
        rows = block_rows(b)
        for f in range(4):
            part_b[rows, f * 512 : (f + 1) * 512] = mm(mixed[rows], wd[f]).astype(BF)

    w_g.wait()
    w_u.wait()
    with jax.named_scope("gates"):
        gates(0, (0, 1))
    to_hid[1].mid()
    with jax.named_scope("gates"):
        gates(0, (2, 3))
    w_d.pass_on()
    to_hid[1].end()
    w_d.wait()
    down(0)
    m_sum[0].start()
    with jax.named_scope("gates"):
        gates(1, (0, 1, 2, 3))
    m_sum[0].mid()
    down(1)
    m_sum[1].start()
    m_sum[0].cross()
    m_sum[1].mid()
    cot_copy.wait()
    to_m[0].start(m_sum[0].result().astype(BF))
    m_sum[1].cross()
    to_m[0].mid()
    to_m[1].start(m_sum[1].result().astype(BF))
    for s in o_sum:
        s.left()
    for s in m_sum:
        s.left()
    gm_s[...] = jnp.zeros(gm_s.shape, F32)

    h_sum = [Reduce(net, me, part_a, bufs[0], b) for b in range(2)]
    to_do = [Gather(net, me, do_full, b) for b in range(2)]

    def norm_rows(b):
        def some_rows(i, _):
            some = rows_of(b * BLOCK + i * 64, 64, 64)
            m = m_full[some].astype(F32)
            g = cot[some].astype(F32)
            r = rms(m)
            mr = m * r
            part_b[some] = (hid[some].astype(F32) + mr * mgain[...]).astype(BF)
            d_m[some] = norm_back(g, m, r, mgain[...]).astype(BF)
            gm_s[...] += jnp.sum(g * mr, axis=0, keepdims=True)
            return 0

        with jax.named_scope("norm_rows"):
            lax.fori_loop(0, BLOCK // 64, some_rows, 0)
        return net.local(part_b.at[block_rows(b)], out_h.at[block_rows(b)])

    def gates_back(b):
        rows = block_rows(b)
        for n in range(4):
            cols = slice(n * TILE, (n + 1) * TILE)
            d_mixed = mm_nt(d_m[rows, 0:512], wd[0, cols])
            for f in range(1, 4):
                d_mixed += mm_nt(d_m[rows, f * 512 : (f + 1) * 512], wd[f, cols])
            g = gate[rows, cols]
            sigma = jax.nn.sigmoid(g)
            dgate[rows, cols] = (
                d_mixed * up[rows, cols] * sigma * (1.0 + g * (1.0 - sigma))
            ).astype(BF)
            dup[rows, cols] = (d_mixed * (g * sigma)).astype(BF)

    def hidden_back(b):
        rows = block_rows(b)
        for f in range(4):
            for n in range(0, 512, TILE):
                d = mm_nt(dgate[rows], wg[f, n : n + TILE])
                d += mm_nt(dup[rows], wu[f, n : n + TILE])
                part_a[rows, f * 512 + n : f * 512 + n + TILE] = d.astype(BF)

    stores = []
    to_m[0].end()
    stores.append(norm_rows(0))
    to_m[1].mid()
    with jax.named_scope("gates_back"):
        gates_back(0)
    with jax.named_scope("hidden_back"):
        hidden_back(0)
    h_sum[0].start()
    to_m[1].end()
    stores.append(norm_rows(1))
    with jax.named_scope("gates_back"):
        gates_back(1)
    h_sum[0].mid()
    with jax.named_scope("hidden_back"):
        hidden_back(1)
    h_sum[1].start()

    def columns(ref, f):
        return ref.at[:, pl.ds(f * 512, 512)]

    def quarter(ref, f, cols=1024):
        return ref.at[pl.ds(f // 2 * 256, 256), pl.ds(f % 2 * 1024, cols)]

    def half(pair, f):
        return pair[f // 2].at[pl.ds(f % 2 * 256, 256)]

    g_down = GradSum(
        net, me, wd, [columns(m_full, f) for f in range(4)], credit.at[0], gdown_h
    )
    g_gate = GradSum(net, me, wg, [quarter(d_m, f) for f in range(4)], credit.at[1], ggate_h)
    g_up = GradSum(
        net, me, wu, [half((mixed, dgate), f) for f in range(4)], credit.at[2], gup_h
    )
    for g in to_m:
        g.left()
    pl.semaphore_signal(ready, inc=1, device_id=me.to_core(), device_id_type=MESH)
    with jax.named_scope("grad_down"):
        for f in range(4):
            wd[f] = mm_tn(mixed[...], d_m[:, f * 512 : (f + 1) * 512]).astype(BF)
    pl.semaphore_wait(ready, 1)
    g_down.start()
    h_sum[0].cross()
    h_sum[1].mid()
    g_down.add()
    with jax.named_scope("grad_gate"):
        for f in range(4):
            wg[f] = mm_tn(hid[:, f * 512 : (f + 1) * 512], dgate[...]).astype(BF)
    g_gate.start()

    def back_to_o(b):
        d_hidden = cot[h_sum[b].at(0, size=CHUNK)].astype(F32) + h_sum[b].result()
        value = ochunk[b]
        r = rms(value)
        to_do[b].start(norm_back(d_hidden, value, r, again[...]).astype(BF))
        ochunk[b] = d_hidden
        return jnp.sum(d_hidden * (value * r), axis=0, keepdims=True)

    ga = back_to_o(0)
    h_sum[1].cross()
    g_down.spread()
    with jax.named_scope("grad_up"):
        for f in range(4):
            wu[f] = mm_tn(hid[:, f * 512 : (f + 1) * 512], dup[...]).astype(BF)
    to_do[0].mid()
    g_gate.add()
    g_up.start()
    ga = ga + back_to_o(1)
    ga_s[me.x] = jnp.broadcast_to(ga, (8, WIDTH))
    ga_far = [net.put(ga_s.at[me.x], ga_s.at[me.x], me.to_x(k)) for k in (1, 3, 2)]
    g_gate.spread()
    g_up.add()
    g_up.spread()
    to_do[0].end()

    dk, dv, dq = gate, up, acc
    dk[...] = jnp.zeros(dk.shape, F32)
    dv[...] = jnp.zeros(dv.shape, F32)
    dq[...] = jnp.zeros(dq.shape, F32)

    def attended_back(b):
        rows = block_rows(b)
        d = mm_nt(do_full[rows, 0:512], wo[0])
        for f in range(1, 4):
            d += mm_nt(do_full[rows, f * 512 : (f + 1) * 512], wo[f])
        d_att[rows] = d.astype(BF)

    def attend_back(b, h):
        rows = block_rows(b)
        cols = slice(h * HEAD, (h + 1) * HEAD)
        q, e = qrot[rows, cols], d_att[rows, cols]
        delta = jnp.sum(e.astype(F32) * att[rows, cols].astype(F32), axis=1, keepdims=True)

        def step(j, _):
            k, v = keys[j, :, cols], vals[j, :, cols]
            s = jnp.where(allowed_keys(j, rows), mm_nt(q, k) - lse[h, rows], BLOCKED)
            p = jnp.exp2(s)
            ds = (p * (mm_nt(e, v) - delta)).astype(BF)
            there = pl.ds(pl.multiple_of(j * COLS + h * HEAD, HEAD), HEAD)
            dq[rows, cols] += mm(ds, k)
            dk[:, there] += mm_tn(ds, q)
            dv[:, there] += mm_tn(p.astype(BF), e)
            return 0

        with jax.named_scope("attend_back"):
            lax.fori_loop(0, me.c + 1, step, 0)

    attended_back(0)
    attend_back(0, 0)
    to_do[1].mid()
    attend_back(0, 1)
    to_do[1].end()
    attended_back(1)
    attend_back(1, 0)
    attend_back(1, 1)

    def kv(j, ref_pair=(mixed, dgate)):
        return ref_pair[j // 2].at[:, pl.ds(j % 2 * 512, 512)]

    for j in range(4):
        kv(j)[:, :COLS] = (dk[:, j * COLS : (j + 1) * COLS] * (1.0 / LOG2E)).astype(BF)
        kv(j)[:, COLS:] = dv[:, j * COLS : (j + 1) * COLS].astype(BF)

    def two(z, core):
        return (mixed, dgate)[z].at[:, pl.ds(pl.multiple_of(core * 512, 512), 512)]

    theirs = [dup.at[:, pl.ds(z * 512, 512)] for z in range(2)]
    swaps = [net.put(two(z, 1 - me.core), theirs[z], me.to_core()) for z in range(2)]
    for g in to_do:
        g.left()
    g_out = GradSum(
        net, me, wo, [d_m.at[pl.ds(f * 128, 128), pl.ds(0, 512)] for f in range(4)],
        credit.at[3], gout_h,
    )
    with jax.named_scope("grad_output"):
        for f in range(4):
            wo[f] = mm_tn(att[...], do_full[:, f * 512 : (f + 1) * 512]).astype(BF)
    g_out.start()
    with jax.named_scope("wait_swaps"):
        for copy in swaps:
            copy.wait_recv()
    own = [two(z, me.core)[...].astype(F32) + theirs[z][...].astype(F32) for z in range(2)]
    upper_half = me.zl == 1
    skv[...] = jnp.where(upper_half, own[0], own[1]).astype(BF)
    kv_far = net.put(skv, rz, me.to_zl())
    with jax.named_scope("rotate_back"):
        dn[0] = two_heads(rotate_back, dq[...] * SCALE, cosine[...], sine[...])
    g_out.add()
    for copy in ga_far:
        copy.wait_recv()
    g_out.spread()
    with jax.named_scope("wait_kv"):
        kv_far.wait_recv()
    own = [two(z, me.core)[...].astype(F32) + theirs[z][...].astype(F32) for z in range(2)]
    d_kv = jnp.where(upper_half, own[1], own[0]) + rz[...].astype(F32)
    with jax.named_scope("rotate_back"):
        dn[1] = two_heads(rotate_back, d_kv[:, :COLS], cosine[...], sine[...])
        dqkv[:, 2 * COLS :] = d_kv[:, COLS:].astype(BF)
        scaled_q = dn[0] * qgain[...]
        scaled_k = dn[1] * kgain[...]
        stat2[me.t] = pair_of_sums(scaled_q * qraw[...], scaled_k * kraw[...])
    stats = [net.put(stat2.at[me.t], stat2.at[me.t], me.to_t(k)) for k in range(1, 8)]
    scale_q = lax.rsqrt(sums_s[:, 0:1] / WIDTH + EPS)
    scale_k = lax.rsqrt(sums_s[:, 4:5] / WIDTH + EPS)
    gy[me.f] = jnp.zeros((8, WIDTH), F32)
    gy[me.f, 0:1] = jnp.sum(ga_s[...], axis=0)[0:1]
    gy[me.f, 1:2] = gm_s[...]
    gy[me.f, 2:3, :COLS] = jnp.sum(dn[0] * (qraw[...] * scale_q), axis=0, keepdims=True)
    gy[me.f, 2:3, COLS : 2 * COLS] = jnp.sum(
        dn[1] * (kraw[...] * scale_k), axis=0, keepdims=True
    )
    gains = [net.put(gy.at[me.f], gy.at[me.f], me.to_y(k)) for k in (1, 3, 2)]
    with jax.named_scope("wait_stats"):
        for copy in stats:
            copy.wait_recv()
    dots = jnp.sum(stat2[...], axis=0).T / WIDTH
    dqkv[:, :COLS] = (
        scale_q * scaled_q - qraw[...] * (scale_q * scale_q * scale_q * dots[:, 0:1])
    ).astype(BF)
    dqkv[:, COLS : 2 * COLS] = (
        scale_k * scaled_k - kraw[...] * (scale_k * scale_k * scale_k * dots[:, 4:5])
    ).astype(BF)

    for copy in stores:
        copy.wait()
    x_sum = [Reduce(net, me, part_b, bufs[1], b) for b in range(2)]
    to_ig = [Gather(net, me, m_full, b) for b in range(2)]

    def input_back(b):
        rows = block_rows(b)
        for f in range(4):
            for n in range(0, 512, TILE):
                d = mm_nt(dqkv[rows], wqkv[f, n : n + TILE])
                part_b[rows, f * 512 + n : f * 512 + n + TILE] = d.astype(BF)

    with jax.named_scope("input_back"):
        input_back(0)
    x_sum[0].start()
    with jax.named_scope("input_back"):
        input_back(1)
    x_sum[0].mid()
    x_sum[1].start()
    g_qkv = GradSum(
        net, me, wqkv, [quarter(do_full, f, 3 * COLS) for f in range(4)], credit.at[4], gqkv_h
    )
    with jax.named_scope("grad_qkv"):
        for f in range(4):
            wqkv[f] = mm_tn(tok[:, f * 512 : (f + 1) * 512], dqkv[...]).astype(BF)
    g_qkv.start()
    x_sum[0].cross()
    x_sum[1].mid()
    g_qkv.add()
    g_down.cross()
    for copy in gains:
        copy.wait_recv()
    gz[...] = gy[0] + gy[1] + gy[2] + gy[3]
    gain_z = net.put(gz, gzr, me.to_zl())
    g_qkv.spread()

    def input_grad(b):
        to_ig[b].start((ochunk[b] + x_sum[b].result()).astype(BF))

    input_grad(0)
    x_sum[1].cross()
    g_gate.cross()
    gain_z.wait_recv()
    gc[...] = gz[...] + gzr[...]
    gain_c = net.put(gc, gcr, me.to_core())
    to_ig[0].mid()
    g_down.finish()
    input_grad(1)
    g_up.cross()
    g_gate.finish()
    to_ig[0].end()
    stores = [net.local(m_full.at[block_rows(0)], ig_h.at[block_rows(0)])]
    to_ig[1].mid()
    g_out.cross()
    gain_c.wait_recv()
    gains_o[...] = gc[...] + gcr[...]
    g_qkv.cross()
    g_up.finish()
    g_out.finish()
    to_ig[1].end()
    stores.append(net.local(m_full.at[block_rows(1)], ig_h.at[block_rows(1)]))
    g_qkv.finish()
    for g in (g_down, g_gate, g_up, g_out, g_qkv):
        g.end()
    for copy in stores:
        copy.wait()
    net.finish()


def sds(*shape, dtype=BF):
    return jax.ShapeDtypeStruct(shape, dtype)


VM = pl.BlockSpec(memory_space=pltpu.VMEM)
ANY = pl.BlockSpec(memory_space=pl.ANY)


def layer(*args):
    def buf(*shape, dtype=BF):
        return pltpu.VMEM(shape, dtype)

    def wide(*shape):
        return pltpu.VMEM(shape, F32)

    reduce_bufs = [
        buf(2, 2, HALF, WIDTH),
        buf(2, 2, CHUNK, WIDTH),
        buf(2, CHUNK, WIDTH),
        buf(2, CHUNK, WIDTH),
    ]
    return pl.pallas_call(
        layer_body,
        name="layer",
        out_shape=[
            sds(ROWS, WIDTH),
            sds(ROWS, WIDTH),
            sds(HIDDEN, 512),
            sds(512, HIDDEN),
            sds(512, HIDDEN),
            sds(512, 3 * COLS),
            sds(COLS, 512),
            sds(8, WIDTH, dtype=F32),
        ],
        out_specs=[ANY] * 7 + [VM],
        in_specs=[ANY, ANY] + [VM] * 6 + [ANY] * 7,
        scratch_shapes=[
            buf(ROWS, WIDTH),
            buf(ROWS, WIDTH),
            buf(4, 512, 3 * COLS),
            buf(4, COLS, 512),
            buf(4, 512, HIDDEN),
            buf(4, 512, HIDDEN),
            buf(4, HIDDEN, 512),
            buf(ROWS, WIDTH),
            wide(ROWS, HIDDEN),
            wide(ROWS, HIDDEN),
            buf(ROWS, HIDDEN),
            buf(ROWS, HIDDEN),
            buf(ROWS, HIDDEN),
            buf(ROWS, WIDTH),
            buf(ROWS, WIDTH),
            buf(ROWS, WIDTH),
            buf(ROWS, WIDTH),
            buf(ROWS, WIDTH),
            *reduce_bufs,
            *reduce_bufs,
            wide(2, CHUNK, WIDTH),
            wide(ROWS, COLS),
            wide(ROWS, COLS),
            wide(ROWS, 8),
            buf(ROWS, COLS),
            buf(4, ROWS, COLS),
            buf(4, ROWS, COLS),
            buf(ROWS, COLS),
            wide(2, ROWS, 1),
            wide(2, ROWS, 1),
            wide(2, ROWS, 1),
            wide(ROWS, COLS),
            wide(ROWS, HEAD),
            wide(ROWS, HEAD),
            pltpu.VMEM((ROWS, HEAD), jnp.int32),
            wide(8, 8, ROWS),
            wide(8, 8, ROWS),
            buf(ROWS, 2 * COLS),
            buf(ROWS, 2 * COLS),
            wide(2, ROWS, COLS),
            buf(ROWS, 3 * COLS),
            buf(ROWS, COLS),
            wide(4, 8, WIDTH),
            wide(1, WIDTH),
            wide(4, 8, WIDTH),
            *[wide(8, WIDTH) for _ in range(4)],
            pltpu.SemaphoreType.DMA((256,)),
            pltpu.SemaphoreType.DMA((256,)),
            pltpu.SemaphoreType.DMA((32,)),
            pltpu.SemaphoreType.REGULAR((5,)),
            pltpu.SemaphoreType.REGULAR,
        ],
        compiler_params=pltpu.CompilerParams(
            collective_id=1, has_side_effects=True, vmem_limit_bytes=63 * MIB
        ),
    )(*args)


def finish_body(*refs):
    arrays, gains, rest = refs[:7], refs[7], refs[8:]
    outs, rest = rest[:9], rest[9:]
    g_outs, rest = rest[:4], rest[4:]
    ins, wides, (in_sem, out_sem) = rest[:7], rest[7:14], rest[14:]
    loads = []
    for i, (a, b) in enumerate(zip(arrays, ins, strict=True)):
        loads.append(pltpu.make_async_copy(a, b, in_sem.at[i]))
        loads[-1].start()
    stores = []

    def store(src, i):
        stores.append(pltpu.make_async_copy(src, outs[i], out_sem.at[i]))
        stores[-1].start()

    for i in range(7):
        loads[i].wait()
        if i == 0:
            store(ins[0], 0)
        elif i == 6:
            for part in range(3):
                wides[6][part] = ins[6][:, part * COLS : (part + 1) * COLS].astype(F32)
                store(wides[6].at[part], 6 + part)
        else:
            wides[i][...] = ins[i][...].astype(F32)
            store(wides[i], i)
    g_outs[0][...] = gains[0:1]
    g_outs[1][...] = gains[1:2]
    g_outs[2][...] = gains[2:3, :COLS]
    g_outs[3][...] = gains[2:3, COLS : 2 * COLS]
    for copy in stores:
        copy.wait()


def finish(*args):
    shapes = [
        (ROWS, WIDTH),
        (ROWS, WIDTH),
        (HIDDEN, 512),
        (512, HIDDEN),
        (512, HIDDEN),
        (COLS, 512),
        (512, 3 * COLS),
    ]
    outs = [sds(ROWS, WIDTH)] + [sds(*s, dtype=F32) for s in shapes[1:6]]
    outs += [sds(512, COLS, dtype=F32)] * 3
    small = [sds(1, n, dtype=F32) for n in (WIDTH, WIDTH, COLS, COLS)]
    wides = [(8, 128)] + shapes[1:6] + [(3, 512, COLS)]
    return pl.pallas_call(
        finish_body,
        name="to_float",
        out_shape=outs + small,
        out_specs=[ANY] * 9 + [VM] * 4,
        in_specs=[ANY] * 7 + [VM],
        scratch_shapes=[pltpu.VMEM(s, BF) for s in shapes]
        + [pltpu.VMEM(s, F32) for s in wides]
        + [pltpu.SemaphoreType.DMA((7,)), pltpu.SemaphoreType.DMA((9,))],
        compiler_params=pltpu.CompilerParams(vmem_limit_bytes=48 * MIB),
    )(*args)


def body(
    tokens, segments, positions, cotangent,
    w_query, w_key, w_value, w_output, w_gate, w_up, w_down,
    query_gain, key_gain, attn_gain, mlp_gain,
):
    del segments
    inverse = ROPE_BASE ** (-np.arange(64, dtype=np.float64) * 2.0 / HEAD)
    freqs = jnp.asarray(np.concatenate([inverse, inverse])[None], F32)
    qgain, kgain, again, mgain = (
        g[None] for g in (query_gain, key_gain, attn_gain, mlp_gain)
    )
    out, d_in, g_down, g_gate, g_up, g_qkv, g_out, gains = layer(
        tokens[0], cotangent[0], positions, freqs, qgain, kgain, again, mgain,
        w_query, w_key, w_value, w_output, w_gate, w_up, w_down,
    )
    out, d_in, g_down, g_gate, g_up, g_out, g_q, g_k, g_v, ga, gm, gq, gk = finish(
        out, d_in, g_down, g_gate, g_up, g_out, g_qkv, gains
    )
    return (
        out[None], d_in[None], g_q, g_k, g_v, g_out, g_gate, g_up, g_down,
        gq[0], gk[0], ga[0], gm[0],
    )


def solution(mesh):
    in_specs = (
        P("fsdp", "context", None),
        P("fsdp", None),
        P("fsdp", None),
        P("fsdp", "context", None),
        P("fsdp", "tensor"),
        P("fsdp", "tensor"),
        P("fsdp", "tensor"),
        P("tensor", "fsdp"),
        P("fsdp", "tensor"),
        P("fsdp", "tensor"),
        P("tensor", "fsdp"),
        P("tensor"),
        P("tensor"),
        P(),
        P(),
    )
    out_specs = (
        P("fsdp", "context", None),
        P("fsdp", "context", None),
        P("fsdp", "tensor"),
        P("fsdp", "tensor"),
        P("fsdp", "tensor"),
        P("tensor", "fsdp"),
        P("fsdp", "tensor"),
        P("fsdp", "tensor"),
        P("tensor", "fsdp"),
        P("tensor"),
        P("tensor"),
        P(),
        P(),
    )
    return jax.shard_map(body, mesh=mesh, in_specs=in_specs, out_specs=out_specs, check_vma=False)
```

```python
import jax
import jax.numpy as jnp
import numpy as np
from jax import lax
from jax.experimental import pallas as pl
from jax.experimental.pallas import tpu as pltpu
from jax.sharding import PartitionSpec as P

MESH = pl.DeviceIdType.MESH
BF = jnp.bfloat16
F32 = jnp.float32
HEAD = 128
WIDTH = 2048
ROWS = 512
COLS = 256
HIDDEN = 1024
BLOCK = 256
CHUNK = 64
HALF = 32
TILE = 256
EPS = 1e-06
ROPE_BASE = 500000.0
BLOCKED = -1000000000.0
LOG2E = 1.4426950408889634
SCALE = HEAD ** (-0.5)
HIGHEST = lax.Precision.HIGHEST
MIB = 2**20
SLOTS = 128


def mm(a, b):
    return lax.dot_general(a, b, (((1,), (0,)), ((), ())), preferred_element_type=F32)


def mm_nt(a, b):
    return lax.dot_general(a, b, (((1,), (1,)), ((), ())), preferred_element_type=F32)


def mm_tn(a, b):
    return lax.dot_general(a, b, (((0,), (0,)), ((), ())), preferred_element_type=F32)


def rows_of(start, size, unit):
    return pl.ds(pl.multiple_of(start, unit), size)


class Place:
    def __init__(self):
        self.f = lax.axis_index("fsdp")
        self.c = lax.axis_index("context")
        self.t = lax.axis_index("tensor")
        self.x = self.t // 2
        self.zh = self.t % 2
        self.zl = self.c // 2
        self.core = self.c % 2

    def x_at(self, k):
        return (self.x + k + 4) % 4

    def to_x(self, k):
        return {"tensor": self.x_at(k) * 2 + self.zh}

    def to_zh(self):
        return {"tensor": self.x * 2 + 1 - self.zh}

    def to_t(self, k):
        return {"tensor": (self.t + k) % 8}

    def to_y(self, k):
        return {"fsdp": (self.f + k) % 4}

    def to_core(self):
        return {"context": self.zl * 2 + 1 - self.core}

    def to_zl(self):
        return {"context": (1 - self.zl) * 2 + self.core}

    def to_far(self):
        return {"context": 3 - self.c}

    def announce(self):
        self.bar = pltpu.get_barrier_semaphore()
        self.peers = [self.to_t(k) for k in range(1, 8)] + [self.to_y(k) for k in range(1, 4)]
        self.peers += [self.to_core(), self.to_zl(), self.to_far()]
        for peer in self.peers:
            pl.semaphore_signal(self.bar, inc=1, device_id=peer, device_id_type=MESH)

    def barrier(self):
        pl.semaphore_wait(self.bar, len(self.peers))


class Net:
    def __init__(self, send, recv, local):
        self.send, self.recv, self.loc = send, recv, local
        self.n = 0
        self.k = 0
        self.free = []
        self.sent = []

    def take(self, count):
        old, self.free = self.free[:count], self.free[count:]
        new = [self.n + i for i in range(count - len(old))]
        self.n += len(new)
        return old + new

    def give(self, slots):
        self.free += slots

    def put(self, src, dst, peer, slot=None):
        if slot is None:
            (slot,) = self.take(1)
        copy = pltpu.make_async_remote_copy(
            src_ref=src,
            dst_ref=dst,
            send_sem=self.send.at[slot],
            recv_sem=self.recv.at[slot],
            device_id=peer,
            device_id_type=MESH,
        )
        copy.start()
        self.sent.append(copy)
        return copy

    def left(self, *copies):
        for copy in copies:
            copy.wait_send()
            self.sent = [other for other in self.sent if other is not copy]

    def local(self, src, dst):
        copy = pltpu.make_async_copy(src, dst, self.loc.at[self.k])
        self.k += 1
        copy.start()
        return copy

    def finish(self):
        self.left(*list(self.sent))


class Reduce:
    def __init__(self, net, me, part, bufs, b, slots):
        self.net, self.me, self.part, self.b, self.slots = net, me, part, b, slots
        self.ra, self.rb, self.zs, self.zr = bufs

    def at(self, k, lower=False, size=HALF):
        start = self.b * BLOCK + self.me.x_at(k) * CHUNK + (HALF if lower else 0)
        return rows_of(start, size, HALF)

    def start(self):
        net, part, b, slots = self.net, self.part, self.b, self.slots
        up, down = self.me.to_x(1), self.me.to_x(-1)
        lower, upper = pl.ds(0, HALF), pl.ds(HALF, HALF)
        self.a0 = net.put(part.at[self.at(2)], self.ra.at[b, 0], up, slots[0])
        self.a1 = net.put(part.at[self.at(2, True)], self.ra.at[b, 1], down, slots[1])
        self.b0 = net.put(part.at[self.at(1, True)], self.rb.at[b, 0, upper], up, slots[2])
        self.b1 = net.put(part.at[self.at(-1)], self.rb.at[b, 1, lower], down, slots[3])

    def mid(self):
        net, me, part, b, slots = self.net, self.me, self.part, self.b, self.slots
        self.a0.wait_recv()
        s = self.at(1)
        part[s] = (part[s].astype(F32) + self.ra[b, 0].astype(F32)).astype(BF)
        self.c0 = net.put(part.at[s], self.rb.at[b, 0, pl.ds(0, HALF)], me.to_x(1), slots[4])
        self.a1.wait_recv()
        s = self.at(-1, True)
        part[s] = (part[s].astype(F32) + self.ra[b, 1].astype(F32)).astype(BF)
        there = self.rb.at[b, 1, pl.ds(HALF, HALF)]
        self.c1 = net.put(part.at[s], there, me.to_x(-1), slots[5])

    def cross(self):
        b = self.b
        for copy in (self.b0, self.b1, self.c0, self.c1):
            copy.wait_recv()
        own = self.part[self.at(0, size=CHUNK)].astype(F32)
        total = own + self.rb[b, 0].astype(F32) + self.rb[b, 1].astype(F32)
        self.zs[b] = total.astype(BF)
        self.z = self.net.put(self.zs.at[b], self.zr.at[b], self.me.to_zh(), self.slots[6])

    def result(self):
        self.z.wait_recv()
        return self.zs[self.b].astype(F32) + self.zr[self.b].astype(F32)

    def left(self):
        self.net.left(self.a0, self.a1, self.b0, self.b1, self.c0, self.c1, self.z)


class Gather:
    def __init__(self, net, me, full, b, slots):
        self.net, self.me, self.full, self.b, self.slots = net, me, full, b, slots

    def at(self, k, lower=False, size=HALF):
        start = self.b * BLOCK + self.me.x_at(k) * CHUNK + (HALF if lower else 0)
        return rows_of(start, size, HALF)

    def send(self, s, k, i):
        ref = self.full.at[s]
        return self.net.put(ref, ref, self.me.to_x(k), self.slots[i])

    def start(self, chunk):
        self.full[self.at(0, size=CHUNK)] = chunk
        self.p0 = self.send(self.at(0), 1, 0)
        self.m0 = self.send(self.at(0, True), -1, 1)
        self.p1 = self.send(self.at(0, True), 1, 2)
        self.m1 = self.send(self.at(0), -1, 3)

    def mid(self):
        self.p0.wait_recv()
        self.f0 = self.send(self.at(-1), 1, 4)
        self.m0.wait_recv()
        self.f1 = self.send(self.at(1, True), -1, 5)

    def end(self):
        for copy in (self.p1, self.m1, self.f0, self.f1):
            copy.wait_recv()

    def left(self):
        self.net.left(self.p0, self.m0, self.p1, self.m1, self.f0, self.f1)


class Weight:
    def __init__(self, net, me, shard, full, slots, own=None):
        self.net, self.me, self.shard, self.full, self.slots = net, me, shard, full, slots
        self.part = shard.shape[0] // self.cuts
        self.own = own or [net.local(shard, full.at[me.f])]

    cuts = 4

    def first(self):
        return self.me.core * 2

    def at(self, lower, parts=1):
        return rows_of((self.first() + lower) * self.part, parts * self.part, self.part)

    def send(self, lower, k, i):
        s, peer = self.at(lower), self.me.to_y(k)
        return self.net.put(
            self.shard.at[s], self.full.at[self.me.f, s], peer, self.slots[i]
        )

    def start(self):
        self.begin()
        self.more()

    def begin(self):
        self.p0, self.m0 = self.send(0, 1, 0), self.send(1, 3, 1)

    def more(self):
        self.p1, self.m1 = self.send(1, 1, 2), self.send(0, 3, 3)

    def hand(self, k, s, peer, i):
        ref = self.full.at[(self.me.f + k) % 4, s]
        return self.net.put(ref, ref, peer, self.slots[i])

    def relay(self):
        self.p0.wait_recv()
        self.f0 = self.hand(3, self.at(0), self.me.to_y(1), 4)
        self.m0.wait_recv()
        self.f1 = self.hand(1, self.at(1), self.me.to_y(3), 5)

    def pass_sides(self):
        core = self.me.to_core()
        self.p1.wait_recv()
        self.n0 = self.hand(3, self.at(0, 2), core, 6)
        self.m1.wait_recv()
        self.n1 = self.hand(1, self.at(0, 2), core, 7)

    def pass_opposite(self):
        self.f0.wait_recv()
        self.f1.wait_recv()
        self.n2 = self.hand(2, self.at(0, 2), self.me.to_core(), 8)

    def pass_on(self):
        self.pass_sides()
        self.pass_opposite()

    def wait(self):
        for copy in (self.n0, self.n1, self.n2):
            copy.wait_recv()
        for copy in self.own:
            copy.wait()
        self.left()

    def left(self):
        near = (self.n0, self.n1, self.n2)
        self.net.left(*near, self.f0, self.f1, self.p0, self.m0, self.p1, self.m1)


class QuarterWeight(Weight):
    cuts = 8

    def first(self):
        return self.me.c * 2

    def both(self, k, i):
        s = self.at(0, 2)
        self.across.append(self.hand(k, s, self.me.to_zl(), i))
        self.near.append(self.hand(k, s, self.me.to_core(), i + 3))

    def pass_sides(self):
        self.across, self.near = [], []
        self.p1.wait_recv()
        self.both(3, 6)
        self.m1.wait_recv()
        self.both(1, 7)

    def pass_opposite(self):
        self.f0.wait_recv()
        self.f1.wait_recv()
        self.both(2, 8)

    def pass_far(self):
        far = rows_of(((self.me.c + 2) % 4) * 2 * self.part, 2 * self.part, self.part)
        for copy, k, i in zip(self.across, (3, 1, 2), (12, 13, 14), strict=True):
            copy.wait_recv()
            self.near.append(self.hand(k, far, self.me.to_core(), i))

    def wait(self):
        for copy in self.near:
            copy.wait_recv()
        for copy in self.own:
            copy.wait()
        self.net.left(
            *self.near, *self.across, self.f0, self.f1, self.p0, self.m0, self.p1, self.m1
        )


class GradSum:
    def __init__(self, net, me, grad, got, credit, out):
        self.net, self.me, self.grad, self.got = net, me, grad, got
        self.slots = net.take(13)
        self.credit, self.out = credit, out
        self.half = grad.shape[1] // 2
        self.mine, self.theirs = self.at(me.core), self.at(1 - me.core)

    def at(self, core, lower=0, parts=2):
        start = core * self.half + lower * (self.half // 2)
        return rows_of(start, parts * self.half // 2, self.half // 2)

    def start(self):
        self.near = [
            self.net.put(
                self.grad.at[f, self.theirs], self.got[f], self.me.to_core(), self.slots[f]
            )
            for f in range(4)
        ]

    def add(self):
        net, me = self.net, self.me
        for f in range(4):
            self.near[f].wait_recv()
            here = self.grad[f, self.mine].astype(F32)
            self.grad[f, self.mine] = (here + self.got[f][...].astype(F32)).astype(BF)
        net.left(*self.near)
        for peer in (me.to_y(1), me.to_y(3), me.to_zl()):
            pl.semaphore_signal(self.credit, inc=1, device_id=peer, device_id_type=MESH)

    def send(self, k, lower, place, way, i):
        me = self.me
        return self.net.put(
            self.grad.at[(me.f + k) % 4, self.at(me.core, lower, 1)],
            self.grad.at[place, self.at(1 - me.core, lower, 1)],
            me.to_y(way),
            self.slots[i],
        )

    def spread(self):
        pl.semaphore_wait(self.credit, 3)
        self.a0, self.a1 = self.send(2, 0, 0, 1, 4), self.send(2, 1, 0, 3, 5)
        self.b0, self.b1 = self.send(1, 1, 1, 1, 6), self.send(3, 0, 2, 3, 7)

    def relay(self):
        me = self.me
        for copy, k, lower in ((self.a0, 1, 0), (self.a1, 3, 1)):
            copy.wait_recv()
            f, s = (me.f + k) % 4, self.at(me.core, lower, 1)
            there = self.grad[0, self.at(1 - me.core, lower, 1)].astype(F32)
            self.grad[f, s] = (self.grad[f, s].astype(F32) + there).astype(BF)
            if k == 1:
                self.c0 = self.send(1, 0, 1, 1, 8)
            else:
                self.c1 = self.send(3, 1, 2, 3, 9)

    def cross(self):
        for copy in (self.b0, self.b1, self.c0, self.c1):
            copy.wait_recv()
        me = self.me
        total = self.grad[me.f, self.mine].astype(F32)
        for k in (1, 2):
            total = total + self.grad[k, self.theirs].astype(F32)
        self.grad[me.f, self.mine] = total.astype(BF)
        self.z = []
        self.cross_half()

    def cross_half(self):
        me, lower = self.me, len(self.z)
        here = self.grad.at[me.f, self.at(me.core, lower, 1)]
        there = self.grad.at[3, self.at(1 - me.core, lower, 1)]
        self.z.append(self.net.put(here, there, me.to_zl(), self.slots[10 + lower]))

    def finish(self):
        for copy in self.z:
            copy.wait_recv()
        me = self.me
        total = self.grad[me.f, self.mine].astype(F32) + self.grad[3, self.theirs].astype(F32)
        self.grad[0, self.theirs] = total.astype(BF)
        final = self.grad.at[0, self.theirs]
        self.store = self.net.local(final, self.out.at[self.mine])
        self.back = self.net.put(final, self.out.at[self.mine], me.to_core(), self.slots[12])

    def end(self):
        self.store.wait()
        self.back.wait_recv()


def rms(value):
    return lax.rsqrt(jnp.mean(value * value, axis=-1, keepdims=True) + EPS)


def norm_back(grad, value, factor, gain):
    scaled = grad * gain
    inner = jnp.mean(scaled * value, axis=-1, keepdims=True)
    return factor * scaled - value * (factor * factor * factor * inner)


def rotate(value, cosine, sine):
    return value * cosine + pltpu.roll(value, 64, axis=1) * sine


def rotate_back(value, cosine, sine):
    return value * cosine - pltpu.roll(value, 64, axis=1) * sine


def two_heads(fn, value, cosine, sine):
    return jnp.concatenate(
        [fn(value[:, :HEAD], cosine, sine), fn(value[:, HEAD:], cosine, sine)], axis=1
    )


def pair_of_sums(first, second):
    ones = jnp.ones((8, COLS), F32)

    def total(v):
        return lax.dot_general(
            ones, v, (((1,), (1,)), ((), ())), precision=HIGHEST, preferred_element_type=F32
        )

    row = lax.broadcasted_iota(jnp.int32, (8, ROWS), 0)
    return jnp.where(row < 4, total(first), total(second))


def layer_body(
    tok_h, cot_h, pos, freqs, qgain, kgain, again, mgain,
    wq_h, wk_h, wv_h, wo_h, wg_h, wu_h, wd_h,
    out_h, ig_h, gdown_h, ggate_h, gup_h, gqkv_h, gout_h, gains_o,
    tok, cot, wqkv, wo, wg, wu, wd, hid, gate, up, mixed, dgate, dup, part_a, part_b,
    m_full, d_m, do_full, ra0, rb0, zs0, zr0, ra1, rb1, zs1, zr1, ochunk,
    qraw, kraw, sums_s, qrot, keys, vals, att, lse, m_s, acc, dq, cosine, sine, low, lowfar,
    stat, stat2, krow, qfar, efar, sfar, srow, dqkv, d_att, ga_s, gm_s, gy, gz, gzr, gc, gcr,
    send, recv, local, credit, ready,
):
    me = Place()
    net = Net(send, recv, local)
    bufs = ((ra0, rb0, zs0, zr0), (ra1, rb1, zs1, zr1))
    me.announce()
    thirds = [
        net.local(w, wqkv.at[me.f, :, pl.ds(i * COLS, COLS)])
        for i, w in enumerate((wq_h, wk_h, wv_h))
    ]
    tok_copy = net.local(tok_h, tok)
    cot_copy = net.local(cot_h, cot)
    w_qk, w_v = (
        Weight(net, me, wqkv.at[me.f, :, cols], wqkv.at[:, :, cols], net.take(9), thirds)
        for cols in (pl.ds(0, 2 * COLS), pl.ds(2 * COLS, COLS))
    )
    w_o, w_u = (Weight(net, me, w, full, net.take(9)) for w, full in ((wo_h, wo), (wu_h, wu)))
    w_g = QuarterWeight(net, me, wg_h, wg, net.take(15))
    w_d = Weight(net, me, wd_h, wd, w_qk.slots)
    sum_slots = [net.take(6) for _ in range(2)]
    all_slots = [net.take(6) for _ in range(2)]
    cross_slots = [[net.take(1) for _ in range(2)] for _ in range(2)]

    def reduces(part, turn):
        return [
            Reduce(net, me, part, bufs[turn], b, sum_slots[b] + cross_slots[turn][b])
            for b in range(2)
        ]

    def gathers(full):
        return [Gather(net, me, full, b, all_slots[b]) for b in range(2)]

    def block_rows(b):
        return slice(b * BLOCK, (b + 1) * BLOCK)

    here = pos[0:1, pl.ds(pl.multiple_of(me.c * ROWS, ROWS), ROWS)].astype(F32)
    places = jnp.broadcast_to(here, (HEAD, ROWS)).T
    angle = places * freqs[0:1, :]
    lane = lax.broadcasted_iota(jnp.int32, (ROWS, HEAD), 1)
    cosine[...] = jnp.cos(angle)
    sin = jnp.sin(angle)
    sine[...] = jnp.where(lane < HEAD // 2, -sin, sin)
    token = lax.broadcasted_iota(jnp.int32, (ROWS, HEAD), 0)
    low[...] = me.c * ROWS + token - places.astype(jnp.int32)
    for i in range(2):
        there = pos[0:1, (2 + i) * ROWS : (3 + i) * ROWS].astype(F32)
        there = jnp.broadcast_to(there, (HEAD, ROWS)).T
        lowfar[i] = (2 + i) * ROWS + token - there.astype(jnp.int32)
    for copy in thirds:
        copy.wait()
    me.barrier()
    w_v.start()
    tok_copy.wait()
    qk_cols, v_cols = slice(0, 2 * COLS), slice(2 * COLS, 3 * COLS)

    def project(k, cols):
        f = (me.f + k) % 4
        some = tok[:, pl.ds(pl.multiple_of(f * 512, 512), 512)]
        return mm(some, wqkv[f, :, cols])

    gate[:, v_cols] = project(0, v_cols)
    w_v.relay()
    w_qk.start()
    gate[:, qk_cols] = project(0, qk_cols)
    w_v.pass_sides()
    w_v.n0.wait_recv()
    w_v.n1.wait_recv()
    gate[:, v_cols] += project(3, v_cols) + project(1, v_cols)
    w_v.pass_opposite()
    w_v.n2.wait_recv()
    with jax.named_scope("values"):
        vals[me.c] = (gate[:, v_cols] + project(2, v_cols)).astype(BF)
    kv_slots = net.take(6)
    v_near = net.put(vals.at[me.c], vals.at[me.c], me.to_core(), kv_slots[0])
    v_far = net.put(vals.at[me.c], vals.at[me.c], me.to_zl(), kv_slots[1])
    w_qk.relay()
    w_o.start()
    w_g.begin()
    w_qk.pass_sides()
    w_qk.n0.wait_recv()
    w_qk.n1.wait_recv()
    gate[:, qk_cols] += project(3, qk_cols) + project(1, qk_cols)
    w_qk.pass_opposite()
    w_qk.n2.wait_recv()
    with jax.named_scope("queries"):
        qk = gate[:, qk_cols] + project(2, qk_cols)
        qraw[...] = qk[:, :COLS]
        kraw[...] = qk[:, COLS:]
        stat[me.t] = pair_of_sums(qraw[...] * qraw[...], kraw[...] * kraw[...])
    stat_slots = net.take(7)
    stats = [
        net.put(stat.at[me.t], stat.at[me.t], me.to_t(k), stat_slots[k - 1]) for k in range(1, 8)
    ]
    keys[me.c] = two_heads(rotate, kraw[...] * kgain[...], cosine[...], sine[...]).astype(BF)
    k_near = net.put(keys.at[me.c], keys.at[me.c], me.to_core(), kv_slots[2])
    k_far = net.put(keys.at[me.c], keys.at[me.c], me.to_zl(), kv_slots[3])
    w_o.relay()
    w_g.more()
    with jax.named_scope("wait_stats"):
        for copy in stats:
            copy.wait_recv()
    row_slots = net.take(3)
    with jax.named_scope("rotate"):
        sums = jnp.sum(stat[...], axis=0)
        krow[me.c] = sums
        rows_far = [
            net.put(krow.at[me.c], krow.at[me.c], peer, slot)
            for peer, slot in zip(
                (me.to_core(), me.to_zl(), me.to_far()), row_slots, strict=True
            )
        ]
        sums_s[...] = sums.T
        scale_q = lax.rsqrt(sums_s[:, 0:1] / WIDTH + EPS)
        q_norm = qraw[...] * (scale_q * (SCALE * LOG2E)) * qgain[...]
        qrot[...] = two_heads(rotate, q_norm, cosine[...], sine[...]).astype(BF)
    other = (1 - me.zl) * 2 + me.core

    m_s[...] = jnp.full(m_s.shape, 2 * BLOCKED, F32)
    acc[...] = jnp.zeros(acc.shape, F32)

    def allowed_keys(j, rows):
        k_index = j * ROWS + lax.broadcasted_iota(jnp.int32, (BLOCK, ROWS), 1)
        first = me.c * ROWS + rows.start
        q_index = first + lax.broadcasted_iota(jnp.int32, (BLOCK, ROWS), 0)
        return (k_index >= low[rows, 0:1]) & (k_index <= q_index)

    heads = [(h, slice(h * HEAD, (h + 1) * HEAD)) for h in range(2)]

    def key_scale(j):
        return lax.rsqrt(krow[j, 4:5, :] / WIDTH + EPS)

    def attend(b, start, stop):
        rows = block_rows(b)

        def step(i, _):
            j = me.c - i
            allowed = allowed_keys(j, rows)
            scale = key_scale(j)
            raw = [mm_nt(qrot[rows, cols], keys[j, :, cols]) * scale for _, cols in heads]
            probs, fades = [], []
            for h, _ in heads:
                s = jnp.where(allowed, raw[h], BLOCKED)
                m_old = m_s[h, rows]
                m_new = jnp.maximum(m_old, jnp.max(s, axis=1, keepdims=True))
                p = jnp.exp2(s - m_new)
                fade = jnp.exp2(m_old - m_new)
                m_s[h, rows] = m_new
                probs.append(p.astype(BF))
                fades.append(fade)
            ones = jnp.ones((ROWS, HEAD), BF)
            sums = [
                mm(probs[h], jnp.concatenate([vals[j, :, cols], ones], axis=1))
                for h, cols in heads
            ]
            for h, _ in heads:
                acc[h, rows] = acc[h, rows] * fades[h] + sums[h]
            return 0

        with jax.named_scope("attend"):
            lax.fori_loop(start, stop, step, 0)

    def attended(b):
        rows = block_rows(b)
        for h, cols in heads:
            att[rows, cols] = (acc[h, rows, :HEAD] / acc[h, rows, HEAD:]).astype(BF)
            lse[h, rows] = m_s[h, rows] + jnp.log2(acc[h, rows, HEAD : HEAD + 1])
        for f in range(4):
            part_a[rows, f * 512 : (f + 1) * 512] = mm(att[rows], wo[f]).astype(BF)

    w_g.relay()
    w_u.start()
    w_g.pass_sides()
    with jax.named_scope("wait_near"):
        v_near.wait_recv()
        k_near.wait_recv()
        rows_far[0].wait_recv()
        v_far.wait_recv()
        v_on = net.put(vals.at[other], vals.at[other], me.to_core(), kv_slots[4])
    for b in range(2):
        attend(b, 0, 1 + me.core)
    with jax.named_scope("wait_far"):
        k_far.wait_recv()
        k_on = net.put(keys.at[other], keys.at[other], me.to_core(), kv_slots[5])
        for copy in (v_on, k_on, rows_far[1], rows_far[2]):
            copy.wait_recv()
    o_sum = reduces(part_a, 0)
    to_hid = gathers(hid)
    w_o.pass_on()
    w_g.pass_opposite()
    attend(0, 1 + me.core, me.c + 1)
    w_o.wait()
    attended(0)
    o_sum[0].start()
    attend(1, 1 + me.core, me.c + 1)
    attended(1)
    o_sum[0].mid()
    o_sum[1].start()
    w_u.relay()
    w_v.left()
    w_qk.left()
    w_d.start()
    net.left(v_near, v_far, k_near, k_far, v_on, k_on, *stats, *rows_far)

    def hidden(b):
        value = o_sum[b].result()
        ochunk[b] = value
        own = tok[o_sum[b].at(0, size=CHUNK)].astype(F32)
        to_hid[b].start((own + value * rms(value) * again[...]).astype(BF))

    o_sum[0].cross()
    o_sum[1].mid()
    hidden(0)
    o_sum[1].cross()
    w_d.relay()
    w_g.pass_far()
    to_hid[0].mid()
    w_u.pass_on()
    hidden(1)
    q_far = net.put(qrot, qfar.at[me.core], me.to_zl())
    to_hid[0].end()

    m_sum = reduces(part_b, 1)
    to_m = gathers(m_full)

    def gates(b, tiles):
        rows = block_rows(b)
        for n in tiles:
            cols = slice(n * TILE, (n + 1) * TILE)
            g = mm(hid[rows], wg[:, :, cols].reshape(WIDTH, TILE))
            u = mm(hid[rows], wu[:, :, cols].reshape(WIDTH, TILE))
            gate[rows, cols] = g
            up[rows, cols] = u
            mixed[rows, cols] = (g * jax.nn.sigmoid(g) * u).astype(BF)

    def down(b):
        rows = block_rows(b)
        for f in range(4):
            part_b[rows, f * 512 : (f + 1) * 512] = mm(mixed[rows], wd[f]).astype(BF)

    w_d.pass_on()
    w_g.wait()
    w_u.wait()
    with jax.named_scope("gates"):
        gates(0, (0, 1))
    to_hid[1].mid()
    with jax.named_scope("gates"):
        gates(0, (2, 3))
    for s in o_sum:
        s.left()
    w_d.wait()
    down(0)
    m_sum[0].start()
    q_far.wait_recv()
    q_on = net.put(qfar.at[me.core], qfar.at[me.core], me.to_core())
    to_hid[1].end()
    with jax.named_scope("gates"):
        gates(1, (0, 1, 2, 3))
    m_sum[0].mid()
    down(1)
    m_sum[1].start()
    m_sum[0].cross()
    m_sum[1].mid()
    cot_copy.wait()
    for g in to_hid:
        g.left()
    q_on.wait_recv()
    net.left(q_far, q_on)
    for w in (w_qk, w_v, w_o, w_g, w_u):
        net.give(w.slots)
    to_m[0].start(m_sum[0].result().astype(BF))
    m_sum[1].cross()
    to_m[0].mid()
    to_m[1].start(m_sum[1].result().astype(BF))
    for s in m_sum:
        s.left()
    gm_s[...] = jnp.zeros(gm_s.shape, F32)

    h_sum = reduces(part_a, 0)
    to_do = gathers(do_full)

    def norm_rows(b):
        def some_rows(i, _):
            some = rows_of(b * BLOCK + i * 64, 64, 64)
            m = m_full[some].astype(F32)
            g = cot[some].astype(F32)
            r = rms(m)
            mr = m * r
            part_b[some] = (hid[some].astype(F32) + mr * mgain[...]).astype(BF)
            d_m[some] = norm_back(g, m, r, mgain[...]).astype(BF)
            gm_s[...] += jnp.sum(g * mr, axis=0, keepdims=True)
            return 0

        with jax.named_scope("norm_rows"):
            lax.fori_loop(0, BLOCK // 64, some_rows, 0)
        return net.local(part_b.at[block_rows(b)], out_h.at[block_rows(b)])

    def gates_back(b):
        rows = block_rows(b)
        for n in range(4):
            cols = slice(n * TILE, (n + 1) * TILE)
            d_mixed = mm_nt(d_m[rows, 0:512], wd[0, cols])
            for f in range(1, 4):
                d_mixed += mm_nt(d_m[rows, f * 512 : (f + 1) * 512], wd[f, cols])
            g = gate[rows, cols]
            sigma = jax.nn.sigmoid(g)
            dgate[rows, cols] = (
                d_mixed * up[rows, cols] * sigma * (1.0 + g * (1.0 - sigma))
            ).astype(BF)
            dup[rows, cols] = (d_mixed * (g * sigma)).astype(BF)

    def hidden_back(b):
        rows = block_rows(b)
        for f in range(4):
            for n in range(0, 512, TILE):
                d = mm_nt(dgate[rows], wg[f, n : n + TILE])
                d += mm_nt(dup[rows], wu[f, n : n + TILE])
                part_a[rows, f * 512 + n : f * 512 + n + TILE] = d.astype(BF)

    stores = []
    to_m[0].end()
    stores.append(norm_rows(0))
    to_m[1].mid()
    with jax.named_scope("gates_back"):
        gates_back(0)
    with jax.named_scope("hidden_back"):
        hidden_back(0)
    h_sum[0].start()
    to_m[1].end()
    stores.append(norm_rows(1))
    for g in to_m:
        g.left()
    pl.semaphore_signal(ready, inc=1, device_id=me.to_core(), device_id_type=MESH)
    h_sum[0].mid()
    with jax.named_scope("gates_back"):
        gates_back(1)
    with jax.named_scope("hidden_back"):
        hidden_back(1)
    h_sum[1].start()

    def columns(ref, f):
        return ref.at[:, pl.ds(f * 512, 512)]

    def quarter(ref, f, cols=1024):
        return ref.at[pl.ds(f // 2 * 256, 256), pl.ds(f % 2 * 1024, cols)]

    def half(pair, f):
        return pair[f // 2].at[pl.ds(f % 2 * 256, 256)]

    g_down = GradSum(
        net, me, wd, [columns(m_full, f) for f in range(4)], credit.at[0], gdown_h
    )
    g_gate = GradSum(net, me, wg, [quarter(d_m, f) for f in range(4)], credit.at[1], ggate_h)
    g_up = GradSum(
        net, me, wu, [half((mixed, dgate), f) for f in range(4)], credit.at[2], gup_h
    )
    with jax.named_scope("grad_down"):
        for f in range(4):
            wd[f] = mm_tn(mixed[...], d_m[:, f * 512 : (f + 1) * 512]).astype(BF)
    pl.semaphore_wait(ready, 1)
    g_down.start()
    h_sum[0].cross()
    with jax.named_scope("grad_gate"):
        for f in range(4):
            wg[f] = mm_tn(hid[:, f * 512 : (f + 1) * 512], dgate[...]).astype(BF)
    h_sum[1].mid()
    g_down.add()
    g_down.spread()

    def back_to_o(b):
        d_hidden = cot[h_sum[b].at(0, size=CHUNK)].astype(F32) + h_sum[b].result()
        value = ochunk[b]
        r = rms(value)
        to_do[b].start(norm_back(d_hidden, value, r, again[...]).astype(BF))
        ochunk[b] = d_hidden
        return jnp.sum(d_hidden * (value * r), axis=0, keepdims=True)

    ga = back_to_o(0)
    g_gate.start()
    h_sum[1].cross()
    to_do[0].mid()
    with jax.named_scope("grad_up"):
        for f in range(4):
            wu[f] = mm_tn(hid[:, f * 512 : (f + 1) * 512], dup[...]).astype(BF)
    ga = ga + back_to_o(1)
    ga_s[me.x] = jnp.broadcast_to(ga, (8, WIDTH))
    ga_far = [net.put(ga_s.at[me.x], ga_s.at[me.x], me.to_x(k)) for k in (1, 3, 2)]
    g_down.relay()
    to_do[0].end()

    dk, dv, deltas, dn = gate, up, m_s, acc
    dk[...] = jnp.zeros(dk.shape, F32)
    dv[...] = jnp.zeros(dv.shape, F32)
    dq[...] = jnp.zeros(dq.shape, F32)

    def attended_back(b):
        rows = block_rows(b)
        d = mm_nt(do_full[rows, 0:512], wo[0])
        for f in range(1, 4):
            d += mm_nt(do_full[rows, f * 512 : (f + 1) * 512], wo[f])
        d_att[rows] = d.astype(BF)

    def attend_back(b, start, stop, with_keys):
        rows = block_rows(b)
        q = [qrot[rows, cols] for _, cols in heads]
        e = [d_att[rows, cols] for _, cols in heads]
        delta = [deltas[h, rows] for h, _ in heads]

        def step(j, _):
            allowed = allowed_keys(j, rows)
            scale = key_scale(j)
            raw = [mm_nt(q[h], keys[j, :, cols]) * scale for h, cols in heads]
            d_probs = [mm_nt(e[h], vals[j, :, cols]) for h, cols in heads]
            probs, d_scores = [], []
            for h, _ in heads:
                s = jnp.where(allowed, raw[h] - lse[h, rows], BLOCKED)
                p = jnp.exp2(s)
                probs.append(p.astype(BF))
                d_scores.append((p * (d_probs[h] - delta[h]) * scale).astype(BF))
            for h, cols in heads:
                dq[rows, cols] += mm(d_scores[h], keys[j, :, cols])
                if with_keys:
                    there = pl.ds(pl.multiple_of((j - home) * COLS + h * HEAD, HEAD), HEAD)
                    dk[:, there] += mm_tn(d_scores[h], q[h])
                    dv[:, there] += mm_tn(probs[h], e[h])
            return 0

        with jax.named_scope("attend_back"):
            lax.fori_loop(start, stop, step, 0)

    def keys_back(b):
        rows = block_rows(b)

        def step(i, _):
            cols8 = sfar[i, b].T
            k_index = me.c * ROWS + lax.broadcasted_iota(jnp.int32, (BLOCK, ROWS), 1)
            allowed = k_index >= lowfar[i, rows, 0:1]
            scale = key_scale(me.c)
            q = [qfar[i, rows, cols] for _, cols in heads]
            e = [efar[i, rows, cols] for _, cols in heads]
            raw = [mm_nt(q[h], keys[me.c, :, cols]) * scale for h, cols in heads]
            d_probs = [mm_nt(e[h], vals[me.c, :, cols]) for h, cols in heads]
            probs, d_scores = [], []
            for h, _ in heads:
                s = jnp.where(allowed, raw[h] - cols8[:, h : h + 1], BLOCKED)
                p = jnp.exp2(s)
                probs.append(p.astype(BF))
                d = d_probs[h] - cols8[:, 2 + h : 3 + h]
                d_scores.append((p * d * scale).astype(BF))
            for h, cols in heads:
                there = pl.ds(pl.multiple_of(me.core * COLS + h * HEAD, HEAD), HEAD)
                dk[:, there] += mm_tn(d_scores[h], q[h])
                dv[:, there] += mm_tn(probs[h], e[h])
            return 0

        with jax.named_scope("keys_back"):
            lax.fori_loop(0, 2 * (1 - me.zl), step, 0)

    home, away = me.zl * 2, (1 - me.zl) * 2
    cross, forward = {}, {}

    def send_far(b):
        rows = block_rows(b)
        for h, cols in heads:
            e, a = d_att[rows, cols].astype(F32), att[rows, cols].astype(F32)
            deltas[h, rows] = jnp.sum(e * a, axis=1, keepdims=True)
        four = [lse[0, rows], lse[1, rows], deltas[0, rows], deltas[1, rows]]
        srow[b] = jnp.concatenate(four + four, axis=1).T
        cross[b] = [
            net.put(d_att.at[rows], efar.at[me.core, rows], me.to_zl(), cross_far[2 * b]),
            net.put(srow.at[b], sfar.at[me.core, b], me.to_zl(), cross_far[2 * b + 1]),
        ]

    def forward_far(b):
        for copy in cross[b]:
            copy.wait_recv()
        e, s = efar.at[me.core, block_rows(b)], sfar.at[me.core, b]
        forward[b] = [
            net.put(e, e, me.to_core(), on_slots[2 * b]),
            net.put(s, s, me.to_core(), on_slots[2 * b + 1]),
        ]

    cross_far, on_slots = net.take(4), net.take(4)
    attended_back(0)
    send_far(0)
    attend_back(0, away, away + 2 * me.zl, False)
    to_do[1].mid()
    attend_back(0, home, me.c + 1, True)
    g_gate.add()
    g_up.start()
    g_gate.spread()
    forward_far(0)
    g_down.cross()
    to_do[1].end()
    attended_back(1)
    send_far(1)
    g_down.cross_half()
    attend_back(1, away, away + 2 * me.zl, False)
    attend_back(1, home, me.c + 1, True)
    g_up.add()
    partner = pl.ds(pl.multiple_of((1 - me.core) * COLS, COLS), COLS)
    own = pl.ds(pl.multiple_of(me.core * COLS, COLS), COLS)

    def key_root(j):
        return jnp.sqrt(krow[j].T[:, 4:5] / WIDTH + EPS) * (1.0 / LOG2E)

    d_m[:, :COLS] = (dk[:, partner] * key_root(home + 1 - me.core)).astype(BF)
    d_m[:, COLS : 2 * COLS] = dv[:, partner].astype(BF)
    from_core = dup.at[:, pl.ds(0, 2 * COLS)]
    swap = net.put(d_m.at[:, pl.ds(0, 2 * COLS)], from_core, me.to_core())
    forward_far(1)
    for copy in forward[0]:
        copy.wait_recv()
    keys_back(0)
    g_gate.relay()
    g_up.spread()
    with jax.named_scope("rotate_back"):
        dn[0] = two_heads(rotate_back, dq[...] * SCALE, cosine[...], sine[...])
    with jax.named_scope("wait_far"):
        for copy in forward[1]:
            copy.wait_recv()
    with jax.named_scope("grad_output"):
        for g in to_do:
            g.left()
        g_out = GradSum(
            net, me, wo, [mixed.at[pl.ds(f * 128, 128), pl.ds(0, 512)] for f in range(4)],
            credit.at[3], gout_h,
        )
        for f in range(4):
            wo[f] = mm_tn(att[...], do_full[:, f * 512 : (f + 1) * 512]).astype(BF)
        g_out.start()
    keys_back(1)
    with jax.named_scope("wait_swap"):
        swap.wait_recv()
    own_root = key_root(me.c)
    d_k = dk[:, own] * own_root + from_core[:, :COLS].astype(F32)
    d_v = dv[:, own] + from_core[:, COLS:].astype(F32)
    with jax.named_scope("rotate_back"):
        dn[1] = two_heads(rotate_back, d_k, cosine[...], sine[...])
        dqkv[:, 2 * COLS :] = d_v.astype(BF)
        scaled_q = dn[0] * qgain[...]
        scaled_k = dn[1] * kgain[...]
        stat2[me.t] = pair_of_sums(scaled_q * qraw[...], scaled_k * kraw[...])
    stats = [
        net.put(stat2.at[me.t], stat2.at[me.t], me.to_t(k), stat_slots[k - 1])
        for k in range(1, 8)
    ]
    scale_q = lax.rsqrt(sums_s[:, 0:1] / WIDTH + EPS)
    scale_k = lax.rsqrt(sums_s[:, 4:5] / WIDTH + EPS)
    for copy in ga_far:
        copy.wait_recv()
    gy[me.f] = jnp.zeros((8, WIDTH), F32)
    gy[me.f, 0:1] = jnp.sum(ga_s[...], axis=0)[0:1]
    gy[me.f, 1:2] = gm_s[...]
    gy[me.f, 2:3, :COLS] = jnp.sum(dn[0] * (qraw[...] * scale_q), axis=0, keepdims=True)
    gy[me.f, 2:3, COLS : 2 * COLS] = jnp.sum(
        dn[1] * (kraw[...] * scale_k), axis=0, keepdims=True
    )
    gains = [net.put(gy.at[me.f], gy.at[me.f], me.to_y(k)) for k in (1, 3, 2)]
    g_out.add()
    with jax.named_scope("wait_stats"):
        for copy in stats:
            copy.wait_recv()
    dots = jnp.sum(stat2[...], axis=0).T / WIDTH
    dqkv[:, :COLS] = (
        scale_q * scaled_q - qraw[...] * (scale_q * scale_q * scale_q * dots[:, 0:1])
    ).astype(BF)
    dqkv[:, COLS : 2 * COLS] = (
        scale_k * scaled_k - kraw[...] * (scale_k * scale_k * scale_k * dots[:, 4:5])
    ).astype(BF)

    for copy in stores:
        copy.wait()
    for s in h_sum:
        s.left()
    x_sum = reduces(part_b, 1)
    to_ig = gathers(m_full)

    def input_back(b):
        rows = block_rows(b)
        for f in range(4):
            for n in range(0, 512, TILE):
                d = mm_nt(dqkv[rows], wqkv[f, n : n + TILE])
                part_b[rows, f * 512 + n : f * 512 + n + TILE] = d.astype(BF)

    def input_grad(b):
        to_ig[b].start((ochunk[b] + x_sum[b].result()).astype(BF))

    g_gate.cross()
    with jax.named_scope("input_back"):
        input_back(0)
    x_sum[0].start()
    g_gate.cross_half()
    with jax.named_scope("input_back"):
        input_back(1)
    g_out.spread()
    x_sum[0].mid()
    x_sum[1].start()
    g_qkv = GradSum(
        net, me, wqkv, [quarter(do_full, f, 3 * COLS) for f in range(4)], credit.at[4], gqkv_h
    )
    with jax.named_scope("grad_qkv"):
        for f in range(4):
            wqkv[f] = mm_tn(tok[:, f * 512 : (f + 1) * 512], dqkv[...]).astype(BF)
    g_qkv.start()
    g_up.relay()
    x_sum[0].cross()
    g_qkv.add()
    x_sum[1].mid()
    g_qkv.spread()
    g_out.relay()
    g_up.cross()
    input_grad(0)
    x_sum[1].cross()
    g_up.cross_half()
    g_qkv.relay()
    to_ig[0].mid()
    g_down.finish()
    g_gate.finish()
    input_grad(1)
    g_out.cross()
    g_out.cross_half()
    for copy in gains:
        copy.wait_recv()
    gz[...] = gy[0] + gy[1] + gy[2] + gy[3]
    gain_z = net.put(gz, gzr, me.to_zl())
    to_ig[0].end()
    stores = [net.local(m_full.at[block_rows(0)], ig_h.at[block_rows(0)])]
    to_ig[1].mid()
    g_qkv.cross()
    g_qkv.cross_half()
    g_up.finish()
    gain_z.wait_recv()
    gc[...] = gz[...] + gzr[...]
    gain_c = net.put(gc, gcr, me.to_core())
    to_ig[1].end()
    stores.append(net.local(m_full.at[block_rows(1)], ig_h.at[block_rows(1)]))
    g_out.finish()
    g_qkv.finish()
    gain_c.wait_recv()
    gains_o[...] = gc[...] + gcr[...]
    for g in (g_down, g_gate, g_up, g_out, g_qkv):
        g.end()
    for copy in stores:
        copy.wait()
    net.finish()


def sds(*shape, dtype=BF):
    return jax.ShapeDtypeStruct(shape, dtype)


VM = pl.BlockSpec(memory_space=pltpu.VMEM)
ANY = pl.BlockSpec(memory_space=pl.ANY)


def layer(*args):
    def buf(*shape, dtype=BF):
        return pltpu.VMEM(shape, dtype)

    def wide(*shape):
        return pltpu.VMEM(shape, F32)

    reduce_bufs = [
        buf(2, 2, HALF, WIDTH),
        buf(2, 2, CHUNK, WIDTH),
        buf(2, CHUNK, WIDTH),
        buf(2, CHUNK, WIDTH),
    ]
    return pl.pallas_call(
        layer_body,
        name="layer",
        out_shape=[
            sds(ROWS, WIDTH),
            sds(ROWS, WIDTH),
            sds(HIDDEN, 512),
            sds(512, HIDDEN),
            sds(512, HIDDEN),
            sds(512, 3 * COLS),
            sds(COLS, 512),
            sds(8, WIDTH, dtype=F32),
        ],
        out_specs=[ANY] * 7 + [VM],
        in_specs=[ANY, ANY] + [VM] * 6 + [ANY] * 7,
        scratch_shapes=[
            buf(ROWS, WIDTH),
            buf(ROWS, WIDTH),
            buf(4, 512, 3 * COLS),
            buf(4, COLS, 512),
            buf(4, 512, HIDDEN),
            buf(4, 512, HIDDEN),
            buf(4, HIDDEN, 512),
            buf(ROWS, WIDTH),
            wide(ROWS, HIDDEN),
            wide(ROWS, HIDDEN),
            buf(ROWS, HIDDEN),
            buf(ROWS, HIDDEN),
            buf(ROWS, HIDDEN),
            buf(ROWS, WIDTH),
            buf(ROWS, WIDTH),
            buf(ROWS, WIDTH),
            buf(ROWS, WIDTH),
            buf(ROWS, WIDTH),
            *reduce_bufs,
            *reduce_bufs,
            wide(2, CHUNK, WIDTH),
            wide(ROWS, COLS),
            wide(ROWS, COLS),
            wide(ROWS, 8),
            buf(ROWS, COLS),
            buf(4, ROWS, COLS),
            buf(4, ROWS, COLS),
            buf(ROWS, COLS),
            wide(2, ROWS, 1),
            wide(2, ROWS, 1),
            wide(2, ROWS, 2 * HEAD),
            wide(ROWS, COLS),
            wide(ROWS, HEAD),
            wide(ROWS, HEAD),
            pltpu.VMEM((ROWS, HEAD), jnp.int32),
            pltpu.VMEM((2, ROWS, HEAD), jnp.int32),
            wide(8, 8, ROWS),
            wide(8, 8, ROWS),
            wide(4, 8, ROWS),
            buf(2, ROWS, COLS),
            buf(2, ROWS, COLS),
            wide(2, 2, 8, BLOCK),
            wide(2, 8, BLOCK),
            buf(ROWS, 3 * COLS),
            buf(ROWS, COLS),
            wide(4, 8, WIDTH),
            wide(1, WIDTH),
            wide(4, 8, WIDTH),
            *[wide(8, WIDTH) for _ in range(4)],
            pltpu.SemaphoreType.DMA((SLOTS,)),
            pltpu.SemaphoreType.DMA((SLOTS,)),
            pltpu.SemaphoreType.DMA((18,)),
            pltpu.SemaphoreType.REGULAR((5,)),
            pltpu.SemaphoreType.REGULAR,
        ],
        compiler_params=pltpu.CompilerParams(
            collective_id=1, has_side_effects=True, vmem_limit_bytes=63 * MIB
        ),
    )(*args)


ARRAYS = (
    (ROWS, WIDTH),
    (ROWS, WIDTH),
    (HIDDEN, 512),
    (512, HIDDEN),
    (512, HIDDEN),
    (COLS, 512),
    (512, 3 * COLS),
)
PIECES = 2


def finish_body(*refs):
    arrays, gains, rest = refs[:7], refs[7], refs[8:]
    outs, rest = rest[:9], rest[9:]
    g_outs, rest = rest[:4], rest[4:]
    ins, wides, (in_sem, out_sem) = rest[:7], rest[7:14], rest[14:]

    def rows(i, p):
        size = ARRAYS[i][0] // PIECES
        return pl.ds(p * size, size)

    order = [(i, p) for i in (1, 2, 3, 4, 6, 5, 0) for p in range(PIECES)]
    loads = {}
    for i, p in order:
        s = rows(i, p)
        loads[i, p] = pltpu.make_async_copy(arrays[i].at[s], ins[i].at[s], in_sem.at[i, p])
        loads[i, p].start()
    stores = []

    def store(src, i, p, s):
        stores.append(pltpu.make_async_copy(src, outs[i].at[s], out_sem.at[i, p]))
        stores[-1].start()

    for i, p in order:
        loads[i, p].wait()
        s = rows(i, p)
        if i == 0:
            store(ins[0].at[s], 0, p, s)
        elif i == 6:
            for k in range(3):
                wides[6][k, s] = ins[6][s, k * COLS : (k + 1) * COLS].astype(F32)
                store(wides[6].at[k, s], 6 + k, p, s)
        else:
            wides[i][s] = ins[i][s].astype(F32)
            store(wides[i].at[s], i, p, s)
    g_outs[0][...] = gains[0:1]
    g_outs[1][...] = gains[1:2]
    g_outs[2][...] = gains[2:3, :COLS]
    g_outs[3][...] = gains[2:3, COLS : 2 * COLS]
    for copy in stores:
        copy.wait()


def finish(*args):
    outs = [sds(ROWS, WIDTH)] + [sds(*s, dtype=F32) for s in ARRAYS[1:6]]
    outs += [sds(512, COLS, dtype=F32)] * 3
    small = [sds(1, n, dtype=F32) for n in (WIDTH, WIDTH, COLS, COLS)]
    wides = [(8, 128), *ARRAYS[1:6], (3, 512, COLS)]
    return pl.pallas_call(
        finish_body,
        name="to_float",
        out_shape=outs + small,
        out_specs=[ANY] * 9 + [VM] * 4,
        in_specs=[ANY] * 7 + [VM],
        scratch_shapes=[pltpu.VMEM(s, BF) for s in ARRAYS]
        + [pltpu.VMEM(s, F32) for s in wides]
        + [pltpu.SemaphoreType.DMA((7, PIECES)), pltpu.SemaphoreType.DMA((9, PIECES))],
        compiler_params=pltpu.CompilerParams(vmem_limit_bytes=62 * MIB),
    )(*args)


def body(
    tokens, segments, positions, cotangent,
    w_query, w_key, w_value, w_output, w_gate, w_up, w_down,
    query_gain, key_gain, attn_gain, mlp_gain,
):
    del segments
    inverse = ROPE_BASE ** (-np.arange(64, dtype=np.float64) * 2.0 / HEAD)
    freqs = jnp.asarray(np.concatenate([inverse, inverse])[None], F32)
    qgain, kgain, again, mgain = (
        g[None] for g in (query_gain, key_gain, attn_gain, mlp_gain)
    )
    out, d_in, g_down, g_gate, g_up, g_qkv, g_out, gains = layer(
        tokens[0], cotangent[0], positions, freqs, qgain, kgain, again, mgain,
        w_query, w_key, w_value, w_output, w_gate, w_up, w_down,
    )
    out, d_in, g_down, g_gate, g_up, g_out, g_q, g_k, g_v, ga, gm, gq, gk = finish(
        out, d_in, g_down, g_gate, g_up, g_out, g_qkv, gains
    )
    return (
        out[None], d_in[None], g_q, g_k, g_v, g_out, g_gate, g_up, g_down,
        gq[0], gk[0], ga[0], gm[0],
    )


def solution(mesh):
    in_specs = (
        P("fsdp", "context", None),
        P("fsdp", None),
        P("fsdp", None),
        P("fsdp", "context", None),
        P("fsdp", "tensor"),
        P("fsdp", "tensor"),
        P("fsdp", "tensor"),
        P("tensor", "fsdp"),
        P("fsdp", "tensor"),
        P("fsdp", "tensor"),
        P("tensor", "fsdp"),
        P("tensor"),
        P("tensor"),
        P(),
        P(),
    )
    out_specs = (
        P("fsdp", "context", None),
        P("fsdp", "context", None),
        P("fsdp", "tensor"),
        P("fsdp", "tensor"),
        P("fsdp", "tensor"),
        P("tensor", "fsdp"),
        P("fsdp", "tensor"),
        P("fsdp", "tensor"),
        P("tensor", "fsdp"),
        P("tensor"),
        P("tensor"),
        P(),
        P(),
    )
    return jax.shard_map(body, mesh=mesh, in_specs=in_specs, out_specs=out_specs, check_vma=False)
```

```python
import functools

import jax
import jax.numpy as jnp
import numpy as np
from jax import lax
from jax.experimental import pallas as pl
from jax.experimental.pallas import tpu as pltpu
from jax.sharding import PartitionSpec as P

MESH = pl.DeviceIdType.MESH
BF = jnp.bfloat16
F32 = jnp.float32
HEAD = 128
WIDTH = 2048
ROWS = 512
COLS = 256
HIDDEN = 1024
BLOCK = 256
CHUNK = 64
HALF = 32
TILE = 256
EPS = 1e-06
ROPE_BASE = 500000.0
BLOCKED = -1000000000.0
LOG2E = 1.4426950408889634
SCALE = HEAD ** (-0.5)
HIGHEST = lax.Precision.HIGHEST
MIB = 2**20
SLOTS = 103
SENDS = 56


def mm(a, b):
    return lax.dot_general(a, b, (((1,), (0,)), ((), ())), preferred_element_type=F32)


def mm_nt(a, b):
    return lax.dot_general(a, b, (((1,), (1,)), ((), ())), preferred_element_type=F32)


def mm_tn(a, b):
    return lax.dot_general(a, b, (((0,), (0,)), ((), ())), preferred_element_type=F32)


def rows_of(start, size, unit):
    return pl.ds(pl.multiple_of(start, unit), size)


class Place:
    def __init__(self):
        self.f = lax.axis_index("fsdp")
        self.c = lax.axis_index("context")
        self.t = lax.axis_index("tensor")
        self.x = self.t // 2
        self.zh = self.t % 2
        self.zl = self.c // 2
        self.core = self.c % 2

    def x_at(self, k):
        return (self.x + k + 4) % 4

    def to_x(self, k):
        return {"tensor": self.x_at(k) * 2 + self.zh}

    def to_zh(self):
        return {"tensor": self.x * 2 + 1 - self.zh}

    def to_t(self, k):
        return {"tensor": (self.t + k) % 8}

    def to_y(self, k):
        return {"fsdp": (self.f + k) % 4}

    def to_core(self):
        return {"context": self.zl * 2 + 1 - self.core}

    def to_zl(self):
        return {"context": (1 - self.zl) * 2 + self.core}

    def to_far(self):
        return {"context": 3 - self.c}

    def announce(self):
        self.bar = pltpu.get_barrier_semaphore()
        self.peers = [self.to_t(k) for k in range(1, 8)] + [self.to_y(k) for k in range(1, 4)]
        self.peers += [self.to_core(), self.to_zl(), self.to_far()]
        for peer in self.peers:
            pl.semaphore_signal(self.bar, inc=1, device_id=peer, device_id_type=MESH)

    def barrier(self):
        pl.semaphore_wait(self.bar, len(self.peers))


class Net:
    def __init__(self, send, recv, local):
        self.send, self.recv, self.loc = send, recv, local
        self.n = 0
        self.k = 0
        self.free = []
        self.free_sends = list(range(SENDS))
        self.sent = []

    def take(self, count):
        old, self.free = self.free[:count], self.free[count:]
        new = [self.n + i for i in range(count - len(old))]
        self.n += len(new)
        return old + new

    def give(self, slots):
        self.free += slots

    def put(self, src, dst, peer, slot=None):
        if slot is None:
            (slot,) = self.take(1)
        if not self.free_sends:
            self.left(self.sent[0][0])
        number = self.free_sends.pop(0)
        copy = pltpu.make_async_remote_copy(
            src_ref=src,
            dst_ref=dst,
            send_sem=self.send.at[number],
            recv_sem=self.recv.at[slot],
            device_id=peer,
            device_id_type=MESH,
        )
        copy.start()
        self.sent.append((copy, number))
        return copy

    def left(self, *copies):
        for copy in copies:
            for i, (other, number) in enumerate(self.sent):
                if other is copy:
                    copy.wait_send()
                    self.free_sends.append(number)
                    del self.sent[i]
                    break

    def local(self, src, dst):
        copy = pltpu.make_async_copy(src, dst, self.loc.at[self.k])
        self.k += 1
        copy.start()
        return copy

    def finish(self):
        self.left(*[copy for copy, _ in self.sent])


class Reduce:
    def __init__(self, net, me, part, bufs, b, slots):
        self.net, self.me, self.part, self.b, self.slots = net, me, part, b, slots
        self.ra, self.rb, self.zs, self.zr = bufs

    def at(self, k, lower=False, size=HALF):
        start = self.b * BLOCK + self.me.x_at(k) * CHUNK + (HALF if lower else 0)
        return rows_of(start, size, HALF)

    def start(self):
        net, part, b, slots = self.net, self.part, self.b, self.slots
        up, down = self.me.to_x(1), self.me.to_x(-1)
        lower, upper = pl.ds(0, HALF), pl.ds(HALF, HALF)
        self.a0 = net.put(part.at[self.at(2)], self.ra.at[b, 0], up, slots[0])
        self.a1 = net.put(part.at[self.at(2, True)], self.ra.at[b, 1], down, slots[1])
        self.b0 = net.put(part.at[self.at(1, True)], self.rb.at[b, 0, upper], up, slots[2])
        self.b1 = net.put(part.at[self.at(-1)], self.rb.at[b, 1, lower], down, slots[3])

    def mid(self):
        net, me, part, b, slots = self.net, self.me, self.part, self.b, self.slots
        self.a0.wait_recv()
        s = self.at(1)
        part[s] = (part[s].astype(F32) + self.ra[b, 0].astype(F32)).astype(BF)
        self.c0 = net.put(part.at[s], self.rb.at[b, 0, pl.ds(0, HALF)], me.to_x(1), slots[4])
        self.a1.wait_recv()
        s = self.at(-1, True)
        part[s] = (part[s].astype(F32) + self.ra[b, 1].astype(F32)).astype(BF)
        there = self.rb.at[b, 1, pl.ds(HALF, HALF)]
        self.c1 = net.put(part.at[s], there, me.to_x(-1), slots[5])

    def cross(self):
        b = self.b
        for copy in (self.b0, self.b1, self.c0, self.c1):
            copy.wait_recv()
        own = self.part[self.at(0, size=CHUNK)].astype(F32)
        total = own + self.rb[b, 0].astype(F32) + self.rb[b, 1].astype(F32)
        self.zs[b] = total.astype(BF)
        self.z = self.net.put(self.zs.at[b], self.zr.at[b], self.me.to_zh(), self.slots[6])

    def result(self):
        self.z.wait_recv()
        return self.zs[self.b].astype(F32) + self.zr[self.b].astype(F32)

    def left(self):
        self.net.left(self.a0, self.a1, self.b0, self.b1, self.c0, self.c1, self.z)


class Gather:
    def __init__(self, net, me, full, b, slots):
        self.net, self.me, self.full, self.b, self.slots = net, me, full, b, slots

    def at(self, k, lower=False, size=HALF):
        start = self.b * BLOCK + self.me.x_at(k) * CHUNK + (HALF if lower else 0)
        return rows_of(start, size, HALF)

    def send(self, s, k, i):
        ref = self.full.at[s]
        return self.net.put(ref, ref, self.me.to_x(k), self.slots[i])

    def start(self, chunk):
        self.full[self.at(0, size=CHUNK)] = chunk
        self.p0 = self.send(self.at(0), 1, 0)
        self.m0 = self.send(self.at(0, True), -1, 1)
        self.p1 = self.send(self.at(0, True), 1, 2)
        self.m1 = self.send(self.at(0), -1, 3)

    def mid(self):
        self.p0.wait_recv()
        self.f0 = self.send(self.at(-1), 1, 4)
        self.m0.wait_recv()
        self.f1 = self.send(self.at(1, True), -1, 5)

    def end(self):
        for copy in (self.p1, self.m1, self.f0, self.f1):
            copy.wait_recv()

    def left(self):
        self.net.left(self.p0, self.m0, self.p1, self.m1, self.f0, self.f1)


class Weight:
    def __init__(self, net, me, shard, full, slots, own=None):
        self.net, self.me, self.shard, self.full, self.slots = net, me, shard, full, slots
        self.part = shard.shape[0] // self.cuts
        self.own = own or [net.local(shard, full.at[me.f])]

    cuts = 4

    def first(self):
        return self.me.core * 2

    def at(self, lower, parts=1):
        return rows_of((self.first() + lower) * self.part, parts * self.part, self.part)

    def send(self, lower, k, i):
        s, peer = self.at(lower), self.me.to_y(k)
        return self.net.put(
            self.shard.at[s], self.full.at[self.me.f, s], peer, self.slots[i]
        )

    def start(self):
        self.begin()
        self.more()

    def begin(self):
        self.p0, self.m0 = self.send(0, 1, 0), self.send(1, 3, 1)

    def more(self):
        self.p1, self.m1 = self.send(1, 1, 2), self.send(0, 3, 3)

    def hand(self, k, s, peer, i):
        ref = self.full.at[(self.me.f + k) % 4, s]
        return self.net.put(ref, ref, peer, self.slots[i])

    def relay(self):
        self.p0.wait_recv()
        self.f0 = self.hand(3, self.at(0), self.me.to_y(1), 4)
        self.m0.wait_recv()
        self.f1 = self.hand(1, self.at(1), self.me.to_y(3), 5)

    def pass_sides(self):
        core = self.me.to_core()
        self.p1.wait_recv()
        self.n0 = self.hand(3, self.at(0, 2), core, 6)
        self.m1.wait_recv()
        self.n1 = self.hand(1, self.at(0, 2), core, 7)

    def pass_opposite(self):
        self.f0.wait_recv()
        self.f1.wait_recv()
        self.n2 = self.hand(2, self.at(0, 2), self.me.to_core(), 8)

    def pass_on(self):
        self.pass_sides()
        self.pass_opposite()

    def wait(self):
        for copy in (self.n0, self.n1, self.n2):
            copy.wait_recv()
        for copy in self.own:
            copy.wait()
        self.left()

    def left(self):
        near = (self.n0, self.n1, self.n2)
        self.net.left(*near, self.f0, self.f1, self.p0, self.m0, self.p1, self.m1)


class QuarterWeight(Weight):
    cuts = 8

    def first(self):
        return self.me.c * 2

    def both(self, k, i):
        s = self.at(0, 2)
        self.across.append(self.hand(k, s, self.me.to_zl(), i))
        self.near.append(self.hand(k, s, self.me.to_core(), i + 3))

    def pass_sides(self):
        self.across, self.near = [], []
        self.p1.wait_recv()
        self.both(3, 6)
        self.m1.wait_recv()
        self.both(1, 7)

    def pass_opposite(self):
        self.f0.wait_recv()
        self.f1.wait_recv()
        self.both(2, 8)

    def pass_far(self):
        far = rows_of(((self.me.c + 2) % 4) * 2 * self.part, 2 * self.part, self.part)
        for copy, k, i in zip(self.across, (3, 1, 2), (12, 13, 14), strict=True):
            copy.wait_recv()
            self.near.append(self.hand(k, far, self.me.to_core(), i))

    def arrive(self):
        for copy in self.near:
            copy.wait_recv()

    def wait(self):
        self.arrive()
        for copy in self.own:
            copy.wait()
        self.left()

    def left(self):
        own = (self.f0, self.f1, self.p0, self.m0, self.p1, self.m1)
        self.net.left(*self.near, *self.across, *own)


class GradSum:
    def __init__(self, net, me, grad, got, credit, out, near, far, landing=None):
        self.net, self.me, self.grad, self.got = net, me, grad, got
        self.landing = landing
        self.slots = near + far + net.take(3)
        self.credit, self.out = credit, out
        self.half = grad.shape[1] // 2
        self.mine, self.theirs = self.at(me.core), self.at(1 - me.core)

    def at(self, core, lower=0, parts=2):
        start = core * self.half + lower * (self.half // 2)
        return rows_of(start, parts * self.half // 2, self.half // 2)

    def start(self):
        self.near = [
            self.net.put(
                self.grad.at[f, self.theirs], self.got[f], self.me.to_core(), self.slots[f]
            )
            for f in range(4)
        ]

    def add(self):
        net, me = self.net, self.me
        for f in range(4):
            self.near[f].wait_recv()
            here = self.grad[f, self.mine].astype(F32)
            self.grad[f, self.mine] = (here + self.got[f][...].astype(F32)).astype(BF)
        if self.landing is None:
            self.release()

    def release(self):
        self.net.left(*self.near)
        near_y, zl = self.credit
        self.grant(zl, self.me.to_zl())
        if self.landing is None:
            for k in (1, 3):
                self.grant(near_y, self.me.to_y(k))

    @staticmethod
    def grant(credit, peer):
        pl.semaphore_signal(credit, inc=1, device_id=peer, device_id_type=MESH)

    def place(self, slot, lower):
        if self.landing is not None:
            return self.landing(slot, lower)
        return self.grad.at[slot, self.at(1 - self.me.core, lower, 1)]

    def send(self, k, lower, place, way, i):
        me = self.me
        return self.net.put(
            self.grad.at[(me.f + k) % 4, self.at(me.core, lower, 1)],
            self.place(place, lower),
            me.to_y(way),
            self.slots[i],
        )

    def spread(self):
        pl.semaphore_wait(self.credit[0], 2)
        self.a0, self.a1 = self.send(2, 0, 0, 1, 4), self.send(2, 1, 0, 3, 5)
        self.b0, self.b1 = self.send(1, 1, 1, 1, 6), self.send(3, 0, 2, 3, 7)

    def relay(self):
        me = self.me
        for copy, k, lower in ((self.a0, 1, 0), (self.a1, 3, 1)):
            copy.wait_recv()
            f, s = (me.f + k) % 4, self.at(me.core, lower, 1)
            there = self.place(0, lower)[...].astype(F32)
            self.grad[f, s] = (self.grad[f, s].astype(F32) + there).astype(BF)
            if k == 1:
                self.c0 = self.send(1, 0, 1, 1, 8)
            else:
                self.c1 = self.send(3, 1, 2, 3, 9)

    def cross(self):
        for copy in (self.b0, self.b1, self.c0, self.c1):
            copy.wait_recv()
        me = self.me
        for lower in range(2):
            s = self.at(me.core, lower, 1)
            total = self.grad[me.f, s].astype(F32)
            for k in (1, 2):
                total = total + self.place(k, lower)[...].astype(F32)
            self.grad[me.f, s] = total.astype(BF)
        pl.semaphore_wait(self.credit[1], 1)
        self.z = []
        self.cross_half()

    def cross_half(self):
        me, lower = self.me, len(self.z)
        here = self.grad.at[me.f, self.at(me.core, lower, 1)]
        there = self.grad.at[3, self.at(1 - me.core, lower, 1)]
        self.z.append(self.net.put(here, there, me.to_zl(), self.slots[10 + lower]))

    def finish(self):
        for copy in self.z:
            copy.wait_recv()
        me = self.me
        total = self.grad[me.f, self.mine].astype(F32) + self.grad[3, self.theirs].astype(F32)
        self.grad[0, self.theirs] = total.astype(BF)
        final = self.grad.at[0, self.theirs]
        self.store = self.net.local(final, self.out.at[self.mine])
        self.back = self.net.put(final, self.out.at[self.mine], me.to_core(), self.slots[12])

    def end(self):
        self.store.wait()
        self.back.wait_recv()


def rms(value):
    return lax.rsqrt(jnp.mean(value * value, axis=-1, keepdims=True) + EPS)


def norm_back(grad, value, factor, gain):
    scaled = grad * gain
    inner = jnp.mean(scaled * value, axis=-1, keepdims=True)
    return factor * scaled - value * (factor * factor * factor * inner)


def rotate(value, cosine, sine):
    return value * cosine + pltpu.roll(value, 64, axis=1) * sine


def rotate_back(value, cosine, sine):
    return value * cosine - pltpu.roll(value, 64, axis=1) * sine


def two_heads(fn, value, cosine, sine):
    return jnp.concatenate(
        [fn(value[:, :HEAD], cosine, sine), fn(value[:, HEAD:], cosine, sine)], axis=1
    )


def pair_of_sums(first, second):
    ones = jnp.ones((8, COLS), F32)

    def total(v):
        return lax.dot_general(
            ones, v, (((1,), (1,)), ((), ())), precision=HIGHEST, preferred_element_type=F32
        )

    row = lax.broadcasted_iota(jnp.int32, (8, ROWS), 0)
    return jnp.where(row < 4, total(first), total(second))


def layer_body(
    tok_h, cot_h, pos, freqs, qgain, kgain, again, mgain,
    wq_h, wk_h, wv_h, wo_h, wg_h, wu_h, wd_h,
    out_h, ig_h, gdown_h, ggate_h, gup_h, gqkv_h, gout_h, gains_h,
    tok, cot, wqkv, wo, wg, wu, wd, hid, gate, up, mixed, dgate, dup, part_a, part_b,
    m_full, d_m, do_full, ra0, rb0, zs0, zr0, ra1, rb1, zs1, zr1, ochunk,
    qraw, kraw, sums_s, qrot, keys, vals, att, lse, m_s, acc, dq, cosine, sine, low, lowfar,
    stat, stat2, krow, qfar, efar, sfar, srow, dqkv, d_att, ga_s, gm_s, gy, gz, gzr, gc, gcr,
    send, recv, local, credit, ready,
):
    me = Place()
    net = Net(send, recv, local)
    bufs = ((ra0, rb0, zs0, zr0), (ra1, rb1, zs1, zr1))
    me.announce()
    thirds = [
        net.local(w, wqkv.at[me.f, :, pl.ds(i * COLS, COLS)])
        for i, w in enumerate((wq_h, wk_h, wv_h))
    ]
    tok_copy = net.local(tok_h, tok)
    cot_copy = net.local(cot_h, cot)
    w_qk, w_v = (
        kind(net, me, wqkv.at[me.f, :, cols], wqkv.at[:, :, cols], net.take(count), thirds)
        for kind, cols, count in (
            (Weight, pl.ds(0, 2 * COLS), 9),
            (QuarterWeight, pl.ds(2 * COLS, COLS), 15),
        )
    )
    w_o, w_u = (Weight(net, me, w, full, net.take(9)) for w, full in ((wo_h, wo), (wu_h, wu)))
    w_g = QuarterWeight(net, me, wg_h, wg, net.take(15))
    w_d = Weight(net, me, wd_h, wd, w_qk.slots)
    sum_slots = [net.take(6) for _ in range(2)]
    all_slots = [net.take(6) for _ in range(2)]
    cross_slots = [[net.take(1) for _ in range(2)] for _ in range(2)]

    def reduces(part, turn):
        return [
            Reduce(net, me, part, bufs[turn], b, sum_slots[b] + cross_slots[turn][b])
            for b in range(2)
        ]

    def gathers(full):
        return [Gather(net, me, full, b, all_slots[b]) for b in range(2)]

    def block_rows(b):
        return slice(b * BLOCK, (b + 1) * BLOCK)

    here = pos[0:1, pl.ds(pl.multiple_of(me.c * ROWS, ROWS), ROWS)].astype(F32)
    places = jnp.broadcast_to(here, (HEAD, ROWS)).T
    angle = places * freqs[0:1, :]
    lane = lax.broadcasted_iota(jnp.int32, (ROWS, HEAD), 1)
    cosine[...] = jnp.cos(angle)
    sin = jnp.sin(angle)
    sine[...] = jnp.where(lane < HEAD // 2, -sin, sin)
    token = lax.broadcasted_iota(jnp.int32, (ROWS, HEAD), 0)
    low[...] = me.c * ROWS + token - places.astype(jnp.int32)
    for i in range(2):
        there = pos[0:1, (2 + i) * ROWS : (3 + i) * ROWS].astype(F32)
        there = jnp.broadcast_to(there, (HEAD, ROWS)).T
        lowfar[i] = (2 + i) * ROWS + token - there.astype(jnp.int32)
    for copy in thirds:
        copy.wait()
    me.barrier()
    w_v.start()
    tok_copy.wait()
    qk_cols, v_cols = slice(0, 2 * COLS), slice(2 * COLS, 3 * COLS)

    def project(k, cols):
        f = (me.f + k) % 4
        some = tok[:, pl.ds(pl.multiple_of(f * 512, 512), 512)]
        return mm(some, wqkv[f, :, cols])

    gate[:, v_cols] = project(0, v_cols)
    w_v.relay()
    w_qk.start()
    gate[:, qk_cols] = project(0, qk_cols)
    w_v.pass_sides()
    w_v.pass_opposite()
    w_qk.relay()
    w_o.start()
    w_g.begin()
    w_v.pass_far()
    w_qk.pass_sides()
    with jax.named_scope("wait_wv"):
        w_v.arrive()
    with jax.named_scope("values"):
        value = gate[:, v_cols] + project(1, v_cols) + project(2, v_cols) + project(3, v_cols)
        vals[me.c] = value.astype(BF)
    kv_slots = net.take(6)
    v_near = net.put(vals.at[me.c], vals.at[me.c], me.to_core(), kv_slots[0])
    v_far = net.put(vals.at[me.c], vals.at[me.c], me.to_zl(), kv_slots[1])
    w_qk.n0.wait_recv()
    w_qk.n1.wait_recv()
    gate[:, qk_cols] += project(3, qk_cols) + project(1, qk_cols)
    w_qk.pass_opposite()
    w_qk.n2.wait_recv()
    with jax.named_scope("queries"):
        qk = gate[:, qk_cols] + project(2, qk_cols)
        qraw[...] = qk[:, :COLS]
        kraw[...] = qk[:, COLS:]
        stat[me.t] = pair_of_sums(qraw[...] * qraw[...], kraw[...] * kraw[...])
    stat_slots = net.take(7)
    stats = [
        net.put(stat.at[me.t], stat.at[me.t], me.to_t(k), stat_slots[k - 1]) for k in range(1, 8)
    ]
    keys[me.c] = two_heads(rotate, kraw[...] * kgain[...], cosine[...], sine[...]).astype(BF)
    k_near = net.put(keys.at[me.c], keys.at[me.c], me.to_core(), kv_slots[2])
    k_far = net.put(keys.at[me.c], keys.at[me.c], me.to_zl(), kv_slots[3])
    w_o.relay()
    w_g.more()
    with jax.named_scope("wait_stats"):
        for copy in stats:
            copy.wait_recv()
    row_slots = net.take(3)
    with jax.named_scope("rotate"):
        sums = jnp.sum(stat[...], axis=0)
        krow[me.c] = sums
        rows_far = [
            net.put(krow.at[me.c], krow.at[me.c], peer, slot)
            for peer, slot in zip(
                (me.to_core(), me.to_zl(), me.to_far()), row_slots, strict=True
            )
        ]
        sums_s[...] = sums.T
        scale_q = lax.rsqrt(sums_s[:, 0:1] / WIDTH + EPS)
        q_norm = qraw[...] * (scale_q * (SCALE * LOG2E)) * qgain[...]
        qrot[...] = two_heads(rotate, q_norm, cosine[...], sine[...]).astype(BF)
    other = (1 - me.zl) * 2 + me.core

    m_s[...] = jnp.full(m_s.shape, 2 * BLOCKED, F32)
    acc[...] = jnp.zeros(acc.shape, F32)

    def allowed_keys(j, rows):
        k_index = j * ROWS + lax.broadcasted_iota(jnp.int32, (BLOCK, ROWS), 1)
        first = me.c * ROWS + rows.start
        q_index = first + lax.broadcasted_iota(jnp.int32, (BLOCK, ROWS), 0)
        return (k_index >= low[rows, 0:1]) & (k_index <= q_index)

    heads = [(h, slice(h * HEAD, (h + 1) * HEAD)) for h in range(2)]

    def key_scale(j):
        return lax.rsqrt(krow[j, 4:5, :] / WIDTH + EPS)

    def attend(b, start, stop):
        rows = block_rows(b)

        def step(i, _):
            j = me.c - i
            allowed = allowed_keys(j, rows)
            scale = key_scale(j)
            raw = [mm_nt(qrot[rows, cols], keys[j, :, cols]) * scale for _, cols in heads]
            probs, fades = [], []
            for h, _ in heads:
                s = jnp.where(allowed, raw[h], BLOCKED)
                m_old = m_s[h, rows]
                m_new = jnp.maximum(m_old, jnp.max(s, axis=1, keepdims=True))
                p = jnp.exp2(s - m_new)
                fade = jnp.exp2(m_old - m_new)
                m_s[h, rows] = m_new
                probs.append(p.astype(BF))
                fades.append(fade)
            ones = jnp.ones((ROWS, HEAD), BF)
            sums = [
                mm(probs[h], jnp.concatenate([vals[j, :, cols], ones], axis=1))
                for h, cols in heads
            ]
            for h, _ in heads:
                acc[h, rows] = acc[h, rows] * fades[h] + sums[h]
            return 0

        with jax.named_scope("attend"):
            lax.fori_loop(start, stop, step, 0)

    def attended(b):
        rows = block_rows(b)
        for h, cols in heads:
            att[rows, cols] = (acc[h, rows, :HEAD] / acc[h, rows, HEAD:]).astype(BF)
            lse[h, rows] = m_s[h, rows] + jnp.log2(acc[h, rows, HEAD : HEAD + 1])
        for f in range(4):
            part_a[rows, f * 512 : (f + 1) * 512] = mm(att[rows], wo[f]).astype(BF)

    w_g.relay()
    w_u.start()
    with jax.named_scope("wait_near"):
        v_near.wait_recv()
        k_near.wait_recv()
        rows_far[0].wait_recv()
        v_far.wait_recv()
        v_on = net.put(vals.at[other], vals.at[other], me.to_core(), kv_slots[4])
    attend(0, 0, 1 + me.core)
    w_g.pass_sides()
    with jax.named_scope("wait_far"):
        k_far.wait_recv()
        k_on = net.put(keys.at[other], keys.at[other], me.to_core(), kv_slots[5])
    attend(1, 0, 1 + me.core)
    with jax.named_scope("wait_far"):
        for copy in (v_on, k_on, rows_far[1], rows_far[2]):
            copy.wait_recv()
    o_sum = reduces(part_a, 0)
    to_hid = gathers(hid)
    w_o.pass_on()
    w_g.pass_opposite()
    attend(0, 1 + me.core, me.c + 1)
    w_o.wait()
    attended(0)
    o_sum[0].start()
    attend(1, 1 + me.core, me.c + 1)
    attended(1)
    o_sum[0].mid()
    o_sum[1].start()
    w_u.relay()
    w_v.left()
    w_qk.left()
    w_d.start()
    net.left(v_near, v_far, k_near, k_far, v_on, k_on, *stats, *rows_far)

    def hidden(b):
        value = o_sum[b].result()
        ochunk[b] = value
        own = tok[o_sum[b].at(0, size=CHUNK)].astype(F32)
        to_hid[b].start((own + value * rms(value) * again[...]).astype(BF))

    o_sum[0].cross()
    o_sum[1].mid()
    hidden(0)
    o_sum[1].cross()
    w_d.relay()
    w_g.pass_far()
    to_hid[0].mid()
    w_u.pass_on()
    hidden(1)
    q_far = net.put(qrot, qfar.at[me.core], me.to_zl())
    for k in (1, 3):
        GradSum.grant(credit.at[0], me.to_y(k))
    to_hid[0].end()

    m_sum = reduces(part_b, 1)
    to_m = gathers(m_full)

    def gates(b, tiles):
        rows = block_rows(b)
        for n in tiles:
            cols = slice(n * TILE, (n + 1) * TILE)
            g = mm(hid[rows], wg[:, :, cols].reshape(WIDTH, TILE))
            u = mm(hid[rows], wu[:, :, cols].reshape(WIDTH, TILE))
            gate[rows, cols] = g
            up[rows, cols] = u
            mixed[rows, cols] = (g * jax.nn.sigmoid(g) * u).astype(BF)

    def down(b):
        rows = block_rows(b)
        for f in range(4):
            part_b[rows, f * 512 : (f + 1) * 512] = mm(mixed[rows], wd[f]).astype(BF)

    w_d.pass_on()
    w_g.wait()
    w_u.wait()
    with jax.named_scope("gates"):
        gates(0, (0, 1))
    to_hid[1].mid()
    with jax.named_scope("gates"):
        gates(0, (2, 3))
    for s in o_sum:
        s.left()
    w_d.wait()
    down(0)
    m_sum[0].start()
    q_far.wait_recv()
    q_on = net.put(qfar.at[me.core], qfar.at[me.core], me.to_core())
    to_hid[1].end()
    with jax.named_scope("gates"):
        gates(1, (0, 1, 2, 3))
    m_sum[0].mid()
    down(1)
    m_sum[1].start()
    m_sum[0].cross()
    m_sum[1].mid()
    cot_copy.wait()
    for g in to_hid:
        g.left()
    q_on.wait_recv()
    net.left(q_far, q_on)
    for w in (w_v, w_qk, w_o, w_g, w_u):
        net.give(w.slots)
    to_m[0].start(m_sum[0].result().astype(BF))
    m_sum[1].cross()
    to_m[0].mid()
    to_m[1].start(m_sum[1].result().astype(BF))
    for s in m_sum:
        s.left()
    gm_s[...] = jnp.zeros(gm_s.shape, F32)

    h_sum = reduces(part_a, 0)
    to_do = gathers(do_full)

    def norm_rows(b):
        def some_rows(i, _):
            some = rows_of(b * BLOCK + i * 64, 64, 64)
            m = m_full[some].astype(F32)
            g = cot[some].astype(F32)
            r = rms(m)
            mr = m * r
            part_b[some] = (hid[some].astype(F32) + mr * mgain[...]).astype(BF)
            d_m[some] = norm_back(g, m, r, mgain[...]).astype(BF)
            gm_s[...] += jnp.sum(g * mr, axis=0, keepdims=True)
            return 0

        with jax.named_scope("norm_rows"):
            lax.fori_loop(0, BLOCK // 64, some_rows, 0)
        return net.local(part_b.at[block_rows(b)], out_h.at[block_rows(b)])

    def gates_back(b):
        rows = block_rows(b)
        for n in range(4):
            cols = slice(n * TILE, (n + 1) * TILE)
            d_mixed = mm_nt(d_m[rows, 0:512], wd[0, cols])
            for f in range(1, 4):
                d_mixed += mm_nt(d_m[rows, f * 512 : (f + 1) * 512], wd[f, cols])
            g = gate[rows, cols]
            sigma = jax.nn.sigmoid(g)
            dgate[rows, cols] = (
                d_mixed * up[rows, cols] * sigma * (1.0 + g * (1.0 - sigma))
            ).astype(BF)
            dup[rows, cols] = (d_mixed * (g * sigma)).astype(BF)

    def hidden_back(b):
        rows = block_rows(b)
        for f in range(4):
            for n in range(0, 512, TILE):
                d = mm_nt(dgate[rows], wg[f, n : n + TILE])
                d += mm_nt(dup[rows], wu[f, n : n + TILE])
                part_a[rows, f * 512 + n : f * 512 + n + TILE] = d.astype(BF)

    stores = []
    to_m[0].end()
    stores.append(norm_rows(0))
    to_m[1].mid()
    with jax.named_scope("gates_back"):
        gates_back(0)
    with jax.named_scope("hidden_back"):
        hidden_back(0)
    h_sum[0].start()
    to_m[1].end()
    stores.append(norm_rows(1))
    for g in to_m:
        g.left()
    pl.semaphore_signal(ready, inc=1, device_id=me.to_core(), device_id_type=MESH)
    h_sum[0].mid()
    with jax.named_scope("gates_back"):
        gates_back(1)
    with jax.named_scope("hidden_back"):
        hidden_back(1)
    h_sum[1].start()

    def columns(ref, f):
        return ref.at[:, pl.ds(f * 512, 512)]

    def quarter(ref, f, cols=1024):
        return ref.at[pl.ds(f // 2 * 256, 256), pl.ds(f % 2 * 1024, cols)]

    def half(pair, f):
        return pair[f // 2].at[pl.ds(f % 2 * 256, 256)]

    near_a, near_b, far_a, far_b, far_c = (net.take(n) for n in (4, 4, 6, 6, 6))

    def in_tok(slot, lower):
        return tok.at[pl.ds(lower * 256, 256), pl.ds(slot * 512, 512)]

    g_down = GradSum(
        net, me, wd, [columns(m_full, f) for f in range(4)],
        (credit.at[0], credit.at[5]), gdown_h, near_a, far_a, in_tok,
    )
    g_gate = GradSum(net, me, wg, [quarter(d_m, f) for f in range(4)], (credit.at[1], credit.at[6]),
        ggate_h, near_b, far_b,
    )
    g_up = GradSum(
        net, me, wu, [half((mixed, dgate), f) for f in range(4)], (credit.at[2], credit.at[7]),
        gup_h, near_a, far_a,
    )
    with jax.named_scope("grad_down"):
        for f in range(4):
            wd[f] = mm_tn(mixed[...], d_m[:, f * 512 : (f + 1) * 512]).astype(BF)
    pl.semaphore_wait(ready, 1)
    g_down.start()
    h_sum[0].cross()
    h_sum[1].mid()
    g_down.add()
    g_down.spread()
    with jax.named_scope("grad_gate"):
        for f in range(4):
            wg[f] = mm_tn(hid[:, f * 512 : (f + 1) * 512], dgate[...]).astype(BF)
    g_down.release()

    def back_to_o(b):
        d_hidden = cot[h_sum[b].at(0, size=CHUNK)].astype(F32) + h_sum[b].result()
        value = ochunk[b]
        r = rms(value)
        to_do[b].start(norm_back(d_hidden, value, r, again[...]).astype(BF))
        ochunk[b] = d_hidden
        return jnp.sum(d_hidden * (value * r), axis=0, keepdims=True)

    ga = back_to_o(0)
    g_gate.start()
    h_sum[1].cross()
    to_do[0].mid()
    with jax.named_scope("grad_up"):
        for f in range(4):
            wu[f] = mm_tn(hid[:, f * 512 : (f + 1) * 512], dup[...]).astype(BF)
    ga = ga + back_to_o(1)
    ga_s[me.x] = jnp.broadcast_to(ga, (8, WIDTH))
    ga_far = [net.put(ga_s.at[me.x], ga_s.at[me.x], me.to_x(k)) for k in (1, 3, 2)]
    g_down.relay()
    to_do[0].end()

    dk, dv, deltas, dn = gate, up, m_s, acc
    dk[...] = jnp.zeros(dk.shape, F32)
    dv[...] = jnp.zeros(dv.shape, F32)
    dq[...] = jnp.zeros(dq.shape, F32)

    def attended_back(b):
        rows = block_rows(b)
        d = mm_nt(do_full[rows, 0:512], wo[0])
        for f in range(1, 4):
            d += mm_nt(do_full[rows, f * 512 : (f + 1) * 512], wo[f])
        d_att[rows] = d.astype(BF)

    def attend_back(b, start, stop, with_keys):
        rows = block_rows(b)
        q = [qrot[rows, cols] for _, cols in heads]
        e = [d_att[rows, cols] for _, cols in heads]
        delta = [deltas[h, rows] for h, _ in heads]

        def step(j, _):
            allowed = allowed_keys(j, rows)
            scale = key_scale(j)
            raw = [mm_nt(q[h], keys[j, :, cols]) * scale for h, cols in heads]
            d_probs = [mm_nt(e[h], vals[j, :, cols]) for h, cols in heads]
            probs, d_scores = [], []
            for h, _ in heads:
                s = jnp.where(allowed, raw[h] - lse[h, rows], BLOCKED)
                p = jnp.exp2(s)
                probs.append(p.astype(BF))
                d_scores.append((p * (d_probs[h] - delta[h]) * scale).astype(BF))
            for h, cols in heads:
                dq[rows, cols] += mm(d_scores[h], keys[j, :, cols])
                if with_keys:
                    there = pl.ds(pl.multiple_of((j - home) * COLS + h * HEAD, HEAD), HEAD)
                    dk[:, there] += mm_tn(d_scores[h], q[h])
                    dv[:, there] += mm_tn(probs[h], e[h])
            return 0

        with jax.named_scope("attend_back"):
            lax.fori_loop(start, stop, step, 0)

    def keys_back(b):
        rows = block_rows(b)

        def step(_, none, i):
            cols8 = sfar[i, b].T
            k_index = me.c * ROWS + lax.broadcasted_iota(jnp.int32, (BLOCK, ROWS), 1)
            allowed = k_index >= lowfar[i, rows, 0:1]
            scale = key_scale(me.c)
            q = [qfar[i, rows, cols] for _, cols in heads]
            e = [efar[i, rows, cols] for _, cols in heads]
            raw = [mm_nt(q[h], keys[me.c, :, cols]) * scale for h, cols in heads]
            d_probs = [mm_nt(e[h], vals[me.c, :, cols]) for h, cols in heads]
            probs, d_scores = [], []
            for h, _ in heads:
                s = jnp.where(allowed, raw[h] - cols8[:, h : h + 1], BLOCKED)
                p = jnp.exp2(s)
                probs.append(p.astype(BF))
                d = d_probs[h] - cols8[:, 2 + h : 3 + h]
                d_scores.append((p * d * scale).astype(BF))
            for h, cols in heads:
                there = pl.ds(pl.multiple_of(me.core * COLS + h * HEAD, HEAD), HEAD)
                dk[:, there] += mm_tn(d_scores[h], q[h])
                dv[:, there] += mm_tn(probs[h], e[h])
            return 0

        for i in (me.core, 1 - me.core):
            if i is not me.core:
                for copy in forward[b]:
                    copy.wait_recv()
            with jax.named_scope("keys_back"):
                lax.fori_loop(0, 1 - me.zl, functools.partial(step, i=i), 0)

    home, away = me.zl * 2, (1 - me.zl) * 2
    cross, forward = {}, {}

    def send_far(b):
        rows = block_rows(b)
        for h, cols in heads:
            e, a = d_att[rows, cols].astype(F32), att[rows, cols].astype(F32)
            deltas[h, rows] = jnp.sum(e * a, axis=1, keepdims=True)
        four = [lse[0, rows], lse[1, rows], deltas[0, rows], deltas[1, rows]]
        srow[b] = jnp.concatenate(four + four, axis=1).T
        cross[b] = [
            net.put(d_att.at[rows], efar.at[me.core, rows], me.to_zl(), cross_far[2 * b]),
            net.put(srow.at[b], sfar.at[me.core, b], me.to_zl(), cross_far[2 * b + 1]),
        ]

    def forward_far(b):
        for copy in cross[b]:
            copy.wait_recv()
        e, s = efar.at[me.core, block_rows(b)], sfar.at[me.core, b]
        forward[b] = [
            net.put(e, e, me.to_core(), on_slots[2 * b]),
            net.put(s, s, me.to_core(), on_slots[2 * b + 1]),
        ]

    cross_far, on_slots = kv_slots[:4], kv_slots[4:] + row_slots[:2]
    attended_back(0)
    send_far(0)
    g_gate.add()
    g_up.start()
    g_gate.spread()
    attend_back(0, away, away + 2 * me.zl, False)
    to_do[1].mid()
    attend_back(0, home, me.c + 1, True)
    forward_far(0)
    g_down.cross()
    tok_copy = net.local(tok_h, tok)
    keys_back(0)
    to_do[1].end()
    attended_back(1)
    send_far(1)
    g_down.cross_half()
    attend_back(1, away, away + 2 * me.zl, False)
    g_gate.relay()
    attend_back(1, home, me.c + 1, True)
    g_up.add()
    partner = pl.ds(pl.multiple_of((1 - me.core) * COLS, COLS), COLS)
    own = pl.ds(pl.multiple_of(me.core * COLS, COLS), COLS)

    def key_root(j):
        return jnp.sqrt(krow[j].T[:, 4:5] / WIDTH + EPS) * (1.0 / LOG2E)

    d_m[:, :COLS] = (dk[:, partner] * key_root(home + 1 - me.core)).astype(BF)
    d_m[:, COLS : 2 * COLS] = dv[:, partner].astype(BF)
    from_core = dup.at[:, pl.ds(0, 2 * COLS)]
    swap = net.put(d_m.at[:, pl.ds(0, 2 * COLS)], from_core, me.to_core(), row_slots[2])
    forward_far(1)
    with jax.named_scope("rotate_back"):
        dn[0] = two_heads(rotate_back, dq[...] * SCALE, cosine[...], sine[...])
    g_up.spread()
    keys_back(1)
    with jax.named_scope("wait_swap"):
        swap.wait_recv()
    own_root = key_root(me.c)
    d_k = dk[:, own] * own_root + from_core[:, :COLS].astype(F32)
    d_v = dv[:, own] + from_core[:, COLS:].astype(F32)
    with jax.named_scope("rotate_back"):
        dn[1] = two_heads(rotate_back, d_k, cosine[...], sine[...])
        dqkv[:, 2 * COLS :] = d_v.astype(BF)
        scaled_q = dn[0] * qgain[...]
        scaled_k = dn[1] * kgain[...]
        stat2[me.t] = pair_of_sums(scaled_q * qraw[...], scaled_k * kraw[...])
    stats = [
        net.put(stat2.at[me.t], stat2.at[me.t], me.to_t(k), stat_slots[k - 1])
        for k in range(1, 8)
    ]
    scale_q = lax.rsqrt(sums_s[:, 0:1] / WIDTH + EPS)
    scale_k = lax.rsqrt(sums_s[:, 4:5] / WIDTH + EPS)
    for copy in ga_far:
        copy.wait_recv()
    gy[me.f] = jnp.zeros((8, WIDTH), F32)
    gy[me.f, 0:1] = jnp.sum(ga_s[...], axis=0)[0:1]
    gy[me.f, 1:2] = gm_s[...]
    gy[me.f, 2:3, :COLS] = jnp.sum(dn[0] * (qraw[...] * scale_q), axis=0, keepdims=True)
    gy[me.f, 2:3, COLS : 2 * COLS] = jnp.sum(
        dn[1] * (kraw[...] * scale_k), axis=0, keepdims=True
    )
    gains = [net.put(gy.at[me.f], gy.at[me.f], me.to_y(k)) for k in (1, 3, 2)]
    with jax.named_scope("grad_output"):
        for g in to_do:
            g.left()
        g_out = GradSum(
            net, me, wo, [mixed.at[pl.ds(f * 128, 128), pl.ds(0, 512)] for f in range(4)],
            (credit.at[3], credit.at[8]), gout_h, near_b, far_b,
        )
        for f in range(4):
            wo[f] = mm_tn(att[...], do_full[:, f * 512 : (f + 1) * 512]).astype(BF)
        g_out.start()
    with jax.named_scope("wait_stats"):
        for copy in stats:
            copy.wait_recv()
    dots = jnp.sum(stat2[...], axis=0).T / WIDTH
    dqkv[:, :COLS] = (
        scale_q * scaled_q - qraw[...] * (scale_q * scale_q * scale_q * dots[:, 0:1])
    ).astype(BF)
    dqkv[:, COLS : 2 * COLS] = (
        scale_k * scaled_k - kraw[...] * (scale_k * scale_k * scale_k * dots[:, 4:5])
    ).astype(BF)

    for copy in stores:
        copy.wait()
    for s in h_sum:
        s.left()
    x_sum = reduces(part_b, 1)
    to_ig = gathers(m_full)

    def input_back(b):
        rows = block_rows(b)
        for f in range(4):
            for n in range(0, 512, TILE):
                d = mm_nt(dqkv[rows], wqkv[f, n : n + TILE])
                part_b[rows, f * 512 + n : f * 512 + n + TILE] = d.astype(BF)

    def input_grad(b):
        to_ig[b].start((ochunk[b] + x_sum[b].result()).astype(BF))

    g_gate.cross()
    g_gate.cross_half()
    with jax.named_scope("input_back"):
        input_back(0)
    x_sum[0].start()
    g_out.add()
    with jax.named_scope("input_back"):
        input_back(1)
    g_qkv = GradSum(
        net, me, wqkv, [quarter(do_full, f, 3 * COLS) for f in range(4)], (credit.at[4], credit.at[9]),
        gqkv_h, near_a, far_c,
    )
    tok_copy.wait()
    with jax.named_scope("grad_qkv"):
        for f in range(4):
            wqkv[f] = mm_tn(tok[:, f * 512 : (f + 1) * 512], dqkv[...]).astype(BF)
    g_qkv.start()
    x_sum[0].mid()
    x_sum[1].start()
    g_up.relay()
    g_out.spread()
    g_qkv.add()
    g_qkv.spread()
    x_sum[0].cross()
    x_sum[1].mid()
    g_up.cross()
    g_out.relay()
    input_grad(0)
    x_sum[1].cross()
    g_up.cross_half()
    g_qkv.relay()
    to_ig[0].mid()
    g_down.finish()
    g_gate.finish()
    input_grad(1)
    g_out.cross()
    g_out.cross_half()
    g_qkv.cross()
    g_qkv.cross_half()
    for copy in gains:
        copy.wait_recv()
    gz[...] = gy[0] + gy[1] + gy[2] + gy[3]
    gain_z = net.put(gz, gzr, me.to_zl())
    to_ig[0].end()
    stores = [net.local(m_full.at[block_rows(0)], ig_h.at[block_rows(0)])]
    to_ig[1].mid()
    g_up.finish()
    gain_z.wait_recv()
    gc[...] = gz[...] + gzr[...]
    gain_c = net.put(gc, gcr, me.to_core())
    to_ig[1].end()
    stores.append(net.local(m_full.at[block_rows(1)], ig_h.at[block_rows(1)]))
    g_out.finish()
    g_qkv.finish()
    gain_c.wait_recv()
    gcr[...] = gc[...] + gcr[...]
    stores.append(net.local(gcr, gains_h))
    for g in (g_down, g_gate, g_up, g_out, g_qkv):
        g.end()
    for copy in stores:
        copy.wait()
    net.finish()


def sds(*shape, dtype=BF):
    return jax.ShapeDtypeStruct(shape, dtype)


VM = pl.BlockSpec(memory_space=pltpu.VMEM)
ANY = pl.BlockSpec(memory_space=pl.ANY)


def layer(*args):
    def buf(*shape, dtype=BF):
        return pltpu.VMEM(shape, dtype)

    def wide(*shape):
        return pltpu.VMEM(shape, F32)

    reduce_bufs = [
        buf(2, 2, HALF, WIDTH),
        buf(2, 2, CHUNK, WIDTH),
        buf(2, CHUNK, WIDTH),
        buf(2, CHUNK, WIDTH),
    ]
    return pl.pallas_call(
        layer_body,
        name="layer",
        out_shape=[
            sds(ROWS, WIDTH),
            sds(ROWS, WIDTH),
            sds(HIDDEN, 512),
            sds(512, HIDDEN),
            sds(512, HIDDEN),
            sds(512, 3 * COLS),
            sds(COLS, 512),
            sds(8, WIDTH, dtype=F32),
        ],
        out_specs=[ANY] * 8,
        in_specs=[ANY, ANY] + [VM] * 6 + [ANY] * 7,
        scratch_shapes=[
            buf(ROWS, WIDTH),
            buf(ROWS, WIDTH),
            buf(4, 512, 3 * COLS),
            buf(4, COLS, 512),
            buf(4, 512, HIDDEN),
            buf(4, 512, HIDDEN),
            buf(4, HIDDEN, 512),
            buf(ROWS, WIDTH),
            wide(ROWS, HIDDEN),
            wide(ROWS, HIDDEN),
            buf(ROWS, HIDDEN),
            buf(ROWS, HIDDEN),
            buf(ROWS, HIDDEN),
            buf(ROWS, WIDTH),
            buf(ROWS, WIDTH),
            buf(ROWS, WIDTH),
            buf(ROWS, WIDTH),
            buf(ROWS, WIDTH),
            *reduce_bufs,
            *reduce_bufs,
            wide(2, CHUNK, WIDTH),
            wide(ROWS, COLS),
            wide(ROWS, COLS),
            wide(ROWS, 8),
            buf(ROWS, COLS),
            buf(4, ROWS, COLS),
            buf(4, ROWS, COLS),
            buf(ROWS, COLS),
            wide(2, ROWS, 1),
            wide(2, ROWS, 1),
            wide(2, ROWS, 2 * HEAD),
            wide(ROWS, COLS),
            wide(ROWS, HEAD),
            wide(ROWS, HEAD),
            pltpu.VMEM((ROWS, HEAD), jnp.int32),
            pltpu.VMEM((2, ROWS, HEAD), jnp.int32),
            wide(8, 8, ROWS),
            wide(8, 8, ROWS),
            wide(4, 8, ROWS),
            buf(2, ROWS, COLS),
            buf(2, ROWS, COLS),
            wide(2, 2, 8, BLOCK),
            wide(2, 8, BLOCK),
            buf(ROWS, 3 * COLS),
            buf(ROWS, COLS),
            wide(4, 8, WIDTH),
            wide(1, WIDTH),
            wide(4, 8, WIDTH),
            *[wide(8, WIDTH) for _ in range(4)],
            pltpu.SemaphoreType.DMA((SENDS,)),
            pltpu.SemaphoreType.DMA((SLOTS,)),
            pltpu.SemaphoreType.DMA((20,)),
            pltpu.SemaphoreType.REGULAR((10,)),
            pltpu.SemaphoreType.REGULAR,
        ],
        compiler_params=pltpu.CompilerParams(
            collective_id=1, has_side_effects=True, vmem_limit_bytes=63 * MIB
        ),
    )(*args)


ARRAYS = (
    (ROWS, WIDTH),
    (ROWS, WIDTH),
    (HIDDEN, 512),
    (512, HIDDEN),
    (512, HIDDEN),
    (COLS, 512),
    (512, 3 * COLS),
)


def finish_body(*refs):
    arrays, gains, outs, rest = refs[:7], refs[7], refs[8:21], refs[21:]
    ins, few, wides, (in_sem, out_sem) = rest[:7], rest[7], rest[8:15], rest[15:]
    order = (1, 2, 3, 4, 6, 5, 0)
    loads = {}
    for i in order:
        loads[i] = pltpu.make_async_copy(arrays[i], ins[i], in_sem.at[i])
        loads[i].start()
    few_load = pltpu.make_async_copy(gains, few, in_sem.at[7])
    few_load.start()
    stores = []

    def store(src, i):
        stores.append(pltpu.make_async_copy(src, outs[i], out_sem.at[i]))
        stores[-1].start()

    for i in order:
        loads[i].wait()
        if i == 0:
            store(ins[0], 0)
        elif i == 6:
            for k in range(3):
                wides[6][k] = ins[6][:, k * COLS : (k + 1) * COLS].astype(F32)
                store(wides[6].at[k], 6 + k)
        else:
            wides[i][...] = ins[i][...].astype(F32)
            store(wides[i], i)
    few_load.wait()
    for i in range(2):
        store(few.at[pl.ds(i, 1)], 9 + i)
        store(few.at[pl.ds(2, 1), pl.ds(i * COLS, COLS)], 11 + i)
    for copy in stores:
        copy.wait()


def finish(*args):
    outs = [sds(ROWS, WIDTH)] + [sds(*s, dtype=F32) for s in ARRAYS[1:6]]
    outs += [sds(512, COLS, dtype=F32)] * 3
    outs += [sds(1, n, dtype=F32) for n in (WIDTH, WIDTH, COLS, COLS)]
    wides = [(8, 128), *ARRAYS[1:6], (3, 512, COLS)]
    return pl.pallas_call(
        finish_body,
        name="to_float",
        out_shape=outs,
        out_specs=[ANY] * 13,
        in_specs=[ANY] * 8,
        scratch_shapes=[pltpu.VMEM(s, BF) for s in ARRAYS]
        + [pltpu.VMEM((8, WIDTH), F32)]
        + [pltpu.VMEM(s, F32) for s in wides]
        + [pltpu.SemaphoreType.DMA((8,)), pltpu.SemaphoreType.DMA((13,))],
        compiler_params=pltpu.CompilerParams(vmem_limit_bytes=62 * MIB),
    )(*args)


def body(
    tokens, segments, positions, cotangent,
    w_query, w_key, w_value, w_output, w_gate, w_up, w_down,
    query_gain, key_gain, attn_gain, mlp_gain,
):
    del segments
    inverse = ROPE_BASE ** (-np.arange(64, dtype=np.float64) * 2.0 / HEAD)
    freqs = jnp.asarray(np.concatenate([inverse, inverse])[None], F32)
    qgain, kgain, again, mgain = (
        g[None] for g in (query_gain, key_gain, attn_gain, mlp_gain)
    )
    out, d_in, g_down, g_gate, g_up, g_qkv, g_out, gains = layer(
        tokens[0], cotangent[0], positions, freqs, qgain, kgain, again, mgain,
        w_query, w_key, w_value, w_output, w_gate, w_up, w_down,
    )
    out, d_in, g_down, g_gate, g_up, g_out, g_q, g_k, g_v, ga, gm, gq, gk = finish(
        out, d_in, g_down, g_gate, g_up, g_out, g_qkv, gains
    )
    return (
        out[None], d_in[None], g_q, g_k, g_v, g_out, g_gate, g_up, g_down,
        gq[0], gk[0], ga[0], gm[0],
    )


def solution(mesh):
    in_specs = (
        P("fsdp", "context", None),
        P("fsdp", None),
        P("fsdp", None),
        P("fsdp", "context", None),
        P("fsdp", "tensor"),
        P("fsdp", "tensor"),
        P("fsdp", "tensor"),
        P("tensor", "fsdp"),
        P("fsdp", "tensor"),
        P("fsdp", "tensor"),
        P("tensor", "fsdp"),
        P("tensor"),
        P("tensor"),
        P(),
        P(),
    )
    out_specs = (
        P("fsdp", "context", None),
        P("fsdp", "context", None),
        P("fsdp", "tensor"),
        P("fsdp", "tensor"),
        P("fsdp", "tensor"),
        P("tensor", "fsdp"),
        P("fsdp", "tensor"),
        P("fsdp", "tensor"),
        P("tensor", "fsdp"),
        P("tensor"),
        P("tensor"),
        P(),
        P(),
    )
    return jax.shard_map(body, mesh=mesh, in_specs=in_specs, out_specs=out_specs, check_vma=False)
```

```python
import functools

import jax
import jax.numpy as jnp
import numpy as np
from jax import lax
from jax.experimental import pallas as pl
from jax.experimental.pallas import tpu as pltpu
from jax.sharding import PartitionSpec as P

MESH = pl.DeviceIdType.MESH
BF = jnp.bfloat16
F32 = jnp.float32
HEAD = 128
WIDTH = 2048
ROWS = 512
COLS = 256
HIDDEN = 1024
BLOCK = 256
CHUNK = 64
HALF = 32
TILE = 256
EPS = 1e-06
ROPE_BASE = 500000.0
BLOCKED = -1000000000.0
LOG2E = 1.4426950408889634
SCALE = HEAD ** (-0.5)
MIB = 2**20
SLOTS = 103
SENDS = 56


def mm(a, b):
    return lax.dot_general(a, b, (((1,), (0,)), ((), ())), preferred_element_type=F32)


def mm_nt(a, b):
    return lax.dot_general(a, b, (((1,), (1,)), ((), ())), preferred_element_type=F32)


def mm_tn(a, b):
    return lax.dot_general(a, b, (((0,), (0,)), ((), ())), preferred_element_type=F32)


def rows_of(start, size, unit):
    return pl.ds(pl.multiple_of(start, unit), size)


class Place:
    def __init__(self):
        self.f = lax.axis_index("fsdp")
        self.c = lax.axis_index("context")
        self.t = lax.axis_index("tensor")
        self.x = self.t // 2
        self.zh = self.t % 2
        self.zl = self.c // 2
        self.core = self.c % 2

    def x_at(self, k):
        return (self.x + k + 4) % 4

    def to_x(self, k):
        return {"tensor": self.x_at(k) * 2 + self.zh}

    def to_zh(self):
        return {"tensor": self.x * 2 + 1 - self.zh}

    def to_t(self, k):
        return {"tensor": (self.t + k) % 8}

    def to_y(self, k):
        return {"fsdp": (self.f + k) % 4}

    def to_core(self):
        return {"context": self.zl * 2 + 1 - self.core}

    def to_zl(self):
        return {"context": (1 - self.zl) * 2 + self.core}

    def to_far(self):
        return {"context": 3 - self.c}

    def announce(self):
        self.bar = pltpu.get_barrier_semaphore()
        self.peers = [self.to_t(k) for k in range(1, 8)] + [self.to_y(k) for k in range(1, 4)]
        self.peers += [self.to_core(), self.to_zl(), self.to_far()]
        for peer in self.peers:
            pl.semaphore_signal(self.bar, inc=1, device_id=peer, device_id_type=MESH)

    def barrier(self):
        pl.semaphore_wait(self.bar, len(self.peers))


class Net:
    def __init__(self, send, recv, local):
        self.send, self.recv, self.loc = send, recv, local
        self.n = 0
        self.k = 0
        self.free = []
        self.free_sends = list(range(SENDS))
        self.sent = []

    def take(self, count):
        old, self.free = self.free[:count], self.free[count:]
        new = [self.n + i for i in range(count - len(old))]
        self.n += len(new)
        return old + new

    def give(self, slots):
        self.free += slots

    def put(self, src, dst, peer, slot=None):
        if slot is None:
            (slot,) = self.take(1)
        if not self.free_sends:
            self.left(self.sent[0][0])
        number = self.free_sends.pop(0)
        copy = pltpu.make_async_remote_copy(
            src_ref=src,
            dst_ref=dst,
            send_sem=self.send.at[number],
            recv_sem=self.recv.at[slot],
            device_id=peer,
            device_id_type=MESH,
        )
        copy.start()
        self.sent.append((copy, number))
        return copy

    def left(self, *copies):
        for copy in copies:
            for i, (other, number) in enumerate(self.sent):
                if other is copy:
                    copy.wait_send()
                    self.free_sends.append(number)
                    del self.sent[i]
                    break

    def local(self, src, dst):
        copy = pltpu.make_async_copy(src, dst, self.loc.at[self.k])
        self.k += 1
        copy.start()
        return copy

    def finish(self):
        self.left(*[copy for copy, _ in self.sent])


class Reduce:
    def __init__(self, net, me, part, bufs, b, slots):
        self.net, self.me, self.part, self.b, self.slots = net, me, part, b, slots
        self.ra, self.rb, self.zs, self.zr = bufs

    def at(self, k, lower=False, size=HALF):
        start = self.b * BLOCK + self.me.x_at(k) * CHUNK + (HALF if lower else 0)
        return rows_of(start, size, HALF)

    def start(self):
        net, part, b, slots = self.net, self.part, self.b, self.slots
        up, down = self.me.to_x(1), self.me.to_x(-1)
        lower, upper = pl.ds(0, HALF), pl.ds(HALF, HALF)
        self.a0 = net.put(part.at[self.at(2)], self.ra.at[b, 0], up, slots[0])
        self.a1 = net.put(part.at[self.at(2, True)], self.ra.at[b, 1], down, slots[1])
        self.b0 = net.put(part.at[self.at(1, True)], self.rb.at[b, 0, upper], up, slots[2])
        self.b1 = net.put(part.at[self.at(-1)], self.rb.at[b, 1, lower], down, slots[3])

    def mid(self):
        net, me, part, b, slots = self.net, self.me, self.part, self.b, self.slots
        self.a0.wait_recv()
        s = self.at(1)
        part[s] = (part[s].astype(F32) + self.ra[b, 0].astype(F32)).astype(BF)
        self.c0 = net.put(part.at[s], self.rb.at[b, 0, pl.ds(0, HALF)], me.to_x(1), slots[4])
        self.a1.wait_recv()
        s = self.at(-1, True)
        part[s] = (part[s].astype(F32) + self.ra[b, 1].astype(F32)).astype(BF)
        there = self.rb.at[b, 1, pl.ds(HALF, HALF)]
        self.c1 = net.put(part.at[s], there, me.to_x(-1), slots[5])

    def cross(self):
        b = self.b
        for copy in (self.b0, self.b1, self.c0, self.c1):
            copy.wait_recv()
        own = self.part[self.at(0, size=CHUNK)].astype(F32)
        total = own + self.rb[b, 0].astype(F32) + self.rb[b, 1].astype(F32)
        self.zs[b] = total.astype(BF)
        self.z = self.net.put(self.zs.at[b], self.zr.at[b], self.me.to_zh(), self.slots[6])

    def result(self):
        self.z.wait_recv()
        return self.zs[self.b].astype(F32) + self.zr[self.b].astype(F32)

    def left(self):
        self.net.left(self.a0, self.a1, self.b0, self.b1, self.c0, self.c1, self.z)


class Gather:
    def __init__(self, net, me, full, b, slots):
        self.net, self.me, self.full, self.b, self.slots = net, me, full, b, slots

    def at(self, k, lower=False, size=HALF):
        start = self.b * BLOCK + self.me.x_at(k) * CHUNK + (HALF if lower else 0)
        return rows_of(start, size, HALF)

    def send(self, s, k, i):
        ref = self.full.at[s]
        return self.net.put(ref, ref, self.me.to_x(k), self.slots[i])

    def start(self, chunk):
        self.full[self.at(0, size=CHUNK)] = chunk
        self.p0 = self.send(self.at(0), 1, 0)
        self.m0 = self.send(self.at(0, True), -1, 1)
        self.p1 = self.send(self.at(0, True), 1, 2)
        self.m1 = self.send(self.at(0), -1, 3)

    def mid(self):
        self.p0.wait_recv()
        self.f0 = self.send(self.at(-1), 1, 4)
        self.m0.wait_recv()
        self.f1 = self.send(self.at(1, True), -1, 5)

    def end(self):
        for copy in (self.p1, self.m1, self.f0, self.f1):
            copy.wait_recv()

    def left(self):
        self.net.left(self.p0, self.m0, self.p1, self.m1, self.f0, self.f1)


class Weight:
    def __init__(self, net, me, shard, full, slots, own=None):
        self.net, self.me, self.shard, self.full, self.slots = net, me, shard, full, slots
        self.part = shard.shape[0] // self.cuts
        self.own = own or [net.local(shard, full.at[me.f])]

    cuts = 4

    def first(self):
        return self.me.core * 2

    def at(self, lower, parts=1):
        return rows_of((self.first() + lower) * self.part, parts * self.part, self.part)

    def send(self, lower, k, i):
        s, peer = self.at(lower), self.me.to_y(k)
        return self.net.put(
            self.shard.at[s], self.full.at[self.me.f, s], peer, self.slots[i]
        )

    def start(self):
        self.begin()
        self.more()

    def begin(self):
        self.p0, self.m0 = self.send(0, 1, 0), self.send(1, 3, 1)

    def more(self):
        self.p1, self.m1 = self.send(1, 1, 2), self.send(0, 3, 3)

    def hand(self, k, s, peer, i):
        ref = self.full.at[(self.me.f + k) % 4, s]
        return self.net.put(ref, ref, peer, self.slots[i])

    def relay(self):
        self.p0.wait_recv()
        self.f0 = self.hand(3, self.at(0), self.me.to_y(1), 4)
        self.m0.wait_recv()
        self.f1 = self.hand(1, self.at(1), self.me.to_y(3), 5)

    def pass_sides(self):
        core = self.me.to_core()
        self.p1.wait_recv()
        self.n0 = self.hand(3, self.at(0, 2), core, 6)
        self.m1.wait_recv()
        self.n1 = self.hand(1, self.at(0, 2), core, 7)

    def pass_opposite(self):
        self.f0.wait_recv()
        self.f1.wait_recv()
        self.n2 = self.hand(2, self.at(0, 2), self.me.to_core(), 8)

    def pass_on(self):
        self.pass_sides()
        self.pass_opposite()

    def wait(self):
        for copy in (self.n0, self.n1, self.n2):
            copy.wait_recv()
        for copy in self.own:
            copy.wait()
        self.left()

    def left(self):
        near = (self.n0, self.n1, self.n2)
        self.net.left(*near, self.f0, self.f1, self.p0, self.m0, self.p1, self.m1)


class QuarterWeight(Weight):
    cuts = 8

    def first(self):
        return self.me.c * 2

    def both(self, k, i):
        s = self.at(0, 2)
        self.across.append(self.hand(k, s, self.me.to_zl(), i))
        self.near.append(self.hand(k, s, self.me.to_core(), i + 3))

    def pass_sides(self):
        self.across, self.near = [], []
        self.p1.wait_recv()
        self.both(3, 6)
        self.m1.wait_recv()
        self.both(1, 7)

    def pass_opposite(self):
        self.f0.wait_recv()
        self.f1.wait_recv()
        self.both(2, 8)

    def pass_far(self):
        far = rows_of(((self.me.c + 2) % 4) * 2 * self.part, 2 * self.part, self.part)
        for copy, k, i in zip(self.across, (3, 1, 2), (12, 13, 14), strict=True):
            copy.wait_recv()
            self.near.append(self.hand(k, far, self.me.to_core(), i))

    def arrive(self):
        for copy in self.near:
            copy.wait_recv()

    def wait(self):
        self.arrive()
        for copy in self.own:
            copy.wait()
        self.left()

    def left(self):
        own = (self.f0, self.f1, self.p0, self.m0, self.p1, self.m1)
        self.net.left(*self.near, *self.across, *own)


class GradSum:
    def __init__(self, net, me, grad, got, credit, out, near, far, landing=None):
        self.net, self.me, self.grad, self.got = net, me, grad, got
        self.landing = landing
        self.slots = near + far + net.take(3)
        self.credit, self.out = credit, out
        self.half = grad.shape[1] // 2
        self.mine, self.theirs = self.at(me.core), self.at(1 - me.core)

    def at(self, core, lower=0, parts=2):
        start = core * self.half + lower * (self.half // 2)
        return rows_of(start, parts * self.half // 2, self.half // 2)

    def start(self):
        self.near = [
            self.net.put(
                self.grad.at[f, self.theirs], self.got[f], self.me.to_core(), self.slots[f]
            )
            for f in range(4)
        ]

    def add(self):
        net, me = self.net, self.me
        for f in range(4):
            self.near[f].wait_recv()
            here = self.grad[f, self.mine].astype(F32)
            self.grad[f, self.mine] = (here + self.got[f][...].astype(F32)).astype(BF)
        if self.landing is None:
            self.release()

    def release(self):
        self.net.left(*self.near)
        near_y, zl = self.credit
        self.grant(zl, self.me.to_zl())
        if self.landing is None:
            for k in (1, 3):
                self.grant(near_y, self.me.to_y(k))

    @staticmethod
    def grant(credit, peer):
        pl.semaphore_signal(credit, inc=1, device_id=peer, device_id_type=MESH)

    def place(self, slot, lower):
        if self.landing is not None:
            return self.landing(slot, lower)
        return self.grad.at[slot, self.at(1 - self.me.core, lower, 1)]

    def send(self, k, lower, place, way, i):
        me = self.me
        return self.net.put(
            self.grad.at[(me.f + k) % 4, self.at(me.core, lower, 1)],
            self.place(place, lower),
            me.to_y(way),
            self.slots[i],
        )

    def spread(self):
        pl.semaphore_wait(self.credit[0], 2)
        self.a0, self.a1 = self.send(2, 0, 0, 1, 4), self.send(2, 1, 0, 3, 5)
        self.b0, self.b1 = self.send(1, 1, 1, 1, 6), self.send(3, 0, 2, 3, 7)

    def relay(self):
        me = self.me
        for copy, k, lower in ((self.a0, 1, 0), (self.a1, 3, 1)):
            copy.wait_recv()
            f, s = (me.f + k) % 4, self.at(me.core, lower, 1)
            there = self.place(0, lower)[...].astype(F32)
            self.grad[f, s] = (self.grad[f, s].astype(F32) + there).astype(BF)
            if k == 1:
                self.c0 = self.send(1, 0, 1, 1, 8)
            else:
                self.c1 = self.send(3, 1, 2, 3, 9)

    def cross(self):
        for copy in (self.b0, self.b1, self.c0, self.c1):
            copy.wait_recv()
        me = self.me
        for lower in range(2):
            s = self.at(me.core, lower, 1)
            total = self.grad[me.f, s].astype(F32)
            for k in (1, 2):
                total = total + self.place(k, lower)[...].astype(F32)
            self.grad[me.f, s] = total.astype(BF)
        pl.semaphore_wait(self.credit[1], 1)
        self.z = []
        self.cross_half()

    def cross_half(self):
        me, lower = self.me, len(self.z)
        here = self.grad.at[me.f, self.at(me.core, lower, 1)]
        there = self.grad.at[3, self.at(1 - me.core, lower, 1)]
        self.z.append(self.net.put(here, there, me.to_zl(), self.slots[10 + lower]))

    def finish(self):
        for copy in self.z:
            copy.wait_recv()
        me = self.me
        total = self.grad[me.f, self.mine].astype(F32) + self.grad[3, self.theirs].astype(F32)
        self.grad[0, self.theirs] = total.astype(BF)
        final = self.grad.at[0, self.theirs]
        self.store = self.net.local(final, self.out.at[self.mine])
        self.back = self.net.put(final, self.out.at[self.mine], me.to_core(), self.slots[12])

    def end(self):
        self.store.wait()
        self.back.wait_recv()


def rms(value):
    return lax.rsqrt(jnp.mean(value * value, axis=-1, keepdims=True) + EPS)


def norm_back(grad, value, factor, gain):
    scaled = grad * gain
    inner = jnp.mean(scaled * value, axis=-1, keepdims=True)
    return factor * scaled - value * (factor * factor * factor * inner)


def rotate(value, cosine, sine):
    return value * cosine + pltpu.roll(value, 64, axis=1) * sine


def rotate_back(value, cosine, sine):
    return value * cosine - pltpu.roll(value, 64, axis=1) * sine


def two_heads(fn, value, cosine, sine):
    return jnp.concatenate(
        [fn(value[:, :HEAD], cosine, sine), fn(value[:, HEAD:], cosine, sine)], axis=1
    )


def pair_of_sums(first, second):
    one, two = (jnp.sum(v, axis=1, keepdims=True) for v in (first, second))
    wide = jnp.concatenate([one] * 4 + [two] * 4, axis=1).T
    row = lax.broadcasted_iota(jnp.int32, (8, HEAD), 0)
    packed = wide[:, :HEAD]
    for i in range(1, 4):
        packed = jnp.where(row % 4 == i, wide[:, i * HEAD : (i + 1) * HEAD], packed)
    return packed


def as_columns(packed):
    tall = packed.T
    return [
        jnp.concatenate([tall[:, k + i : k + i + 1] for i in range(4)], axis=0) for k in (0, 4)
    ]


def folded(row):
    return jnp.concatenate([row[:, i * COLS : (i + 1) * COLS] for i in range(8)], axis=0)


def layer_body(
    tok_h, cot_h, pos, freqs, qgain, kgain, again, mgain,
    wq_h, wk_h, wv_h, wo_h, wg_h, wu_h, wd_h,
    out_h, ig_h, gdown_h, ggate_h, gup_h, gqkv_h, gout_h, gains_h,
    tok, cot, wqkv, wo, wg, wu, wd, hid, gate, up, mixed, dgate, dup, part_a, part_b,
    m_full, d_m, do_full, ra0, rb0, zs0, zr0, ra1, rb1, zs1, zr1, ochunk,
    qraw, kraw, sums_s, qrot, keys, vals, att, lse, m_s, acc, dq, cosine, sine, low, lowfar,
    stat, stat2, krow, qfar, efar, sfar, srow, dqkv, d_att, ga_s, gm_s, gy, gz, gzr, gc, gcr, gains,
    send, recv, local, credit, ready,
):
    me = Place()
    net = Net(send, recv, local)
    bufs = ((ra0, rb0, zs0, zr0), (ra1, rb1, zs1, zr1))
    me.announce()
    thirds = [
        net.local(w, wqkv.at[me.f, :, pl.ds(i * COLS, COLS)])
        for i, w in enumerate((wq_h, wk_h, wv_h))
    ]
    tok_copy = net.local(tok_h, tok)
    cot_copy = net.local(cot_h, cot)
    w_qk, w_v = (
        kind(net, me, wqkv.at[me.f, :, cols], wqkv.at[:, :, cols], net.take(count), thirds)
        for kind, cols, count in (
            (Weight, pl.ds(0, 2 * COLS), 9),
            (QuarterWeight, pl.ds(2 * COLS, COLS), 15),
        )
    )
    w_o, w_u = (Weight(net, me, w, full, net.take(9)) for w, full in ((wo_h, wo), (wu_h, wu)))
    w_g = QuarterWeight(net, me, wg_h, wg, net.take(15))
    w_d = Weight(net, me, wd_h, wd, w_qk.slots)
    sum_slots = [net.take(6) for _ in range(2)]
    all_slots = [net.take(6) for _ in range(2)]
    cross_slots = [[net.take(1) for _ in range(2)] for _ in range(2)]

    def reduces(part, turn):
        return [
            Reduce(net, me, part, bufs[turn], b, sum_slots[b] + cross_slots[turn][b])
            for b in range(2)
        ]

    def gathers(full):
        return [Gather(net, me, full, b, all_slots[b]) for b in range(2)]

    def block_rows(b):
        return slice(b * BLOCK, (b + 1) * BLOCK)

    here = pos[0:1, pl.ds(pl.multiple_of(me.c * ROWS, ROWS), ROWS)].astype(F32)
    places = jnp.broadcast_to(here, (HEAD, ROWS)).T
    angle = places * freqs[0:1, :]
    lane = lax.broadcasted_iota(jnp.int32, (ROWS, HEAD), 1)
    cosine[...] = jnp.cos(angle)
    sin = jnp.sin(angle)
    sine[...] = jnp.where(lane < HEAD // 2, -sin, sin)
    token = lax.broadcasted_iota(jnp.int32, (ROWS, HEAD), 0)
    low[...] = me.c * ROWS + token - places.astype(jnp.int32)
    for i in range(2):
        there = pos[0:1, (2 + i) * ROWS : (3 + i) * ROWS].astype(F32)
        there = jnp.broadcast_to(there, (HEAD, ROWS)).T
        lowfar[i] = (2 + i) * ROWS + token - there.astype(jnp.int32)
    for copy in thirds:
        copy.wait()
    me.barrier()
    w_v.start()
    tok_copy.wait()
    qk_cols, v_cols = slice(0, 2 * COLS), slice(2 * COLS, 3 * COLS)

    def project(k, cols):
        f = (me.f + k) % 4
        some = tok[:, pl.ds(pl.multiple_of(f * 512, 512), 512)]
        return mm(some, wqkv[f, :, cols])

    gate[:, v_cols] = project(0, v_cols)
    w_v.relay()
    w_qk.start()
    gate[:, qk_cols] = project(0, qk_cols)
    w_v.pass_sides()
    w_v.pass_opposite()
    w_qk.relay()
    w_o.start()
    w_g.begin()
    w_v.pass_far()
    w_qk.pass_sides()
    with jax.named_scope("wait_wv"):
        w_v.arrive()
    with jax.named_scope("values"):
        value = gate[:, v_cols] + project(1, v_cols) + project(2, v_cols) + project(3, v_cols)
        vals[me.c] = value.astype(BF)
    kv_slots = net.take(6)
    v_near = net.put(vals.at[me.c], vals.at[me.c], me.to_core(), kv_slots[0])
    v_far = net.put(vals.at[me.c], vals.at[me.c], me.to_zl(), kv_slots[1])
    w_qk.n0.wait_recv()
    w_qk.n1.wait_recv()
    gate[:, qk_cols] += project(3, qk_cols) + project(1, qk_cols)
    w_qk.pass_opposite()
    w_qk.n2.wait_recv()
    with jax.named_scope("queries"):
        qk = gate[:, qk_cols] + project(2, qk_cols)
        qraw[...] = qk[:, :COLS]
        kraw[...] = qk[:, COLS:]
        stat[me.t] = pair_of_sums(qraw[...] * qraw[...], kraw[...] * kraw[...])
    stat_slots = net.take(7)
    stats = [
        net.put(stat.at[me.t], stat.at[me.t], me.to_t(k), stat_slots[k - 1]) for k in range(1, 8)
    ]
    keys[me.c] = two_heads(rotate, kraw[...] * kgain[...], cosine[...], sine[...]).astype(BF)
    k_near = net.put(keys.at[me.c], keys.at[me.c], me.to_core(), kv_slots[2])
    k_far = net.put(keys.at[me.c], keys.at[me.c], me.to_zl(), kv_slots[3])
    w_o.relay()
    w_g.more()
    with jax.named_scope("wait_stats"):
        for copy in stats:
            copy.wait_recv()
    row_slots = net.take(3)
    with jax.named_scope("rotate"):
        packed = jnp.sum(stat[...], axis=0)
        krow[me.c] = packed
        rows_far = [
            net.put(krow.at[me.c], krow.at[me.c], peer, slot)
            for peer, slot in zip(
                (me.to_core(), me.to_zl(), me.to_far()), row_slots, strict=True
            )
        ]
        sum_q, sum_k = as_columns(packed)
        sums_s[:, 0:1] = sum_q
        sums_s[:, 4:5] = sum_k
        scale_q = lax.rsqrt(sum_q / WIDTH + EPS)
        q_norm = qraw[...] * (scale_q * (SCALE * LOG2E)) * qgain[...]
        qrot[...] = two_heads(rotate, q_norm, cosine[...], sine[...]).astype(BF)
    other = (1 - me.zl) * 2 + me.core

    m_s[...] = jnp.full(m_s.shape, 2 * BLOCKED, F32)
    acc[...] = jnp.zeros(acc.shape, F32)

    def allowed_keys(j, rows):
        k_index = j * ROWS + lax.broadcasted_iota(jnp.int32, (BLOCK, ROWS), 1)
        first = me.c * ROWS + rows.start
        q_index = first + lax.broadcasted_iota(jnp.int32, (BLOCK, ROWS), 0)
        return (k_index >= low[rows, 0:1]) & (k_index <= q_index)

    heads = [(h, slice(h * HEAD, (h + 1) * HEAD)) for h in range(2)]

    def key_scale(j):
        row = jnp.concatenate([krow[j, i : i + 1, :] for i in range(4, 8)], axis=1)
        return lax.rsqrt(row / WIDTH + EPS)

    def attend(b, start, stop):
        rows = block_rows(b)

        def step(i, _):
            j = me.c - i
            allowed = allowed_keys(j, rows)
            scale = key_scale(j)
            raw = [mm_nt(qrot[rows, cols], keys[j, :, cols]) * scale for _, cols in heads]
            probs, fades = [], []
            for h, _ in heads:
                s = jnp.where(allowed, raw[h], BLOCKED)
                m_old = m_s[h, rows]
                m_new = jnp.maximum(m_old, jnp.max(s, axis=1, keepdims=True))
                p = jnp.exp2(s - m_new)
                fade = jnp.exp2(m_old - m_new)
                m_s[h, rows] = m_new
                probs.append(p.astype(BF))
                fades.append(fade)
            ones = jnp.ones((ROWS, HEAD), BF)
            sums = [
                mm(probs[h], jnp.concatenate([vals[j, :, cols], ones], axis=1))
                for h, cols in heads
            ]
            for h, _ in heads:
                acc[h, rows] = acc[h, rows] * fades[h] + sums[h]
            return 0

        with jax.named_scope("attend"):
            lax.fori_loop(start, stop, step, 0)

    def attended(b):
        rows = block_rows(b)
        for h, cols in heads:
            att[rows, cols] = (acc[h, rows, :HEAD] / acc[h, rows, HEAD:]).astype(BF)
            lse[h, rows] = m_s[h, rows] + jnp.log2(acc[h, rows, HEAD : HEAD + 1])
        for f in range(4):
            part_a[rows, f * 512 : (f + 1) * 512] = mm(att[rows], wo[f]).astype(BF)

    w_g.relay()
    w_u.start()
    with jax.named_scope("wait_near"):
        v_near.wait_recv()
        k_near.wait_recv()
        rows_far[0].wait_recv()
        v_far.wait_recv()
        v_on = net.put(vals.at[other], vals.at[other], me.to_core(), kv_slots[4])
    attend(0, 0, 1 + me.core)
    w_g.pass_sides()
    with jax.named_scope("wait_far"):
        k_far.wait_recv()
        k_on = net.put(keys.at[other], keys.at[other], me.to_core(), kv_slots[5])
    attend(1, 0, 1 + me.core)
    with jax.named_scope("wait_far"):
        for copy in (v_on, k_on, rows_far[1], rows_far[2]):
            copy.wait_recv()
    o_sum = reduces(part_a, 0)
    to_hid = gathers(hid)
    w_o.pass_on()
    w_g.pass_opposite()
    attend(0, 1 + me.core, me.c + 1)
    w_o.wait()
    attended(0)
    o_sum[0].start()
    attend(1, 1 + me.core, me.c + 1)
    attended(1)
    o_sum[0].mid()
    o_sum[1].start()
    w_u.relay()
    w_v.left()
    w_qk.left()
    w_d.start()
    net.left(v_near, v_far, k_near, k_far, v_on, k_on, *stats, *rows_far)

    def hidden(b):
        value = o_sum[b].result()
        ochunk[b] = value
        own = tok[o_sum[b].at(0, size=CHUNK)].astype(F32)
        to_hid[b].start((own + value * rms(value) * again[...]).astype(BF))

    o_sum[0].cross()
    o_sum[1].mid()
    hidden(0)
    o_sum[1].cross()
    w_d.relay()
    w_g.pass_far()
    to_hid[0].mid()
    w_u.pass_on()
    hidden(1)
    q_far = net.put(qrot, qfar.at[me.core], me.to_zl())
    for k in (1, 3):
        GradSum.grant(credit.at[0], me.to_y(k))
    to_hid[0].end()

    m_sum = reduces(part_b, 1)
    to_m = gathers(m_full)

    def gates(b, tiles):
        rows = block_rows(b)
        for n in tiles:
            cols = slice(n * TILE, (n + 1) * TILE)
            g = mm(hid[rows], wg[:, :, cols].reshape(WIDTH, TILE))
            u = mm(hid[rows], wu[:, :, cols].reshape(WIDTH, TILE))
            gate[rows, cols] = g
            up[rows, cols] = u
            mixed[rows, cols] = (g * jax.nn.sigmoid(g) * u).astype(BF)

    def down(b):
        rows = block_rows(b)
        for f in range(4):
            part_b[rows, f * 512 : (f + 1) * 512] = mm(mixed[rows], wd[f]).astype(BF)

    w_d.pass_on()
    w_g.wait()
    w_u.wait()
    with jax.named_scope("gates"):
        gates(0, (0, 1))
    to_hid[1].mid()
    with jax.named_scope("gates"):
        gates(0, (2, 3))
    for s in o_sum:
        s.left()
    w_d.wait()
    down(0)
    m_sum[0].start()
    q_far.wait_recv()
    q_on = net.put(qfar.at[me.core], qfar.at[me.core], me.to_core())
    to_hid[1].end()
    with jax.named_scope("gates"):
        gates(1, (0, 1, 2, 3))
    m_sum[0].mid()
    down(1)
    m_sum[1].start()
    m_sum[0].cross()
    m_sum[1].mid()
    cot_copy.wait()
    for g in to_hid:
        g.left()
    q_on.wait_recv()
    net.left(q_far, q_on)
    for w in (w_v, w_qk, w_o, w_g, w_u):
        net.give(w.slots)
    to_m[0].start(m_sum[0].result().astype(BF))
    m_sum[1].cross()
    to_m[0].mid()
    to_m[1].start(m_sum[1].result().astype(BF))
    for s in m_sum:
        s.left()
    gm_s[...] = jnp.zeros(gm_s.shape, F32)

    h_sum = reduces(part_a, 0)
    to_do = gathers(do_full)

    def norm_rows(b):
        def some_rows(i, _):
            some = rows_of(b * BLOCK + i * 64, 64, 64)
            m = m_full[some].astype(F32)
            g = cot[some].astype(F32)
            r = rms(m)
            mr = m * r
            part_b[some] = (hid[some].astype(F32) + mr * mgain[...]).astype(BF)
            d_m[some] = norm_back(g, m, r, mgain[...]).astype(BF)
            gm_s[...] += jnp.sum(g * mr, axis=0, keepdims=True)
            return 0

        with jax.named_scope("norm_rows"):
            lax.fori_loop(0, BLOCK // 64, some_rows, 0)
        return net.local(part_b.at[block_rows(b)], out_h.at[block_rows(b)])

    def gates_back(b):
        rows = block_rows(b)
        for n in range(4):
            cols = slice(n * TILE, (n + 1) * TILE)
            d_mixed = mm_nt(d_m[rows, 0:512], wd[0, cols])
            for f in range(1, 4):
                d_mixed += mm_nt(d_m[rows, f * 512 : (f + 1) * 512], wd[f, cols])
            g = gate[rows, cols]
            sigma = jax.nn.sigmoid(g)
            dgate[rows, cols] = (
                d_mixed * up[rows, cols] * sigma * (1.0 + g * (1.0 - sigma))
            ).astype(BF)
            dup[rows, cols] = (d_mixed * (g * sigma)).astype(BF)

    def hidden_back(b):
        rows = block_rows(b)
        for f in range(4):
            for n in range(0, 512, TILE):
                d = mm_nt(dgate[rows], wg[f, n : n + TILE])
                d += mm_nt(dup[rows], wu[f, n : n + TILE])
                part_a[rows, f * 512 + n : f * 512 + n + TILE] = d.astype(BF)

    stores = []
    to_m[0].end()
    stores.append(norm_rows(0))
    to_m[1].mid()
    with jax.named_scope("gates_back"):
        gates_back(0)
    with jax.named_scope("hidden_back"):
        hidden_back(0)
    h_sum[0].start()
    to_m[1].end()
    stores.append(norm_rows(1))
    for g in to_m:
        g.left()
    pl.semaphore_signal(ready, inc=1, device_id=me.to_core(), device_id_type=MESH)
    h_sum[0].mid()
    with jax.named_scope("gates_back"):
        gates_back(1)
    def columns(ref, f):
        return ref.at[:, pl.ds(f * 512, 512)]

    def quarter(ref, f, cols=1024):
        return ref.at[pl.ds(f // 2 * 256, 256), pl.ds(f % 2 * 1024, cols)]

    def half(pair, f):
        return pair[f // 2].at[pl.ds(f % 2 * 256, 256)]

    near_a, near_b, far_a, far_b, far_c = (net.take(n) for n in (4, 4, 6, 6, 6))

    def in_tok(slot, lower):
        return tok.at[pl.ds(lower * 256, 256), pl.ds(slot * 512, 512)]

    g_down = GradSum(
        net, me, wd, [columns(m_full, f) for f in range(4)],
        (credit.at[0], credit.at[5]), gdown_h, near_a, far_a, in_tok,
    )
    g_gate = GradSum(net, me, wg, [quarter(d_m, f) for f in range(4)], (credit.at[1], credit.at[6]),
        ggate_h, near_b, far_b,
    )
    g_up = GradSum(
        net, me, wu, [half((mixed, dgate), f) for f in range(4)], (credit.at[2], credit.at[7]),
        gup_h, near_a, far_a,
    )
    with jax.named_scope("grad_down"):
        for f in range(4):
            wd[f] = mm_tn(mixed[...], d_m[:, f * 512 : (f + 1) * 512]).astype(BF)
    pl.semaphore_wait(ready, 1)
    g_down.start()
    with jax.named_scope("hidden_back"):
        hidden_back(1)
    h_sum[1].start()

    h_sum[0].cross()
    g_down.add()
    g_down.spread()
    h_sum[1].mid()
    with jax.named_scope("grad_gate"):
        for f in range(4):
            wg[f] = mm_tn(hid[:, f * 512 : (f + 1) * 512], dgate[...]).astype(BF)
    g_down.release()

    def back_to_o(b):
        d_hidden = cot[h_sum[b].at(0, size=CHUNK)].astype(F32) + h_sum[b].result()
        value = ochunk[b]
        r = rms(value)
        to_do[b].start(norm_back(d_hidden, value, r, again[...]).astype(BF))
        ochunk[b] = d_hidden
        return jnp.sum(d_hidden * (value * r), axis=0, keepdims=True)

    ga = back_to_o(0)
    g_gate.start()
    h_sum[1].cross()
    g_down.relay()
    to_do[0].mid()
    with jax.named_scope("grad_up"):
        for f in range(4):
            wu[f] = mm_tn(hid[:, f * 512 : (f + 1) * 512], dup[...]).astype(BF)
    g_gate.add()
    g_up.start()
    ga = ga + back_to_o(1)
    ga_s[me.x] = folded(ga)
    ga_far = [net.put(ga_s.at[me.x], ga_s.at[me.x], me.to_x(k)) for k in (1, 3, 2)]
    g_gate.spread()
    to_do[0].end()

    dk, dv, deltas, dn = gate, up, m_s, acc
    dk[...] = jnp.zeros(dk.shape, F32)
    dv[...] = jnp.zeros(dv.shape, F32)
    dq[...] = jnp.zeros(dq.shape, F32)

    def attended_back(b):
        rows = block_rows(b)
        d = mm_nt(do_full[rows, 0:512], wo[0])
        for f in range(1, 4):
            d += mm_nt(do_full[rows, f * 512 : (f + 1) * 512], wo[f])
        d_att[rows] = d.astype(BF)

    def attend_back(b, start, stop, with_keys):
        rows = block_rows(b)
        q = [qrot[rows, cols] for _, cols in heads]
        e = [d_att[rows, cols] for _, cols in heads]
        delta = [deltas[h, rows] for h, _ in heads]

        def step(j, _):
            allowed = allowed_keys(j, rows)
            scale = key_scale(j)
            raw = [mm_nt(q[h], keys[j, :, cols]) * scale for h, cols in heads]
            d_probs = [mm_nt(e[h], vals[j, :, cols]) for h, cols in heads]
            probs, d_scores = [], []
            for h, _ in heads:
                s = jnp.where(allowed, raw[h] - lse[h, rows], BLOCKED)
                p = jnp.exp2(s)
                probs.append(p.astype(BF))
                d_scores.append((p * (d_probs[h] - delta[h]) * scale).astype(BF))
            for h, cols in heads:
                dq[rows, cols] += mm(d_scores[h], keys[j, :, cols])
                if with_keys:
                    there = pl.ds(pl.multiple_of((j - home) * COLS + h * HEAD, HEAD), HEAD)
                    dk[:, there] += mm_tn(d_scores[h], q[h])
                    dv[:, there] += mm_tn(probs[h], e[h])
            return 0

        with jax.named_scope("attend_back"):
            lax.fori_loop(start, stop, step, 0)

    def keys_back(b):
        rows = block_rows(b)

        def step(_, none, i):
            cols8 = sfar[i, b].T
            k_index = me.c * ROWS + lax.broadcasted_iota(jnp.int32, (BLOCK, ROWS), 1)
            allowed = k_index >= lowfar[i, rows, 0:1]
            scale = key_scale(me.c)
            q = [qfar[i, rows, cols] for _, cols in heads]
            e = [efar[i, rows, cols] for _, cols in heads]
            raw = [mm_nt(q[h], keys[me.c, :, cols]) * scale for h, cols in heads]
            d_probs = [mm_nt(e[h], vals[me.c, :, cols]) for h, cols in heads]
            probs, d_scores = [], []
            for h, _ in heads:
                s = jnp.where(allowed, raw[h] - cols8[:, h : h + 1], BLOCKED)
                p = jnp.exp2(s)
                probs.append(p.astype(BF))
                d = d_probs[h] - cols8[:, 2 + h : 3 + h]
                d_scores.append((p * d * scale).astype(BF))
            for h, cols in heads:
                there = pl.ds(pl.multiple_of(me.core * COLS + h * HEAD, HEAD), HEAD)
                dk[:, there] += mm_tn(d_scores[h], q[h])
                dv[:, there] += mm_tn(probs[h], e[h])
            return 0

        def from_queries(i):
            with jax.named_scope("keys_back"):
                lax.fori_loop(0, 1 - me.zl, functools.partial(step, i=i), 0)

        from_queries(me.core)
        for copy in forward[b]:
            copy.wait_recv()
        from_queries(1 - me.core)

    home, away = me.zl * 2, (1 - me.zl) * 2
    cross, forward = {}, {}

    def send_far(b):
        rows = block_rows(b)
        for h, cols in heads:
            e, a = d_att[rows, cols].astype(F32), att[rows, cols].astype(F32)
            deltas[h, rows] = jnp.sum(e * a, axis=1, keepdims=True)
        four = [lse[0, rows], lse[1, rows], deltas[0, rows], deltas[1, rows]]
        srow[b] = jnp.concatenate(four + four, axis=1).T
        cross[b] = [
            net.put(d_att.at[rows], efar.at[me.core, rows], me.to_zl(), cross_far[2 * b]),
            net.put(srow.at[b], sfar.at[me.core, b], me.to_zl(), cross_far[2 * b + 1]),
        ]

    def forward_far(b):
        for copy in cross[b]:
            copy.wait_recv()
        e, s = efar.at[me.core, block_rows(b)], sfar.at[me.core, b]
        forward[b] = [
            net.put(e, e, me.to_core(), on_slots[2 * b]),
            net.put(s, s, me.to_core(), on_slots[2 * b + 1]),
        ]

    cross_far, on_slots = kv_slots[:4], kv_slots[4:] + row_slots[:2]
    attended_back(0)
    send_far(0)
    attend_back(0, away, away + 2 * me.zl, False)
    to_do[1].mid()
    attend_back(0, home, me.c + 1, True)
    forward_far(0)
    g_down.cross()
    tok_copy = net.local(tok_h, tok)
    keys_back(0)
    g_gate.relay()
    to_do[1].end()
    attended_back(1)
    send_far(1)
    g_down.cross_half()
    attend_back(1, away, away + 2 * me.zl, False)
    attend_back(1, home, me.c + 1, True)
    g_up.add()
    partner = pl.ds(pl.multiple_of((1 - me.core) * COLS, COLS), COLS)
    own = pl.ds(pl.multiple_of(me.core * COLS, COLS), COLS)

    def key_root(j):
        return jnp.sqrt(as_columns(krow[j])[1] / WIDTH + EPS) * (1.0 / LOG2E)

    d_m[:, :COLS] = (dk[:, partner] * key_root(home + 1 - me.core)).astype(BF)
    d_m[:, COLS : 2 * COLS] = dv[:, partner].astype(BF)
    from_core = dup.at[:, pl.ds(0, 2 * COLS)]
    swap = net.put(d_m.at[:, pl.ds(0, 2 * COLS)], from_core, me.to_core(), row_slots[2])
    forward_far(1)
    with jax.named_scope("rotate_back"):
        dn[0] = two_heads(rotate_back, dq[...] * SCALE, cosine[...], sine[...])
    g_up.spread()
    keys_back(1)
    with jax.named_scope("wait_swap"):
        swap.wait_recv()
    own_root = key_root(me.c)
    d_k = dk[:, own] * own_root + from_core[:, :COLS].astype(F32)
    d_v = dv[:, own] + from_core[:, COLS:].astype(F32)
    with jax.named_scope("rotate_back"):
        dn[1] = two_heads(rotate_back, d_k, cosine[...], sine[...])
        dqkv[:, 2 * COLS :] = d_v.astype(BF)
        scaled_q = dn[0] * qgain[...]
        scaled_k = dn[1] * kgain[...]
        stat2[me.t] = pair_of_sums(scaled_q * qraw[...], scaled_k * kraw[...])
    stats = [
        net.put(stat2.at[me.t], stat2.at[me.t], me.to_t(k), stat_slots[k - 1])
        for k in range(1, 8)
    ]
    scale_q = lax.rsqrt(sums_s[:, 0:1] / WIDTH + EPS)
    scale_k = lax.rsqrt(sums_s[:, 4:5] / WIDTH + EPS)
    for copy in ga_far:
        copy.wait_recv()
    gy[me.f] = jnp.zeros((8, 3 * COLS), F32)
    gy[me.f, :, :COLS] = jnp.sum(ga_s[...], axis=0)
    gy[me.f, :, COLS : 2 * COLS] = folded(gm_s[...])
    gy[me.f, 0:1, 2 * COLS :] = jnp.sum(dn[0] * (qraw[...] * scale_q), axis=0, keepdims=True)
    gy[me.f, 1:2, 2 * COLS :] = jnp.sum(dn[1] * (kraw[...] * scale_k), axis=0, keepdims=True)
    gain_y = [net.put(gy.at[me.f], gy.at[me.f], me.to_y(k)) for k in (1, 3, 2)]
    with jax.named_scope("grad_output"):
        for g in to_do:
            g.left()
        g_out = GradSum(
            net, me, wo, [mixed.at[pl.ds(f * 128, 128), pl.ds(0, 512)] for f in range(4)],
            (credit.at[3], credit.at[8]), gout_h, near_b, far_b,
        )
        for f in range(4):
            wo[f] = mm_tn(att[...], do_full[:, f * 512 : (f + 1) * 512]).astype(BF)
        g_out.start()
    with jax.named_scope("wait_stats"):
        for copy in stats:
            copy.wait_recv()
    dot_q, dot_k = (d / WIDTH for d in as_columns(jnp.sum(stat2[...], axis=0)))
    dqkv[:, :COLS] = (
        scale_q * scaled_q - qraw[...] * (scale_q * scale_q * scale_q * dot_q)
    ).astype(BF)
    dqkv[:, COLS : 2 * COLS] = (
        scale_k * scaled_k - kraw[...] * (scale_k * scale_k * scale_k * dot_k)
    ).astype(BF)

    for copy in stores:
        copy.wait()
    for s in h_sum:
        s.left()
    x_sum = reduces(part_b, 1)
    to_ig = gathers(m_full)

    def input_back(b):
        rows = block_rows(b)
        for f in range(4):
            for n in range(0, 512, TILE):
                d = mm_nt(dqkv[rows], wqkv[f, n : n + TILE])
                part_b[rows, f * 512 + n : f * 512 + n + TILE] = d.astype(BF)

    def input_grad(b):
        to_ig[b].start((ochunk[b] + x_sum[b].result()).astype(BF))

    with jax.named_scope("input_back"):
        input_back(0)
    x_sum[0].start()
    g_gate.cross()
    g_gate.cross_half()
    g_up.relay()
    g_out.add()
    with jax.named_scope("input_back"):
        input_back(1)
    g_qkv = GradSum(
        net, me, wqkv, [quarter(do_full, f, 3 * COLS) for f in range(4)], (credit.at[4], credit.at[9]),
        gqkv_h, near_a, far_c,
    )
    tok_copy.wait()
    with jax.named_scope("grad_qkv"):
        for f in range(4):
            wqkv[f] = mm_tn(tok[:, f * 512 : (f + 1) * 512], dqkv[...]).astype(BF)
    g_qkv.start()
    x_sum[0].mid()
    x_sum[1].start()
    g_out.spread()
    g_qkv.add()
    g_qkv.spread()
    for copy in gain_y:
        copy.wait_recv()
    gz[...] = gy[0] + gy[1] + gy[2] + gy[3]
    gain_z = net.put(gz, gzr, me.to_zl())
    x_sum[0].cross()
    g_up.cross()
    x_sum[1].mid()
    g_out.relay()
    input_grad(0)
    x_sum[1].cross()
    g_up.cross_half()
    g_qkv.relay()
    to_ig[0].mid()
    gain_z.wait_recv()
    gc[...] = gz[...] + gzr[...]
    gain_c = net.put(gc, gcr, me.to_core())
    g_down.finish()
    g_gate.finish()
    g_qkv.cross()
    g_qkv.cross_half()
    input_grad(1)
    g_out.cross()
    g_out.cross_half()
    to_ig[0].end()
    stores = [net.local(m_full.at[block_rows(0)], ig_h.at[block_rows(0)])]
    to_ig[1].mid()
    g_up.finish()
    gain_c.wait_recv()
    total = gc[...] + gcr[...]
    for i in range(8):
        cols = slice(i * COLS, (i + 1) * COLS)
        gains[0:1, cols] = total[i : i + 1, :COLS]
        gains[1:2, cols] = total[i : i + 1, COLS : 2 * COLS]
    for i in range(2):
        gains[2:3, i * COLS : (i + 1) * COLS] = total[i : i + 1, 2 * COLS :]
    stores.append(net.local(gains, gains_h))
    to_ig[1].end()
    stores.append(net.local(m_full.at[block_rows(1)], ig_h.at[block_rows(1)]))
    g_qkv.finish()
    g_out.finish()
    for g in (g_down, g_gate, g_up, g_out, g_qkv):
        g.end()
    for copy in stores:
        copy.wait()
    net.finish()


def sds(*shape, dtype=BF):
    return jax.ShapeDtypeStruct(shape, dtype)


VM = pl.BlockSpec(memory_space=pltpu.VMEM)
ANY = pl.BlockSpec(memory_space=pl.ANY)


def layer(*args):
    def buf(*shape, dtype=BF):
        return pltpu.VMEM(shape, dtype)

    def wide(*shape):
        return pltpu.VMEM(shape, F32)

    reduce_bufs = [
        buf(2, 2, HALF, WIDTH),
        buf(2, 2, CHUNK, WIDTH),
        buf(2, CHUNK, WIDTH),
        buf(2, CHUNK, WIDTH),
    ]
    return pl.pallas_call(
        layer_body,
        name="layer",
        out_shape=[
            sds(ROWS, WIDTH),
            sds(ROWS, WIDTH),
            sds(HIDDEN, 512),
            sds(512, HIDDEN),
            sds(512, HIDDEN),
            sds(512, 3 * COLS),
            sds(COLS, 512),
            sds(8, WIDTH, dtype=F32),
        ],
        out_specs=[ANY] * 8,
        in_specs=[ANY, ANY] + [VM] * 6 + [ANY] * 7,
        scratch_shapes=[
            buf(ROWS, WIDTH),
            buf(ROWS, WIDTH),
            buf(4, 512, 3 * COLS),
            buf(4, COLS, 512),
            buf(4, 512, HIDDEN),
            buf(4, 512, HIDDEN),
            buf(4, HIDDEN, 512),
            buf(ROWS, WIDTH),
            wide(ROWS, HIDDEN),
            wide(ROWS, HIDDEN),
            buf(ROWS, HIDDEN),
            buf(ROWS, HIDDEN),
            buf(ROWS, HIDDEN),
            buf(ROWS, WIDTH),
            buf(ROWS, WIDTH),
            buf(ROWS, WIDTH),
            buf(ROWS, WIDTH),
            buf(ROWS, WIDTH),
            *reduce_bufs,
            *reduce_bufs,
            wide(2, CHUNK, WIDTH),
            wide(ROWS, COLS),
            wide(ROWS, COLS),
            wide(ROWS, 8),
            buf(ROWS, COLS),
            buf(4, ROWS, COLS),
            buf(4, ROWS, COLS),
            buf(ROWS, COLS),
            wide(2, ROWS, 1),
            wide(2, ROWS, 1),
            wide(2, ROWS, 2 * HEAD),
            wide(ROWS, COLS),
            wide(ROWS, HEAD),
            wide(ROWS, HEAD),
            pltpu.VMEM((ROWS, HEAD), jnp.int32),
            pltpu.VMEM((2, ROWS, HEAD), jnp.int32),
            wide(8, 8, HEAD),
            wide(8, 8, HEAD),
            wide(4, 8, HEAD),
            buf(2, ROWS, COLS),
            buf(2, ROWS, COLS),
            wide(2, 2, 8, BLOCK),
            wide(2, 8, BLOCK),
            buf(ROWS, 3 * COLS),
            buf(ROWS, COLS),
            wide(4, 8, COLS),
            wide(1, WIDTH),
            wide(4, 8, 3 * COLS),
            *[wide(8, 3 * COLS) for _ in range(4)],
            wide(8, WIDTH),
            pltpu.SemaphoreType.DMA((SENDS,)),
            pltpu.SemaphoreType.DMA((SLOTS,)),
            pltpu.SemaphoreType.DMA((20,)),
            pltpu.SemaphoreType.REGULAR((10,)),
            pltpu.SemaphoreType.REGULAR,
        ],
        compiler_params=pltpu.CompilerParams(
            collective_id=1, has_side_effects=True, vmem_limit_bytes=63 * MIB
        ),
    )(*args)


ARRAYS = (
    (ROWS, WIDTH),
    (ROWS, WIDTH),
    (HIDDEN, 512),
    (512, HIDDEN),
    (512, HIDDEN),
    (COLS, 512),
    (512, 3 * COLS),
)


def finish_body(*refs):
    arrays, gains, outs, rest = refs[:7], refs[7], refs[8:21], refs[21:]
    ins, few, wides, (in_sem, out_sem) = rest[:7], rest[7], rest[8:15], rest[15:]
    order = (1, 2, 3, 4, 6, 5, 0)
    loads = {}
    for i in order:
        loads[i] = pltpu.make_async_copy(arrays[i], ins[i], in_sem.at[i])
        loads[i].start()
    few_load = pltpu.make_async_copy(gains, few, in_sem.at[7])
    few_load.start()
    stores = []

    def store(src, i):
        stores.append(pltpu.make_async_copy(src, outs[i], out_sem.at[i]))
        stores[-1].start()

    for i in order:
        loads[i].wait()
        if i == 0:
            store(ins[0], 0)
        elif i == 6:
            for k in range(3):
                wides[6][k] = ins[6][:, k * COLS : (k + 1) * COLS].astype(F32)
                store(wides[6].at[k], 6 + k)
        else:
            wides[i][...] = ins[i][...].astype(F32)
            store(wides[i], i)
    few_load.wait()
    for i in range(2):
        store(few.at[pl.ds(i, 1)], 9 + i)
        store(few.at[pl.ds(2, 1), pl.ds(i * COLS, COLS)], 11 + i)
    for copy in stores:
        copy.wait()


def finish(*args):
    outs = [sds(ROWS, WIDTH)] + [sds(*s, dtype=F32) for s in ARRAYS[1:6]]
    outs += [sds(512, COLS, dtype=F32)] * 3
    outs += [sds(1, n, dtype=F32) for n in (WIDTH, WIDTH, COLS, COLS)]
    wides = [(8, 128), *ARRAYS[1:6], (3, 512, COLS)]
    return pl.pallas_call(
        finish_body,
        name="to_float",
        out_shape=outs,
        out_specs=[ANY] * 13,
        in_specs=[ANY] * 8,
        scratch_shapes=[pltpu.VMEM(s, BF) for s in ARRAYS]
        + [pltpu.VMEM((8, WIDTH), F32)]
        + [pltpu.VMEM(s, F32) for s in wides]
        + [pltpu.SemaphoreType.DMA((8,)), pltpu.SemaphoreType.DMA((13,))],
        compiler_params=pltpu.CompilerParams(vmem_limit_bytes=62 * MIB),
    )(*args)


def body(
    tokens, segments, positions, cotangent,
    w_query, w_key, w_value, w_output, w_gate, w_up, w_down,
    query_gain, key_gain, attn_gain, mlp_gain,
):
    del segments
    inverse = ROPE_BASE ** (-np.arange(64, dtype=np.float64) * 2.0 / HEAD)
    freqs = jnp.asarray(np.concatenate([inverse, inverse])[None], F32)
    qgain, kgain, again, mgain = (
        g[None] for g in (query_gain, key_gain, attn_gain, mlp_gain)
    )
    out, d_in, g_down, g_gate, g_up, g_qkv, g_out, gains = layer(
        tokens[0], cotangent[0], positions, freqs, qgain, kgain, again, mgain,
        w_query, w_key, w_value, w_output, w_gate, w_up, w_down,
    )
    out, d_in, g_down, g_gate, g_up, g_out, g_q, g_k, g_v, ga, gm, gq, gk = finish(
        out, d_in, g_down, g_gate, g_up, g_out, g_qkv, gains
    )
    return (
        out[None], d_in[None], g_q, g_k, g_v, g_out, g_gate, g_up, g_down,
        gq[0], gk[0], ga[0], gm[0],
    )


def solution(mesh):
    in_specs = (
        P("fsdp", "context", None),
        P("fsdp", None),
        P("fsdp", None),
        P("fsdp", "context", None),
        P("fsdp", "tensor"),
        P("fsdp", "tensor"),
        P("fsdp", "tensor"),
        P("tensor", "fsdp"),
        P("fsdp", "tensor"),
        P("fsdp", "tensor"),
        P("tensor", "fsdp"),
        P("tensor"),
        P("tensor"),
        P(),
        P(),
    )
    out_specs = (
        P("fsdp", "context", None),
        P("fsdp", "context", None),
        P("fsdp", "tensor"),
        P("fsdp", "tensor"),
        P("fsdp", "tensor"),
        P("tensor", "fsdp"),
        P("fsdp", "tensor"),
        P("fsdp", "tensor"),
        P("tensor", "fsdp"),
        P("tensor"),
        P("tensor"),
        P(),
        P(),
    )
    return jax.shard_map(body, mesh=mesh, in_specs=in_specs, out_specs=out_specs, check_vma=False)
```

```python
import functools

import jax
import jax.numpy as jnp
import numpy as np
from jax import lax
from jax.experimental import pallas as pl
from jax.experimental.pallas import tpu as pltpu
from jax.sharding import PartitionSpec as P

MESH = pl.DeviceIdType.MESH
BF = jnp.bfloat16
F32 = jnp.float32
HEAD = 128
WIDTH = 2048
ROWS = 512
COLS = 256
HIDDEN = 1024
BLOCK = 256
CHUNK = 64
HALF = 32
TILE = 256
EPS = 1e-06
ROPE_BASE = 500000.0
BLOCKED = -1000000000.0
LOG2E = 1.4426950408889634
SCALE = HEAD ** (-0.5)
MIB = 2**20
SLOTS = 105
SENDS = 56


def mm(a, b):
    return lax.dot_general(a, b, (((1,), (0,)), ((), ())), preferred_element_type=F32)


def mm_nt(a, b):
    return lax.dot_general(a, b, (((1,), (1,)), ((), ())), preferred_element_type=F32)


def mm_tn(a, b):
    return lax.dot_general(a, b, (((0,), (0,)), ((), ())), preferred_element_type=F32)


def rows_of(start, size, unit):
    return pl.ds(pl.multiple_of(start, unit), size)


class Place:
    def __init__(self):
        self.f = lax.axis_index("fsdp")
        self.c = lax.axis_index("context")
        self.t = lax.axis_index("tensor")
        self.x = self.t // 2
        self.zh = self.t % 2
        self.zl = self.c // 2
        self.core = self.c % 2

    def x_at(self, k):
        return (self.x + k + 4) % 4

    def to_x(self, k):
        return {"tensor": self.x_at(k) * 2 + self.zh}

    def to_zh(self):
        return {"tensor": self.x * 2 + 1 - self.zh}

    def to_t(self, k):
        return {"tensor": (self.t + k) % 8}

    def to_y(self, k):
        return {"fsdp": (self.f + k) % 4}

    def to_core(self):
        return {"context": self.zl * 2 + 1 - self.core}

    def to_zl(self):
        return {"context": (1 - self.zl) * 2 + self.core}

    def to_far(self):
        return {"context": 3 - self.c}

    def announce(self):
        self.bar = pltpu.get_barrier_semaphore()
        self.peers = [self.to_t(k) for k in range(1, 8)] + [self.to_y(k) for k in range(1, 4)]
        self.peers += [self.to_core(), self.to_zl(), self.to_far()]
        for peer in self.peers:
            pl.semaphore_signal(self.bar, inc=1, device_id=peer, device_id_type=MESH)

    def barrier(self):
        pl.semaphore_wait(self.bar, len(self.peers))


class Net:
    def __init__(self, send, recv, local):
        self.send, self.recv, self.loc = send, recv, local
        self.n = 0
        self.k = 0
        self.free = []
        self.free_sends = list(range(SENDS))
        self.sent = []

    def take(self, count):
        old, self.free = self.free[:count], self.free[count:]
        new = [self.n + i for i in range(count - len(old))]
        self.n += len(new)
        return old + new

    def give(self, slots):
        self.free += slots

    def put(self, src, dst, peer, slot=None):
        if slot is None:
            (slot,) = self.take(1)
        number = self.number()
        copy = pltpu.make_async_remote_copy(
            src_ref=src,
            dst_ref=dst,
            send_sem=self.send.at[number],
            recv_sem=self.recv.at[slot],
            device_id=peer,
            device_id_type=MESH,
        )
        copy.start()
        self.sent.append((copy, number))
        return copy

    def make(self, src, dst, peer, slot):
        return pltpu.make_async_remote_copy(
            src_ref=src,
            dst_ref=dst,
            send_sem=self.send.at[self.number()],
            recv_sem=self.recv.at[slot],
            device_id=peer,
            device_id_type=MESH,
        )

    def number(self):
        if not self.free_sends:
            self.left(self.sent[0][0])
        return self.free_sends.pop(0)

    def left(self, *copies):
        for copy in copies:
            for i, (other, number) in enumerate(self.sent):
                if other is copy:
                    copy.wait_send()
                    self.free_sends.append(number)
                    del self.sent[i]
                    break

    def local(self, src, dst):
        copy = pltpu.make_async_copy(src, dst, self.loc.at[self.k])
        self.k += 1
        copy.start()
        return copy

    def finish(self):
        self.left(*[copy for copy, _ in self.sent])


class Reduce:
    def __init__(self, net, me, part, bufs, b, slots):
        self.net, self.me, self.part, self.b, self.slots = net, me, part, b, slots
        self.ra, self.rb, self.zs, self.zr = bufs

    def at(self, k, lower=False, size=HALF):
        start = self.b * BLOCK + self.me.x_at(k) * CHUNK + (HALF if lower else 0)
        return rows_of(start, size, HALF)

    def start(self):
        net, part, b, slots = self.net, self.part, self.b, self.slots
        up, down = self.me.to_x(1), self.me.to_x(-1)
        lower, upper = pl.ds(0, HALF), pl.ds(HALF, HALF)
        self.a0 = net.put(part.at[self.at(2)], self.ra.at[b, 0], up, slots[0])
        self.a1 = net.put(part.at[self.at(2, True)], self.ra.at[b, 1], down, slots[1])
        self.b0 = net.put(part.at[self.at(1, True)], self.rb.at[b, 0, upper], up, slots[2])
        self.b1 = net.put(part.at[self.at(-1)], self.rb.at[b, 1, lower], down, slots[3])

    def mid(self):
        net, me, part, b, slots = self.net, self.me, self.part, self.b, self.slots
        self.a0.wait_recv()
        s = self.at(1)
        part[s] = (part[s].astype(F32) + self.ra[b, 0].astype(F32)).astype(BF)
        self.c0 = net.put(part.at[s], self.rb.at[b, 0, pl.ds(0, HALF)], me.to_x(1), slots[4])
        self.a1.wait_recv()
        s = self.at(-1, True)
        part[s] = (part[s].astype(F32) + self.ra[b, 1].astype(F32)).astype(BF)
        there = self.rb.at[b, 1, pl.ds(HALF, HALF)]
        self.c1 = net.put(part.at[s], there, me.to_x(-1), slots[5])

    def cross(self):
        b = self.b
        for copy in (self.b0, self.b1, self.c0, self.c1):
            copy.wait_recv()
        own = self.part[self.at(0, size=CHUNK)].astype(F32)
        total = own + self.rb[b, 0].astype(F32) + self.rb[b, 1].astype(F32)
        self.zs[b] = total.astype(BF)
        self.z = self.net.put(self.zs.at[b], self.zr.at[b], self.me.to_zh(), self.slots[6])

    def result(self):
        self.z.wait_recv()
        return self.zs[self.b].astype(F32) + self.zr[self.b].astype(F32)

    def left(self):
        self.net.left(self.a0, self.a1, self.b0, self.b1, self.c0, self.c1, self.z)


class Gather:
    def __init__(self, net, me, full, b, slots):
        self.net, self.me, self.full, self.b, self.slots = net, me, full, b, slots

    def at(self, k, lower=False, size=HALF):
        start = self.b * BLOCK + self.me.x_at(k) * CHUNK + (HALF if lower else 0)
        return rows_of(start, size, HALF)

    def send(self, s, k, i):
        ref = self.full.at[s]
        return self.net.put(ref, ref, self.me.to_x(k), self.slots[i])

    def start(self, chunk):
        self.full[self.at(0, size=CHUNK)] = chunk
        self.p0 = self.send(self.at(0), 1, 0)
        self.m0 = self.send(self.at(0, True), -1, 1)
        self.p1 = self.send(self.at(0, True), 1, 2)
        self.m1 = self.send(self.at(0), -1, 3)

    def mid(self):
        self.p0.wait_recv()
        self.f0 = self.send(self.at(-1), 1, 4)
        self.m0.wait_recv()
        self.f1 = self.send(self.at(1, True), -1, 5)

    def end(self):
        for copy in (self.p1, self.m1, self.f0, self.f1):
            copy.wait_recv()

    def left(self):
        self.net.left(self.p0, self.m0, self.p1, self.m1, self.f0, self.f1)


class Weight:
    def __init__(self, net, me, shard, full, slots, own=None):
        self.net, self.me, self.shard, self.full, self.slots = net, me, shard, full, slots
        self.part = shard.shape[0] // self.cuts
        self.own = own or [net.local(shard, full.at[me.f])]

    cuts = 4

    def first(self):
        return self.me.core * 2

    def at(self, lower, parts=1):
        return rows_of((self.first() + lower) * self.part, parts * self.part, self.part)

    def send(self, lower, k, i):
        s, peer = self.at(lower), self.me.to_y(k)
        return self.net.put(
            self.shard.at[s], self.full.at[self.me.f, s], peer, self.slots[i]
        )

    def start(self):
        self.begin()
        self.more()

    def begin(self):
        self.p0, self.m0 = self.send(0, 1, 0), self.send(1, 3, 1)

    def more(self):
        self.p1, self.m1 = self.send(1, 1, 2), self.send(0, 3, 3)

    def hand(self, k, s, peer, i):
        ref = self.full.at[(self.me.f + k) % 4, s]
        return self.net.put(ref, ref, peer, self.slots[i])

    def relay(self):
        self.p0.wait_recv()
        self.f0 = self.hand(3, self.at(0), self.me.to_y(1), 4)
        self.m0.wait_recv()
        self.f1 = self.hand(1, self.at(1), self.me.to_y(3), 5)

    def pass_sides(self):
        core = self.me.to_core()
        self.p1.wait_recv()
        self.n0 = self.hand(3, self.at(0, 2), core, 6)
        self.m1.wait_recv()
        self.n1 = self.hand(1, self.at(0, 2), core, 7)

    def pass_opposite(self):
        self.f0.wait_recv()
        self.f1.wait_recv()
        self.n2 = self.hand(2, self.at(0, 2), self.me.to_core(), 8)

    def pass_on(self):
        self.pass_sides()
        self.pass_opposite()

    def wait(self):
        for copy in (self.n0, self.n1, self.n2):
            copy.wait_recv()
        for copy in self.own:
            copy.wait()
        self.left()

    def left(self):
        near = (self.n0, self.n1, self.n2)
        self.net.left(*near, self.f0, self.f1, self.p0, self.m0, self.p1, self.m1)


class QuarterWeight(Weight):
    cuts = 8

    def first(self):
        return self.me.c * 2

    def both(self, k, i):
        s = self.at(0, 2)
        self.across.append(self.hand(k, s, self.me.to_zl(), i))
        self.near.append(self.hand(k, s, self.me.to_core(), i + 3))

    def pass_sides(self):
        self.across, self.near = [], []
        self.p1.wait_recv()
        self.both(3, 6)
        self.m1.wait_recv()
        self.both(1, 7)

    def pass_opposite(self):
        self.f0.wait_recv()
        self.f1.wait_recv()
        self.across.append(self.hand(2, self.at(0), self.me.to_zl(), 8))
        self.near.append(self.hand(2, self.at(0, 2), self.me.to_core(), 11))

    def pass_rest(self):
        self.across.append(self.hand(2, self.at(1), self.me.to_zl(), 15))

    def pass_far(self):
        far = rows_of(((self.me.c + 2) % 4) * 2 * self.part, 2 * self.part, self.part)
        for copy in self.across[:2]:
            copy.wait_recv()
        for k, i in ((3, 12), (1, 13)):
            self.near.append(self.hand(k, far, self.me.to_core(), i))
        for copy in self.across[2:]:
            copy.wait_recv()
        self.near.append(self.hand(2, far, self.me.to_core(), 14))

    def arrive(self):
        for copy in self.near:
            copy.wait_recv()

    def wait(self):
        self.arrive()
        for copy in self.own:
            copy.wait()
        self.left()

    def left(self):
        own = (self.f0, self.f1, self.p0, self.m0, self.p1, self.m1)
        self.net.left(*self.near, *self.across, *own)


class GradSum:
    def __init__(self, net, me, grad, got, credit, out, near, far, landing=None):
        self.net, self.me, self.grad, self.got = net, me, grad, got
        self.landing = landing
        self.slots = near + far + net.take(3)
        self.credit, self.out = credit, out
        self.half = grad.shape[1] // 2
        self.mine, self.theirs = self.at(me.core), self.at(1 - me.core)

    def at(self, core, lower=0, parts=2):
        start = core * self.half + lower * (self.half // 2)
        return rows_of(start, parts * self.half // 2, self.half // 2)

    def start(self):
        self.near = [
            self.net.put(
                self.grad.at[f, self.theirs], self.got[f], self.me.to_core(), self.slots[f]
            )
            for f in range(4)
        ]

    def add(self):
        net, me = self.net, self.me
        for f in range(4):
            self.near[f].wait_recv()
            here = self.grad[f, self.mine].astype(F32)
            self.grad[f, self.mine] = (here + self.got[f][...].astype(F32)).astype(BF)
        if self.landing is None:
            self.release()

    def release(self):
        self.net.left(*self.near)
        near_y, zl = self.credit
        self.grant(zl, self.me.to_zl())
        if self.landing is None:
            for k in (1, 3):
                self.grant(near_y, self.me.to_y(k))

    @staticmethod
    def grant(credit, peer):
        pl.semaphore_signal(credit, inc=1, device_id=peer, device_id_type=MESH)

    def place(self, slot, lower):
        if self.landing is not None:
            return self.landing(slot, lower)
        return self.grad.at[slot, self.at(1 - self.me.core, lower, 1)]

    def send(self, k, lower, place, way, i):
        me = self.me
        return self.net.put(
            self.grad.at[(me.f + k) % 4, self.at(me.core, lower, 1)],
            self.place(place, lower),
            me.to_y(way),
            self.slots[i],
        )

    def spread(self):
        pl.semaphore_wait(self.credit[0], 2)
        self.a0, self.a1 = self.send(2, 0, 0, 1, 4), self.send(2, 1, 0, 3, 5)
        self.b0, self.b1 = self.send(1, 1, 1, 1, 6), self.send(3, 0, 2, 3, 7)

    def relay(self):
        me = self.me
        for copy, k, lower in ((self.a0, 1, 0), (self.a1, 3, 1)):
            copy.wait_recv()
            f, s = (me.f + k) % 4, self.at(me.core, lower, 1)
            there = self.place(0, lower)[...].astype(F32)
            self.grad[f, s] = (self.grad[f, s].astype(F32) + there).astype(BF)
            if k == 1:
                self.c0 = self.send(1, 0, 1, 1, 8)
            else:
                self.c1 = self.send(3, 1, 2, 3, 9)

    def cross(self):
        for copy in (self.b0, self.b1, self.c0, self.c1):
            copy.wait_recv()
        me = self.me
        for lower in range(2):
            s = self.at(me.core, lower, 1)
            total = self.grad[me.f, s].astype(F32)
            for k in (1, 2):
                total = total + self.place(k, lower)[...].astype(F32)
            self.grad[me.f, s] = total.astype(BF)
        pl.semaphore_wait(self.credit[1], 1)
        self.z = []
        self.cross_half()

    def cross_half(self):
        me, lower = self.me, len(self.z)
        here = self.grad.at[me.f, self.at(me.core, lower, 1)]
        there = self.grad.at[3, self.at(1 - me.core, lower, 1)]
        self.z.append(self.net.put(here, there, me.to_zl(), self.slots[10 + lower]))

    def finish(self):
        for copy in self.z:
            copy.wait_recv()
        me = self.me
        total = self.grad[me.f, self.mine].astype(F32) + self.grad[3, self.theirs].astype(F32)
        self.grad[0, self.theirs] = total.astype(BF)
        final = self.grad.at[0, self.theirs]
        self.store = self.net.local(final, self.out.at[self.mine])
        self.back = self.net.put(final, self.out.at[self.mine], me.to_core(), self.slots[12])

    def end(self):
        self.store.wait()
        self.back.wait_recv()


def rms(value):
    return lax.rsqrt(jnp.mean(value * value, axis=-1, keepdims=True) + EPS)


def norm_back(grad, value, factor, gain):
    scaled = grad * gain
    inner = jnp.mean(scaled * value, axis=-1, keepdims=True)
    return factor * scaled - value * (factor * factor * factor * inner)


def rotate(value, cosine, sine):
    return value * cosine + pltpu.roll(value, 64, axis=1) * sine


def rotate_back(value, cosine, sine):
    return value * cosine - pltpu.roll(value, 64, axis=1) * sine


def two_heads(fn, value, cosine, sine):
    return jnp.concatenate(
        [fn(value[:, :HEAD], cosine, sine), fn(value[:, HEAD:], cosine, sine)], axis=1
    )


def pair_of_sums(first, second):
    one, two = (jnp.sum(v, axis=1, keepdims=True) for v in (first, second))
    wide = jnp.concatenate([one] * 4 + [two] * 4, axis=1).T
    row = lax.broadcasted_iota(jnp.int32, (8, HEAD), 0)
    packed = wide[:, :HEAD]
    for i in range(1, 4):
        packed = jnp.where(row % 4 == i, wide[:, i * HEAD : (i + 1) * HEAD], packed)
    return packed


def as_columns(packed):
    tall = packed.T
    return [
        jnp.concatenate([tall[:, k + i : k + i + 1] for i in range(4)], axis=0) for k in (0, 4)
    ]


def folded(row):
    return jnp.concatenate([row[:, i * COLS : (i + 1) * COLS] for i in range(8)], axis=0)


def layer_body(
    tok_h, cot_h, pos, freqs, qgain, kgain, again, mgain,
    wq_h, wk_h, wv_h, wo_h, wg_h, wu_h, wd_h,
    out_h, ig_h, gdown_h, ggate_h, gup_h, gqkv_h, gout_h, gains_h,
    tok, cot, wqkv, wo, wg, wu, wd, hid, gate, up, mixed, dgate, dup, part_a, part_b,
    m_full, d_m, do_full, ra0, rb0, zs0, zr0, ra1, rb1, zs1, zr1, ochunk,
    qraw, kraw, sums_s, qrot, keys, vals, att, lse, m_s, acc, dq, cosine, sine, low, lowfar,
    stat, stat2, krow, qfar, efar, sfar, srow, dqkv, d_att, ga_s, gm_s, gy, gz, gzr, gc, gcr, gains,
    send, recv, local, credit, ready,
):
    me = Place()
    net = Net(send, recv, local)
    bufs = ((ra0, rb0, zs0, zr0), (ra1, rb1, zs1, zr1))
    me.announce()
    thirds = [
        net.local(w, wqkv.at[me.f, :, pl.ds(i * COLS, COLS)])
        for i, w in enumerate((wq_h, wk_h, wv_h))
    ]
    tok_copy = net.local(tok_h, tok)
    cot_copy = net.local(cot_h, cot)
    w_qk, w_v = (
        kind(net, me, wqkv.at[me.f, :, cols], wqkv.at[:, :, cols], net.take(count), thirds)
        for kind, cols, count in (
            (Weight, pl.ds(0, 2 * COLS), 9),
            (QuarterWeight, pl.ds(2 * COLS, COLS), 16),
        )
    )
    w_o, w_u = (Weight(net, me, w, full, net.take(9)) for w, full in ((wo_h, wo), (wu_h, wu)))
    w_g = QuarterWeight(net, me, wg_h, wg, net.take(16))
    w_d = Weight(net, me, wd_h, wd, w_qk.slots)
    sum_slots = [net.take(6) for _ in range(2)]
    all_slots = [net.take(6) for _ in range(2)]
    cross_slots = [[net.take(1) for _ in range(2)] for _ in range(2)]

    def reduces(part, turn):
        return [
            Reduce(net, me, part, bufs[turn], b, sum_slots[b] + cross_slots[turn][b])
            for b in range(2)
        ]

    def gathers(full):
        return [Gather(net, me, full, b, all_slots[b]) for b in range(2)]

    def block_rows(b):
        return slice(b * BLOCK, (b + 1) * BLOCK)

    here = pos[0:1, pl.ds(pl.multiple_of(me.c * ROWS, ROWS), ROWS)].astype(F32)
    places = jnp.broadcast_to(here, (HEAD, ROWS)).T
    angle = places * freqs[0:1, :]
    lane = lax.broadcasted_iota(jnp.int32, (ROWS, HEAD), 1)
    cosine[...] = jnp.cos(angle)
    sin = jnp.sin(angle)
    sine[...] = jnp.where(lane < HEAD // 2, -sin, sin)
    token = lax.broadcasted_iota(jnp.int32, (ROWS, HEAD), 0)
    low[...] = me.c * ROWS + token - places.astype(jnp.int32)
    for i in range(2):
        there = pos[0:1, (2 + i) * ROWS : (3 + i) * ROWS].astype(F32)
        there = jnp.broadcast_to(there, (HEAD, ROWS)).T
        lowfar[i] = (2 + i) * ROWS + token - there.astype(jnp.int32)
    for copy in thirds:
        copy.wait()
    me.barrier()
    w_v.start()
    tok_copy.wait()
    qk_cols, v_cols = slice(0, 2 * COLS), slice(2 * COLS, 3 * COLS)

    def project(k, cols):
        f = (me.f + k) % 4
        some = tok[:, pl.ds(pl.multiple_of(f * 512, 512), 512)]
        return mm(some, wqkv[f, :, cols])

    gate[:, v_cols] = project(0, v_cols)
    w_v.relay()
    w_qk.start()
    gate[:, qk_cols] = project(0, qk_cols)
    w_v.pass_sides()
    w_v.pass_opposite()
    w_v.pass_rest()
    w_qk.relay()
    w_o.start()
    w_g.begin()
    w_v.pass_far()
    w_qk.pass_sides()
    with jax.named_scope("wait_wv"):
        w_v.arrive()
    with jax.named_scope("values"):
        value = gate[:, v_cols] + project(1, v_cols) + project(2, v_cols) + project(3, v_cols)
        vals[me.c] = value.astype(BF)
    kv_slots = net.take(6)
    v_near = net.put(vals.at[me.c], vals.at[me.c], me.to_core(), kv_slots[0])
    v_far = net.put(vals.at[me.c], vals.at[me.c], me.to_zl(), kv_slots[1])
    w_qk.n0.wait_recv()
    w_qk.n1.wait_recv()
    gate[:, qk_cols] += project(3, qk_cols) + project(1, qk_cols)
    w_qk.pass_opposite()
    w_qk.n2.wait_recv()
    with jax.named_scope("queries"):
        qk = gate[:, qk_cols] + project(2, qk_cols)
        qraw[...] = qk[:, :COLS]
        kraw[...] = qk[:, COLS:]
        stat[me.t] = pair_of_sums(qraw[...] * qraw[...], kraw[...] * kraw[...])
    stat_slots = net.take(7)
    stats = [
        net.put(stat.at[me.t], stat.at[me.t], me.to_t(k), stat_slots[k - 1]) for k in range(1, 8)
    ]
    keys[me.c] = two_heads(rotate, kraw[...] * kgain[...], cosine[...], sine[...]).astype(BF)
    k_near = net.put(keys.at[me.c], keys.at[me.c], me.to_core(), kv_slots[2])
    k_far = net.put(keys.at[me.c], keys.at[me.c], me.to_zl(), kv_slots[3])
    w_o.relay()
    w_g.more()
    with jax.named_scope("wait_stats"):
        for copy in stats:
            copy.wait_recv()
    row_slots = net.take(3)
    with jax.named_scope("rotate"):
        packed = jnp.sum(stat[...], axis=0)
        krow[me.c] = packed
        rows_far = [
            net.put(krow.at[me.c], krow.at[me.c], peer, slot)
            for peer, slot in zip(
                (me.to_core(), me.to_zl(), me.to_far()), row_slots, strict=True
            )
        ]
        sum_q, sum_k = as_columns(packed)
        sums_s[:, 0:1] = sum_q
        sums_s[:, 4:5] = sum_k
        scale_q = lax.rsqrt(sum_q / WIDTH + EPS)
        q_norm = qraw[...] * (scale_q * (SCALE * LOG2E)) * qgain[...]
        qrot[...] = two_heads(rotate, q_norm, cosine[...], sine[...]).astype(BF)
    other = (1 - me.zl) * 2 + me.core

    m_s[...] = jnp.full(m_s.shape, 2 * BLOCKED, F32)
    acc[...] = jnp.zeros(acc.shape, F32)

    def allowed_keys(j, rows):
        k_index = j * ROWS + lax.broadcasted_iota(jnp.int32, (BLOCK, ROWS), 1)
        first = me.c * ROWS + rows.start
        q_index = first + lax.broadcasted_iota(jnp.int32, (BLOCK, ROWS), 0)
        return (k_index >= low[rows, 0:1]) & (k_index <= q_index)

    heads = [(h, slice(h * HEAD, (h + 1) * HEAD)) for h in range(2)]

    def key_scale(j):
        row = jnp.concatenate([krow[j, i : i + 1, :] for i in range(4, 8)], axis=1)
        return lax.rsqrt(row / WIDTH + EPS)

    def attend(b, start, stop):
        rows = block_rows(b)

        def step(i, _):
            j = me.c - i
            allowed = allowed_keys(j, rows)
            scale = key_scale(j)
            raw = [mm_nt(qrot[rows, cols], keys[j, :, cols]) * scale for _, cols in heads]
            probs, fades = [], []
            for h, _ in heads:
                s = jnp.where(allowed, raw[h], BLOCKED)
                m_old = m_s[h, rows]
                m_new = jnp.maximum(m_old, jnp.max(s, axis=1, keepdims=True))
                p = jnp.exp2(s - m_new)
                fade = jnp.exp2(m_old - m_new)
                m_s[h, rows] = m_new
                probs.append(p.astype(BF))
                fades.append(fade)
            ones = jnp.ones((ROWS, HEAD), BF)
            sums = [
                mm(probs[h], jnp.concatenate([vals[j, :, cols], ones], axis=1))
                for h, cols in heads
            ]
            for h, _ in heads:
                acc[h, rows] = acc[h, rows] * fades[h] + sums[h]
            return 0

        with jax.named_scope("attend"):
            lax.fori_loop(start, stop, step, 0)

    def attended(b):
        rows = block_rows(b)
        for h, cols in heads:
            att[rows, cols] = (acc[h, rows, :HEAD] / acc[h, rows, HEAD:]).astype(BF)
            lse[h, rows] = m_s[h, rows] + jnp.log2(acc[h, rows, HEAD : HEAD + 1])
        for f in range(4):
            part_a[rows, f * 512 : (f + 1) * 512] = mm(att[rows], wo[f]).astype(BF)

    w_g.relay()
    w_u.start()
    with jax.named_scope("wait_near"):
        v_near.wait_recv()
        k_near.wait_recv()
        rows_far[0].wait_recv()
        v_far.wait_recv()
        v_on = net.put(vals.at[other], vals.at[other], me.to_core(), kv_slots[4])
    attend(0, 0, 1 + me.core)
    w_g.pass_sides()
    with jax.named_scope("wait_far"):
        k_far.wait_recv()
        k_on = net.put(keys.at[other], keys.at[other], me.to_core(), kv_slots[5])
    attend(1, 0, 1 + me.core)
    with jax.named_scope("wait_far"):
        for copy in (v_on, k_on, rows_far[1], rows_far[2]):
            copy.wait_recv()
    o_sum = reduces(part_a, 0)
    to_hid = gathers(hid)
    w_o.pass_on()
    w_g.pass_opposite()
    attend(0, 1 + me.core, me.c + 1)
    w_o.wait()
    attended(0)
    o_sum[0].start()
    attend(1, 1 + me.core, me.c + 1)
    attended(1)
    o_sum[0].mid()
    o_sum[1].start()
    w_u.relay()
    w_v.left()
    w_qk.left()
    w_d.start()
    net.left(v_near, v_far, k_near, k_far, v_on, k_on, *stats, *rows_far)

    def hidden(b):
        value = o_sum[b].result()
        ochunk[b] = value
        own = tok[o_sum[b].at(0, size=CHUNK)].astype(F32)
        to_hid[b].start((own + value * rms(value) * again[...]).astype(BF))

    o_sum[0].cross()
    w_g.pass_rest()
    o_sum[1].mid()
    hidden(0)
    o_sum[1].cross()
    w_d.relay()
    w_g.pass_far()
    to_hid[0].mid()
    w_u.pass_on()
    hidden(1)
    q_far = net.put(qrot, qfar.at[me.core], me.to_zl())
    for k in (1, 3):
        GradSum.grant(credit.at[0], me.to_y(k))
    to_hid[0].end()

    m_sum = reduces(part_b, 1)
    to_m = gathers(m_full)

    def gates(b, tiles):
        rows = block_rows(b)
        for n in tiles:
            cols = slice(n * TILE, (n + 1) * TILE)
            g = mm(hid[rows], wg[:, :, cols].reshape(WIDTH, TILE))
            u = mm(hid[rows], wu[:, :, cols].reshape(WIDTH, TILE))
            gate[rows, cols] = g
            up[rows, cols] = u
            mixed[rows, cols] = (g * jax.nn.sigmoid(g) * u).astype(BF)

    def down(b):
        rows = block_rows(b)
        for f in range(4):
            part_b[rows, f * 512 : (f + 1) * 512] = mm(mixed[rows], wd[f]).astype(BF)

    w_d.pass_on()
    w_g.wait()
    w_u.wait()
    with jax.named_scope("gates"):
        gates(0, (0, 1))
    to_hid[1].mid()
    with jax.named_scope("gates"):
        gates(0, (2, 3))
    for s in o_sum:
        s.left()
    w_d.wait()
    down(0)
    m_sum[0].start()
    q_far.wait_recv()
    q_on = net.put(qfar.at[me.core], qfar.at[me.core], me.to_core())
    to_hid[1].end()
    with jax.named_scope("gates"):
        gates(1, (0, 1, 2, 3))
    m_sum[0].mid()
    down(1)
    m_sum[1].start()
    m_sum[0].cross()
    m_sum[1].mid()
    cot_copy.wait()
    for g in to_hid:
        g.left()
    q_on.wait_recv()
    net.left(q_far, q_on)
    for w in (w_v, w_qk, w_o, w_g, w_u):
        net.give(w.slots)
    to_m[0].start(m_sum[0].result().astype(BF))
    m_sum[1].cross()
    to_m[0].mid()
    to_m[1].start(m_sum[1].result().astype(BF))
    for s in m_sum:
        s.left()
    gm_s[...] = jnp.zeros(gm_s.shape, F32)

    h_sum = reduces(part_a, 0)
    to_do = gathers(do_full)

    def norm_rows(b):
        def some_rows(i, _):
            some = rows_of(b * BLOCK + i * 64, 64, 64)
            m = m_full[some].astype(F32)
            g = cot[some].astype(F32)
            r = rms(m)
            mr = m * r
            part_b[some] = (hid[some].astype(F32) + mr * mgain[...]).astype(BF)
            d_m[some] = norm_back(g, m, r, mgain[...]).astype(BF)
            gm_s[...] += jnp.sum(g * mr, axis=0, keepdims=True)
            return 0

        with jax.named_scope("norm_rows"):
            lax.fori_loop(0, BLOCK // 64, some_rows, 0)
        return net.local(part_b.at[block_rows(b)], out_h.at[block_rows(b)])

    def gates_back(b):
        rows = block_rows(b)
        for n in range(4):
            cols = slice(n * TILE, (n + 1) * TILE)
            d_mixed = mm_nt(d_m[rows, 0:512], wd[0, cols])
            for f in range(1, 4):
                d_mixed += mm_nt(d_m[rows, f * 512 : (f + 1) * 512], wd[f, cols])
            g = gate[rows, cols]
            sigma = jax.nn.sigmoid(g)
            dgate[rows, cols] = (
                d_mixed * up[rows, cols] * sigma * (1.0 + g * (1.0 - sigma))
            ).astype(BF)
            dup[rows, cols] = (d_mixed * (g * sigma)).astype(BF)

    def hidden_back(b):
        rows = block_rows(b)
        for f in range(4):
            for n in range(0, 512, TILE):
                d = mm_nt(dgate[rows], wg[f, n : n + TILE])
                d += mm_nt(dup[rows], wu[f, n : n + TILE])
                part_a[rows, f * 512 + n : f * 512 + n + TILE] = d.astype(BF)

    stores = []
    to_m[0].end()
    stores.append(norm_rows(0))
    to_m[1].mid()
    with jax.named_scope("gates_back"):
        gates_back(0)
    with jax.named_scope("hidden_back"):
        hidden_back(0)
    h_sum[0].start()
    to_m[1].end()
    stores.append(norm_rows(1))
    for g in to_m:
        g.left()
    pl.semaphore_signal(ready, inc=1, device_id=me.to_core(), device_id_type=MESH)
    h_sum[0].mid()
    with jax.named_scope("gates_back"):
        gates_back(1)
    def columns(ref, f):
        return ref.at[:, pl.ds(f * 512, 512)]

    def quarter(ref, f, cols=1024):
        return ref.at[pl.ds(f // 2 * 256, 256), pl.ds(f % 2 * 1024, cols)]

    def half(pair, f):
        return pair[f // 2].at[pl.ds(f % 2 * 256, 256)]

    near_a, near_b, far_a, far_b, far_c = (net.take(n) for n in (4, 4, 6, 6, 6))

    def in_tok(slot, lower):
        return tok.at[pl.ds(lower * 256, 256), pl.ds(slot * 512, 512)]

    g_down = GradSum(
        net, me, wd, [columns(m_full, f) for f in range(4)],
        (credit.at[0], credit.at[5]), gdown_h, near_a, far_a, in_tok,
    )
    g_gate = GradSum(net, me, wg, [quarter(d_m, f) for f in range(4)], (credit.at[1], credit.at[6]),
        ggate_h, near_b, far_b,
    )
    g_up = GradSum(
        net, me, wu, [half((mixed, dgate), f) for f in range(4)], (credit.at[2], credit.at[7]),
        gup_h, near_a, far_a,
    )
    with jax.named_scope("grad_down"):
        for f in range(4):
            wd[f] = mm_tn(mixed[...], d_m[:, f * 512 : (f + 1) * 512]).astype(BF)
    pl.semaphore_wait(ready, 1)
    g_down.start()
    with jax.named_scope("hidden_back"):
        hidden_back(1)
    h_sum[1].start()

    h_sum[0].cross()
    g_down.add()
    g_down.spread()
    h_sum[1].mid()
    with jax.named_scope("grad_gate"):
        for f in range(4):
            wg[f] = mm_tn(hid[:, f * 512 : (f + 1) * 512], dgate[...]).astype(BF)
    g_down.release()

    def back_to_o(b):
        d_hidden = cot[h_sum[b].at(0, size=CHUNK)].astype(F32) + h_sum[b].result()
        value = ochunk[b]
        r = rms(value)
        to_do[b].start(norm_back(d_hidden, value, r, again[...]).astype(BF))
        ochunk[b] = d_hidden
        return jnp.sum(d_hidden * (value * r), axis=0, keepdims=True)

    ga = back_to_o(0)
    g_gate.start()
    h_sum[1].cross()
    g_down.relay()
    to_do[0].mid()
    with jax.named_scope("grad_up"):
        for f in range(4):
            wu[f] = mm_tn(hid[:, f * 512 : (f + 1) * 512], dup[...]).astype(BF)
    g_gate.add()
    g_up.start()
    ga = ga + back_to_o(1)
    ga_s[me.x] = folded(ga)
    ga_far = [net.put(ga_s.at[me.x], ga_s.at[me.x], me.to_x(k)) for k in (1, 3, 2)]
    g_gate.spread()
    to_do[0].end()

    dk, dv, deltas, dn = gate, up, m_s, acc
    dk[...] = jnp.zeros(dk.shape, F32)
    dv[...] = jnp.zeros(dv.shape, F32)
    dq[...] = jnp.zeros(dq.shape, F32)

    def attended_back(b):
        rows = block_rows(b)
        d = mm_nt(do_full[rows, 0:512], wo[0])
        for f in range(1, 4):
            d += mm_nt(do_full[rows, f * 512 : (f + 1) * 512], wo[f])
        d_att[rows] = d.astype(BF)

    def attend_back(b, start, stop, with_keys):
        rows = block_rows(b)
        q = [qrot[rows, cols] for _, cols in heads]
        e = [d_att[rows, cols] for _, cols in heads]
        delta = [deltas[h, rows] for h, _ in heads]

        def step(j, _):
            allowed = allowed_keys(j, rows)
            scale = key_scale(j)
            raw = [mm_nt(q[h], keys[j, :, cols]) * scale for h, cols in heads]
            d_probs = [mm_nt(e[h], vals[j, :, cols]) for h, cols in heads]
            probs, d_scores = [], []
            for h, _ in heads:
                s = jnp.where(allowed, raw[h] - lse[h, rows], BLOCKED)
                p = jnp.exp2(s)
                probs.append(p.astype(BF))
                d_scores.append((p * (d_probs[h] - delta[h]) * scale).astype(BF))
            for h, cols in heads:
                dq[rows, cols] += mm(d_scores[h], keys[j, :, cols])
                if with_keys:
                    there = pl.ds(pl.multiple_of((j - home) * COLS + h * HEAD, HEAD), HEAD)
                    dk[:, there] += mm_tn(d_scores[h], q[h])
                    dv[:, there] += mm_tn(probs[h], e[h])
            return 0

        with jax.named_scope("attend_back"):
            lax.fori_loop(start, stop, step, 0)

    def keys_back(b):
        rows = block_rows(b)

        def step(_, none, i):
            cols8 = sfar[i, b].T
            k_index = me.c * ROWS + lax.broadcasted_iota(jnp.int32, (BLOCK, ROWS), 1)
            allowed = k_index >= lowfar[i, rows, 0:1]
            scale = key_scale(me.c)
            q = [qfar[i, rows, cols] for _, cols in heads]
            e = [efar[i, rows, cols] for _, cols in heads]
            raw = [mm_nt(q[h], keys[me.c, :, cols]) * scale for h, cols in heads]
            d_probs = [mm_nt(e[h], vals[me.c, :, cols]) for h, cols in heads]
            probs, d_scores = [], []
            for h, _ in heads:
                s = jnp.where(allowed, raw[h] - cols8[:, h : h + 1], BLOCKED)
                p = jnp.exp2(s)
                probs.append(p.astype(BF))
                d = d_probs[h] - cols8[:, 2 + h : 3 + h]
                d_scores.append((p * d * scale).astype(BF))
            for h, cols in heads:
                there = pl.ds(pl.multiple_of(me.core * COLS + h * HEAD, HEAD), HEAD)
                dk[:, there] += mm_tn(d_scores[h], q[h])
                dv[:, there] += mm_tn(probs[h], e[h])
            return 0

        def from_queries(i):
            with jax.named_scope("keys_back"):
                lax.fori_loop(0, 1 - me.zl, functools.partial(step, i=i), 0)

        from_queries(me.core)

        @pl.when(me.zl == 0)
        def _():
            for copy in forward[b]:
                copy.wait_recv()

        from_queries(1 - me.core)

    home, away = me.zl * 2, (1 - me.zl) * 2
    cross, forward = {}, {}

    def send_far(b):
        rows = block_rows(b)
        for h, cols in heads:
            e, a = d_att[rows, cols].astype(F32), att[rows, cols].astype(F32)
            deltas[h, rows] = jnp.sum(e * a, axis=1, keepdims=True)
        cross[b] = [
            net.make(d_att.at[rows], efar.at[me.core, rows], me.to_zl(), cross_far[2 * b]),
            net.make(srow.at[b], sfar.at[me.core, b], me.to_zl(), cross_far[2 * b + 1]),
        ]

        @pl.when(me.zl == 1)
        def _():
            cross[b][0].start()
            four = [lse[0, rows], lse[1, rows], deltas[0, rows], deltas[1, rows]]
            srow[b] = jnp.concatenate(four + four, axis=1).T
            cross[b][1].start()

    def forward_far(b):
        e, s = efar.at[me.core, block_rows(b)], sfar.at[me.core, b]
        forward[b] = [
            net.make(e, e, me.to_core(), on_slots[2 * b]),
            net.make(s, s, me.to_core(), on_slots[2 * b + 1]),
        ]

        @pl.when(me.zl == 0)
        def _():
            for copy in cross[b]:
                copy.wait_recv()
            for copy in forward[b]:
                copy.start()

    def far_left():
        @pl.when(me.zl == 1)
        def _():
            for b in range(2):
                for copy in cross[b]:
                    copy.wait_send()

        @pl.when(me.zl == 0)
        def _():
            for b in range(2):
                for copy in forward[b]:
                    copy.wait_send()

    cross_far, on_slots = kv_slots[:4], kv_slots[4:] + row_slots[:2]
    attended_back(0)
    send_far(0)
    attend_back(0, away, away + 2 * me.zl, False)
    to_do[1].mid()
    g_down.cross()
    tok_copy = net.local(tok_h, tok)
    attend_back(0, home, me.c + 1, True)
    forward_far(0)
    keys_back(0)
    to_do[1].end()
    attended_back(1)
    send_far(1)
    g_down.cross_half()
    g_gate.relay()
    attend_back(1, away, away + 2 * me.zl, False)
    attend_back(1, home, me.c + 1, True)
    g_up.add()
    partner = pl.ds(pl.multiple_of((1 - me.core) * COLS, COLS), COLS)
    own = pl.ds(pl.multiple_of(me.core * COLS, COLS), COLS)

    def key_root(j):
        return jnp.sqrt(as_columns(krow[j])[1] / WIDTH + EPS) * (1.0 / LOG2E)

    d_m[:, :COLS] = (dk[:, partner] * key_root(home + 1 - me.core)).astype(BF)
    d_m[:, COLS : 2 * COLS] = dv[:, partner].astype(BF)
    from_core = dup.at[:, pl.ds(0, 2 * COLS)]
    swap = net.put(d_m.at[:, pl.ds(0, 2 * COLS)], from_core, me.to_core(), row_slots[2])
    with jax.named_scope("rotate_back"):
        dn[0] = two_heads(rotate_back, dq[...] * SCALE, cosine[...], sine[...])
    forward_far(1)
    g_up.spread()
    keys_back(1)
    with jax.named_scope("wait_swap"):
        swap.wait_recv()
    own_root = key_root(me.c)
    d_k = dk[:, own] * own_root + from_core[:, :COLS].astype(F32)
    d_v = dv[:, own] + from_core[:, COLS:].astype(F32)
    with jax.named_scope("rotate_back"):
        dn[1] = two_heads(rotate_back, d_k, cosine[...], sine[...])
        dqkv[:, 2 * COLS :] = d_v.astype(BF)
        scaled_q = dn[0] * qgain[...]
        scaled_k = dn[1] * kgain[...]
        stat2[me.t] = pair_of_sums(scaled_q * qraw[...], scaled_k * kraw[...])
    stats = [
        net.put(stat2.at[me.t], stat2.at[me.t], me.to_t(k), stat_slots[k - 1])
        for k in range(1, 8)
    ]
    scale_q = lax.rsqrt(sums_s[:, 0:1] / WIDTH + EPS)
    scale_k = lax.rsqrt(sums_s[:, 4:5] / WIDTH + EPS)
    for copy in ga_far:
        copy.wait_recv()
    gy[me.f] = jnp.zeros((8, 3 * COLS), F32)
    gy[me.f, :, :COLS] = jnp.sum(ga_s[...], axis=0)
    gy[me.f, :, COLS : 2 * COLS] = folded(gm_s[...])
    gy[me.f, 0:1, 2 * COLS :] = jnp.sum(dn[0] * (qraw[...] * scale_q), axis=0, keepdims=True)
    gy[me.f, 1:2, 2 * COLS :] = jnp.sum(dn[1] * (kraw[...] * scale_k), axis=0, keepdims=True)
    gain_y = [net.put(gy.at[me.f], gy.at[me.f], me.to_y(k)) for k in (1, 3, 2)]
    g_gate.cross()
    g_gate.cross_half()
    with jax.named_scope("grad_output"):
        for g in to_do:
            g.left()
        g_out = GradSum(
            net, me, wo, [mixed.at[pl.ds(f * 128, 128), pl.ds(0, 512)] for f in range(4)],
            (credit.at[3], credit.at[8]), gout_h, near_b, far_b,
        )
        for f in range(4):
            wo[f] = mm_tn(att[...], do_full[:, f * 512 : (f + 1) * 512]).astype(BF)
        g_out.start()
    with jax.named_scope("wait_stats"):
        for copy in stats:
            copy.wait_recv()
    dot_q, dot_k = (d / WIDTH for d in as_columns(jnp.sum(stat2[...], axis=0)))
    dqkv[:, :COLS] = (
        scale_q * scaled_q - qraw[...] * (scale_q * scale_q * scale_q * dot_q)
    ).astype(BF)
    dqkv[:, COLS : 2 * COLS] = (
        scale_k * scaled_k - kraw[...] * (scale_k * scale_k * scale_k * dot_k)
    ).astype(BF)

    for copy in stores:
        copy.wait()
    for s in h_sum:
        s.left()
    x_sum = reduces(part_b, 1)
    to_ig = gathers(m_full)

    def input_back(b):
        rows = block_rows(b)
        for f in range(4):
            for n in range(0, 512, TILE):
                d = mm_nt(dqkv[rows], wqkv[f, n : n + TILE])
                part_b[rows, f * 512 + n : f * 512 + n + TILE] = d.astype(BF)

    def input_grad(b):
        to_ig[b].start((ochunk[b] + x_sum[b].result()).astype(BF))

    with jax.named_scope("input_back"):
        input_back(0)
    x_sum[0].start()
    g_up.relay()
    g_out.add()
    with jax.named_scope("input_back"):
        input_back(1)
    g_qkv = GradSum(
        net, me, wqkv, [quarter(do_full, f, 3 * COLS) for f in range(4)], (credit.at[4], credit.at[9]),
        gqkv_h, near_a, far_c,
    )
    tok_copy.wait()
    with jax.named_scope("grad_qkv"):
        for f in range(4):
            wqkv[f] = mm_tn(tok[:, f * 512 : (f + 1) * 512], dqkv[...]).astype(BF)
    g_qkv.start()
    x_sum[0].mid()
    x_sum[1].start()
    g_out.spread()
    g_qkv.add()
    g_qkv.spread()
    for copy in gain_y:
        copy.wait_recv()
    gz[...] = gy[0] + gy[1] + gy[2] + gy[3]
    gain_z = net.put(gz, gzr, me.to_zl())
    x_sum[0].cross()
    g_up.cross()
    x_sum[1].mid()
    g_out.relay()
    input_grad(0)
    x_sum[1].cross()
    g_up.cross_half()
    g_qkv.relay()
    to_ig[0].mid()
    gain_z.wait_recv()
    gc[...] = gz[...] + gzr[...]
    gain_c = net.put(gc, gcr, me.to_core())
    g_down.finish()
    g_gate.finish()
    input_grad(1)
    g_qkv.cross()
    g_qkv.cross_half()
    g_out.cross()
    g_out.cross_half()
    to_ig[0].end()
    stores = [net.local(m_full.at[block_rows(0)], ig_h.at[block_rows(0)])]
    to_ig[1].mid()
    g_up.finish()
    gain_c.wait_recv()
    total = gc[...] + gcr[...]
    for i in range(8):
        cols = slice(i * COLS, (i + 1) * COLS)
        gains[0:1, cols] = total[i : i + 1, :COLS]
        gains[1:2, cols] = total[i : i + 1, COLS : 2 * COLS]
    for i in range(2):
        gains[2:3, i * COLS : (i + 1) * COLS] = total[i : i + 1, 2 * COLS :]
    stores.append(net.local(gains, gains_h))
    to_ig[1].end()
    stores.append(net.local(m_full.at[block_rows(1)], ig_h.at[block_rows(1)]))
    g_qkv.finish()
    g_out.finish()
    for g in (g_down, g_gate, g_up, g_out, g_qkv):
        g.end()
    for copy in stores:
        copy.wait()
    far_left()
    net.finish()


def sds(*shape, dtype=BF):
    return jax.ShapeDtypeStruct(shape, dtype)


VM = pl.BlockSpec(memory_space=pltpu.VMEM)
ANY = pl.BlockSpec(memory_space=pl.ANY)


def layer(*args):
    def buf(*shape, dtype=BF):
        return pltpu.VMEM(shape, dtype)

    def wide(*shape):
        return pltpu.VMEM(shape, F32)

    reduce_bufs = [
        buf(2, 2, HALF, WIDTH),
        buf(2, 2, CHUNK, WIDTH),
        buf(2, CHUNK, WIDTH),
        buf(2, CHUNK, WIDTH),
    ]
    return pl.pallas_call(
        layer_body,
        name="layer",
        out_shape=[
            sds(ROWS, WIDTH),
            sds(ROWS, WIDTH),
            sds(HIDDEN, 512),
            sds(512, HIDDEN),
            sds(512, HIDDEN),
            sds(512, 3 * COLS),
            sds(COLS, 512),
            sds(8, WIDTH, dtype=F32),
        ],
        out_specs=[ANY] * 8,
        in_specs=[ANY, ANY] + [VM] * 6 + [ANY] * 7,
        scratch_shapes=[
            buf(ROWS, WIDTH),
            buf(ROWS, WIDTH),
            buf(4, 512, 3 * COLS),
            buf(4, COLS, 512),
            buf(4, 512, HIDDEN),
            buf(4, 512, HIDDEN),
            buf(4, HIDDEN, 512),
            buf(ROWS, WIDTH),
            wide(ROWS, HIDDEN),
            wide(ROWS, HIDDEN),
            buf(ROWS, HIDDEN),
            buf(ROWS, HIDDEN),
            buf(ROWS, HIDDEN),
            buf(ROWS, WIDTH),
            buf(ROWS, WIDTH),
            buf(ROWS, WIDTH),
            buf(ROWS, WIDTH),
            buf(ROWS, WIDTH),
            *reduce_bufs,
            *reduce_bufs,
            wide(2, CHUNK, WIDTH),
            wide(ROWS, COLS),
            wide(ROWS, COLS),
            wide(ROWS, 8),
            buf(ROWS, COLS),
            buf(4, ROWS, COLS),
            buf(4, ROWS, COLS),
            buf(ROWS, COLS),
            wide(2, ROWS, 1),
            wide(2, ROWS, 1),
            wide(2, ROWS, 2 * HEAD),
            wide(ROWS, COLS),
            wide(ROWS, HEAD),
            wide(ROWS, HEAD),
            pltpu.VMEM((ROWS, HEAD), jnp.int32),
            pltpu.VMEM((2, ROWS, HEAD), jnp.int32),
            wide(8, 8, HEAD),
            wide(8, 8, HEAD),
            wide(4, 8, HEAD),
            buf(2, ROWS, COLS),
            buf(2, ROWS, COLS),
            wide(2, 2, 8, BLOCK),
            wide(2, 8, BLOCK),
            buf(ROWS, 3 * COLS),
            buf(ROWS, COLS),
            wide(4, 8, COLS),
            wide(1, WIDTH),
            wide(4, 8, 3 * COLS),
            *[wide(8, 3 * COLS) for _ in range(4)],
            wide(8, WIDTH),
            pltpu.SemaphoreType.DMA((SENDS,)),
            pltpu.SemaphoreType.DMA((SLOTS,)),
            pltpu.SemaphoreType.DMA((20,)),
            pltpu.SemaphoreType.REGULAR((10,)),
            pltpu.SemaphoreType.REGULAR,
        ],
        compiler_params=pltpu.CompilerParams(
            collective_id=1, has_side_effects=True, vmem_limit_bytes=63 * MIB
        ),
    )(*args)


ARRAYS = (
    (ROWS, WIDTH),
    (ROWS, WIDTH),
    (HIDDEN, 512),
    (512, HIDDEN),
    (512, HIDDEN),
    (COLS, 512),
    (512, 3 * COLS),
)


def finish_body(*refs):
    arrays, gains, outs, rest = refs[:7], refs[7], refs[8:21], refs[21:]
    ins, few, wides, (in_sem, out_sem) = rest[:7], rest[7], rest[8:15], rest[15:]
    order = (1, 2, 3, 4, 6, 5, 0)
    loads = {}
    for i in order:
        loads[i] = pltpu.make_async_copy(arrays[i], ins[i], in_sem.at[i])
        loads[i].start()
    few_load = pltpu.make_async_copy(gains, few, in_sem.at[7])
    few_load.start()
    stores = []

    def store(src, i):
        stores.append(pltpu.make_async_copy(src, outs[i], out_sem.at[i]))
        stores[-1].start()

    for i in order:
        loads[i].wait()
        if i == 0:
            store(ins[0], 0)
        elif i == 6:
            for k in range(3):
                wides[6][k] = ins[6][:, k * COLS : (k + 1) * COLS].astype(F32)
                store(wides[6].at[k], 6 + k)
        else:
            wides[i][...] = ins[i][...].astype(F32)
            store(wides[i], i)
    few_load.wait()
    for i in range(2):
        store(few.at[pl.ds(i, 1)], 9 + i)
        store(few.at[pl.ds(2, 1), pl.ds(i * COLS, COLS)], 11 + i)
    for copy in stores:
        copy.wait()


def finish(*args):
    outs = [sds(ROWS, WIDTH)] + [sds(*s, dtype=F32) for s in ARRAYS[1:6]]
    outs += [sds(512, COLS, dtype=F32)] * 3
    outs += [sds(1, n, dtype=F32) for n in (WIDTH, WIDTH, COLS, COLS)]
    wides = [(8, 128), *ARRAYS[1:6], (3, 512, COLS)]
    return pl.pallas_call(
        finish_body,
        name="to_float",
        out_shape=outs,
        out_specs=[ANY] * 13,
        in_specs=[ANY] * 8,
        scratch_shapes=[pltpu.VMEM(s, BF) for s in ARRAYS]
        + [pltpu.VMEM((8, WIDTH), F32)]
        + [pltpu.VMEM(s, F32) for s in wides]
        + [pltpu.SemaphoreType.DMA((8,)), pltpu.SemaphoreType.DMA((13,))],
        compiler_params=pltpu.CompilerParams(vmem_limit_bytes=62 * MIB),
    )(*args)


def body(
    tokens, segments, positions, cotangent,
    w_query, w_key, w_value, w_output, w_gate, w_up, w_down,
    query_gain, key_gain, attn_gain, mlp_gain,
):
    del segments
    inverse = ROPE_BASE ** (-np.arange(64, dtype=np.float64) * 2.0 / HEAD)
    freqs = jnp.asarray(np.concatenate([inverse, inverse])[None], F32)
    qgain, kgain, again, mgain = (
        g[None] for g in (query_gain, key_gain, attn_gain, mlp_gain)
    )
    out, d_in, g_down, g_gate, g_up, g_qkv, g_out, gains = layer(
        tokens[0], cotangent[0], positions, freqs, qgain, kgain, again, mgain,
        w_query, w_key, w_value, w_output, w_gate, w_up, w_down,
    )
    out, d_in, g_down, g_gate, g_up, g_out, g_q, g_k, g_v, ga, gm, gq, gk = finish(
        out, d_in, g_down, g_gate, g_up, g_out, g_qkv, gains
    )
    return (
        out[None], d_in[None], g_q, g_k, g_v, g_out, g_gate, g_up, g_down,
        gq[0], gk[0], ga[0], gm[0],
    )


def solution(mesh):
    in_specs = (
        P("fsdp", "context", None),
        P("fsdp", None),
        P("fsdp", None),
        P("fsdp", "context", None),
        P("fsdp", "tensor"),
        P("fsdp", "tensor"),
        P("fsdp", "tensor"),
        P("tensor", "fsdp"),
        P("fsdp", "tensor"),
        P("fsdp", "tensor"),
        P("tensor", "fsdp"),
        P("tensor"),
        P("tensor"),
        P(),
        P(),
    )
    out_specs = (
        P("fsdp", "context", None),
        P("fsdp", "context", None),
        P("fsdp", "tensor"),
        P("fsdp", "tensor"),
        P("fsdp", "tensor"),
        P("tensor", "fsdp"),
        P("fsdp", "tensor"),
        P("fsdp", "tensor"),
        P("tensor", "fsdp"),
        P("tensor"),
        P("tensor"),
        P(),
        P(),
    )
    return jax.shard_map(body, mesh=mesh, in_specs=in_specs, out_specs=out_specs, check_vma=False)
```

```python
import functools

import jax
import jax.numpy as jnp
import numpy as np
from jax import lax
from jax.experimental import pallas as pl
from jax.experimental.pallas import tpu as pltpu
from jax.sharding import PartitionSpec as P

MESH = pl.DeviceIdType.MESH
BF = jnp.bfloat16
F32 = jnp.float32
HEAD = 128
WIDTH = 2048
ROWS = 512
COLS = 256
HIDDEN = 1024
BLOCK = 256
CHUNK = 64
HALF = 32
TILE = 256
EPS = 1e-06
ROPE_BASE = 500000.0
BLOCKED = -1000000000.0
LOG2E = 1.4426950408889634
SCALE = HEAD ** (-0.5)
MIB = 2**20
SLOTS = 105
SENDS = 56


def mm(a, b):
    return lax.dot_general(a, b, (((1,), (0,)), ((), ())), preferred_element_type=F32)


def mm_nt(a, b):
    return lax.dot_general(a, b, (((1,), (1,)), ((), ())), preferred_element_type=F32)


def mm_tn(a, b):
    return lax.dot_general(a, b, (((0,), (0,)), ((), ())), preferred_element_type=F32)


def rows_of(start, size, unit):
    return pl.ds(pl.multiple_of(start, unit), size)


class Place:
    def __init__(self):
        self.f = lax.axis_index("fsdp")
        self.c = lax.axis_index("context")
        self.t = lax.axis_index("tensor")
        self.x = self.t // 2
        self.zh = self.t % 2
        self.zl = self.c // 2
        self.core = self.c % 2

    def x_at(self, k):
        return (self.x + k + 4) % 4

    def to_x(self, k):
        return {"tensor": self.x_at(k) * 2 + self.zh}

    def to_zh(self):
        return {"tensor": self.x * 2 + 1 - self.zh}

    def to_t(self, k):
        return {"tensor": (self.t + k) % 8}

    def to_y(self, k):
        return {"fsdp": (self.f + k) % 4}

    def to_core(self):
        return {"context": self.zl * 2 + 1 - self.core}

    def to_zl(self):
        return {"context": (1 - self.zl) * 2 + self.core}

    def to_far(self):
        return {"context": 3 - self.c}

    def announce(self):
        self.bar = pltpu.get_barrier_semaphore()
        self.peers = [self.to_t(k) for k in range(1, 8)] + [self.to_y(k) for k in range(1, 4)]
        self.peers += [self.to_core(), self.to_zl(), self.to_far()]
        for peer in self.peers:
            pl.semaphore_signal(self.bar, inc=1, device_id=peer, device_id_type=MESH)

    def barrier(self):
        pl.semaphore_wait(self.bar, len(self.peers))


class Net:
    def __init__(self, send, recv, local):
        self.send, self.recv, self.loc = send, recv, local
        self.n = 0
        self.k = 0
        self.free = []
        self.free_sends = list(range(SENDS))
        self.sent = []

    def take(self, count):
        old, self.free = self.free[:count], self.free[count:]
        new = [self.n + i for i in range(count - len(old))]
        self.n += len(new)
        return old + new

    def give(self, slots):
        self.free += slots

    def put(self, src, dst, peer, slot=None):
        if slot is None:
            (slot,) = self.take(1)
        number = self.number()
        copy = pltpu.make_async_remote_copy(
            src_ref=src,
            dst_ref=dst,
            send_sem=self.send.at[number],
            recv_sem=self.recv.at[slot],
            device_id=peer,
            device_id_type=MESH,
        )
        copy.start()
        self.sent.append((copy, number))
        return copy

    def make(self, src, dst, peer, slot):
        return pltpu.make_async_remote_copy(
            src_ref=src,
            dst_ref=dst,
            send_sem=self.send.at[self.number()],
            recv_sem=self.recv.at[slot],
            device_id=peer,
            device_id_type=MESH,
        )

    def number(self):
        if not self.free_sends:
            self.left(self.sent[0][0])
        return self.free_sends.pop(0)

    def left(self, *copies):
        for copy in copies:
            for i, (other, number) in enumerate(self.sent):
                if other is copy:
                    copy.wait_send()
                    self.free_sends.append(number)
                    del self.sent[i]
                    break

    def local(self, src, dst):
        copy = pltpu.make_async_copy(src, dst, self.loc.at[self.k])
        self.k += 1
        copy.start()
        return copy

    def finish(self):
        self.left(*[copy for copy, _ in self.sent])


class Reduce:
    def __init__(self, net, me, part, bufs, b, slots):
        self.net, self.me, self.part, self.b, self.slots = net, me, part, b, slots
        self.ra, self.rb, self.zs, self.zr = bufs

    def at(self, k, lower=False, size=HALF):
        start = self.b * BLOCK + self.me.x_at(k) * CHUNK + (HALF if lower else 0)
        return rows_of(start, size, HALF)

    def start(self):
        net, part, b, slots = self.net, self.part, self.b, self.slots
        up, down = self.me.to_x(1), self.me.to_x(-1)
        lower, upper = pl.ds(0, HALF), pl.ds(HALF, HALF)
        self.a0 = net.put(part.at[self.at(2)], self.ra.at[b, 0], up, slots[0])
        self.a1 = net.put(part.at[self.at(2, True)], self.ra.at[b, 1], down, slots[1])
        self.b0 = net.put(part.at[self.at(1, True)], self.rb.at[b, 0, upper], up, slots[2])
        self.b1 = net.put(part.at[self.at(-1)], self.rb.at[b, 1, lower], down, slots[3])

    def mid(self):
        net, me, part, b, slots = self.net, self.me, self.part, self.b, self.slots
        self.a0.wait_recv()
        s = self.at(1)
        part[s] = (part[s].astype(F32) + self.ra[b, 0].astype(F32)).astype(BF)
        self.c0 = net.put(part.at[s], self.rb.at[b, 0, pl.ds(0, HALF)], me.to_x(1), slots[4])
        self.a1.wait_recv()
        s = self.at(-1, True)
        part[s] = (part[s].astype(F32) + self.ra[b, 1].astype(F32)).astype(BF)
        there = self.rb.at[b, 1, pl.ds(HALF, HALF)]
        self.c1 = net.put(part.at[s], there, me.to_x(-1), slots[5])

    def cross(self):
        b = self.b
        for copy in (self.b0, self.b1, self.c0, self.c1):
            copy.wait_recv()
        own = self.part[self.at(0, size=CHUNK)].astype(F32)
        total = own + self.rb[b, 0].astype(F32) + self.rb[b, 1].astype(F32)
        self.zs[b] = total.astype(BF)
        self.z = self.net.put(self.zs.at[b], self.zr.at[b], self.me.to_zh(), self.slots[6])

    def result(self):
        self.z.wait_recv()
        return self.zs[self.b].astype(F32) + self.zr[self.b].astype(F32)

    def left(self):
        self.net.left(self.a0, self.a1, self.b0, self.b1, self.c0, self.c1, self.z)


class Gather:
    def __init__(self, net, me, full, b, slots):
        self.net, self.me, self.full, self.b, self.slots = net, me, full, b, slots

    def at(self, k, lower=False, size=HALF):
        start = self.b * BLOCK + self.me.x_at(k) * CHUNK + (HALF if lower else 0)
        return rows_of(start, size, HALF)

    def send(self, s, k, i):
        ref = self.full.at[s]
        return self.net.put(ref, ref, self.me.to_x(k), self.slots[i])

    def start(self, chunk):
        self.full[self.at(0, size=CHUNK)] = chunk
        self.p0 = self.send(self.at(0), 1, 0)
        self.m0 = self.send(self.at(0, True), -1, 1)
        self.p1 = self.send(self.at(0, True), 1, 2)
        self.m1 = self.send(self.at(0), -1, 3)

    def mid(self):
        self.p0.wait_recv()
        self.f0 = self.send(self.at(-1), 1, 4)
        self.m0.wait_recv()
        self.f1 = self.send(self.at(1, True), -1, 5)

    def end(self):
        for copy in (self.p1, self.m1, self.f0, self.f1):
            copy.wait_recv()

    def left(self):
        self.net.left(self.p0, self.m0, self.p1, self.m1, self.f0, self.f1)


class Weight:
    def __init__(self, net, me, shard, full, slots, own=None):
        self.net, self.me, self.shard, self.full, self.slots = net, me, shard, full, slots
        self.part = shard.shape[0] // self.cuts
        self.own = own or [net.local(shard, full.at[me.f])]

    cuts = 4

    def first(self):
        return self.me.core * 2

    def at(self, lower, parts=1):
        return rows_of((self.first() + lower) * self.part, parts * self.part, self.part)

    def send(self, lower, k, i):
        s, peer = self.at(lower), self.me.to_y(k)
        return self.net.put(
            self.shard.at[s], self.full.at[self.me.f, s], peer, self.slots[i]
        )

    def start(self):
        self.begin()
        self.more()

    def begin(self):
        self.p0, self.m0 = self.send(0, 1, 0), self.send(1, 3, 1)

    def more(self):
        self.p1, self.m1 = self.send(1, 1, 2), self.send(0, 3, 3)

    def hand(self, k, s, peer, i):
        ref = self.full.at[(self.me.f + k) % 4, s]
        return self.net.put(ref, ref, peer, self.slots[i])

    def relay(self):
        self.p0.wait_recv()
        self.f0 = self.hand(3, self.at(0), self.me.to_y(1), 4)
        self.m0.wait_recv()
        self.f1 = self.hand(1, self.at(1), self.me.to_y(3), 5)

    def pass_sides(self):
        core = self.me.to_core()
        self.p1.wait_recv()
        self.n0 = self.hand(3, self.at(0, 2), core, 6)
        self.m1.wait_recv()
        self.n1 = self.hand(1, self.at(0, 2), core, 7)

    def pass_opposite(self):
        self.f0.wait_recv()
        self.f1.wait_recv()
        self.n2 = self.hand(2, self.at(0, 2), self.me.to_core(), 8)

    def pass_on(self):
        self.pass_sides()
        self.pass_opposite()

    def wait(self):
        for copy in (self.n0, self.n1, self.n2):
            copy.wait_recv()
        for copy in self.own:
            copy.wait()
        self.left()

    def left(self):
        near = (self.n0, self.n1, self.n2)
        self.net.left(*near, self.f0, self.f1, self.p0, self.m0, self.p1, self.m1)


class QuarterWeight(Weight):
    cuts = 8

    def first(self):
        return self.me.c * 2

    def both(self, k, i):
        s = self.at(0, 2)
        self.across.append(self.hand(k, s, self.me.to_zl(), i))
        self.near.append(self.hand(k, s, self.me.to_core(), i + 3))

    def pass_sides(self):
        self.across, self.near = [], []
        self.p1.wait_recv()
        self.both(3, 6)
        self.m1.wait_recv()
        self.both(1, 7)

    def pass_opposite(self):
        self.f0.wait_recv()
        self.f1.wait_recv()
        self.across.append(self.hand(2, self.at(0), self.me.to_zl(), 8))
        self.near.append(self.hand(2, self.at(0, 2), self.me.to_core(), 11))

    def pass_rest(self):
        self.across.append(self.hand(2, self.at(1), self.me.to_zl(), 15))

    def pass_far(self):
        far = rows_of(((self.me.c + 2) % 4) * 2 * self.part, 2 * self.part, self.part)
        for copy in self.across[:2]:
            copy.wait_recv()
        for k, i in ((3, 12), (1, 13)):
            self.near.append(self.hand(k, far, self.me.to_core(), i))
        for copy in self.across[2:]:
            copy.wait_recv()
        self.near.append(self.hand(2, far, self.me.to_core(), 14))

    def arrive(self):
        for copy in self.near:
            copy.wait_recv()

    def wait(self):
        self.arrive()
        for copy in self.own:
            copy.wait()
        self.left()

    def left(self):
        own = (self.f0, self.f1, self.p0, self.m0, self.p1, self.m1)
        self.net.left(*self.near, *self.across, *own)


class GradSum:
    def __init__(self, net, me, grad, got, credit, out, near, far, landing=None):
        self.net, self.me, self.grad, self.got = net, me, grad, got
        self.landing = landing
        self.slots = near + far + net.take(3)
        self.credit, self.out = credit, out
        self.half = grad.shape[1] // 2
        self.mine, self.theirs = self.at(me.core), self.at(1 - me.core)

    def at(self, core, lower=0, parts=2):
        start = core * self.half + lower * (self.half // 2)
        return rows_of(start, parts * self.half // 2, self.half // 2)

    def start(self):
        self.near = [
            self.net.put(
                self.grad.at[f, self.theirs], self.got[f], self.me.to_core(), self.slots[f]
            )
            for f in range(4)
        ]

    def add(self):
        net, me = self.net, self.me
        for f in range(4):
            self.near[f].wait_recv()
            here = self.grad[f, self.mine].astype(F32)
            self.grad[f, self.mine] = (here + self.got[f][...].astype(F32)).astype(BF)
        if self.landing is None:
            self.release()

    def release(self):
        self.net.left(*self.near)
        near_y, zl = self.credit
        self.grant(zl, self.me.to_zl())
        if self.landing is None:
            for k in (1, 3):
                self.grant(near_y, self.me.to_y(k))

    @staticmethod
    def grant(credit, peer):
        pl.semaphore_signal(credit, inc=1, device_id=peer, device_id_type=MESH)

    def place(self, slot, lower):
        if self.landing is not None:
            return self.landing(slot, lower)
        return self.grad.at[slot, self.at(1 - self.me.core, lower, 1)]

    def send(self, k, lower, place, way, i):
        me = self.me
        return self.net.put(
            self.grad.at[(me.f + k) % 4, self.at(me.core, lower, 1)],
            self.place(place, lower),
            me.to_y(way),
            self.slots[i],
        )

    def spread(self):
        pl.semaphore_wait(self.credit[0], 2)
        self.a0, self.a1 = self.send(2, 0, 0, 1, 4), self.send(2, 1, 0, 3, 5)
        self.b0, self.b1 = self.send(1, 1, 1, 1, 6), self.send(3, 0, 2, 3, 7)

    def relay(self):
        me = self.me
        for copy, k, lower in ((self.a0, 1, 0), (self.a1, 3, 1)):
            copy.wait_recv()
            f, s = (me.f + k) % 4, self.at(me.core, lower, 1)
            there = self.place(0, lower)[...].astype(F32)
            self.grad[f, s] = (self.grad[f, s].astype(F32) + there).astype(BF)
            if k == 1:
                self.c0 = self.send(1, 0, 1, 1, 8)
            else:
                self.c1 = self.send(3, 1, 2, 3, 9)

    def cross(self):
        for copy in (self.b0, self.b1, self.c0, self.c1):
            copy.wait_recv()
        me = self.me
        for lower in range(2):
            s = self.at(me.core, lower, 1)
            total = self.grad[me.f, s].astype(F32)
            for k in (1, 2):
                total = total + self.place(k, lower)[...].astype(F32)
            self.grad[me.f, s] = total.astype(BF)
        pl.semaphore_wait(self.credit[1], 1)
        self.z = []
        self.cross_half()

    def cross_half(self):
        me, lower = self.me, len(self.z)
        here = self.grad.at[me.f, self.at(me.core, lower, 1)]
        there = self.grad.at[3, self.at(1 - me.core, lower, 1)]
        self.z.append(self.net.put(here, there, me.to_zl(), self.slots[10 + lower]))

    def finish(self):
        for copy in self.z:
            copy.wait_recv()
        me = self.me
        total = self.grad[me.f, self.mine].astype(F32) + self.grad[3, self.theirs].astype(F32)
        self.grad[0, self.theirs] = total.astype(BF)
        final = self.grad.at[0, self.theirs]
        self.store = self.net.local(final, self.out.at[self.mine])
        self.back = self.net.put(final, self.out.at[self.mine], me.to_core(), self.slots[12])

    def end(self):
        self.store.wait()
        self.back.wait_recv()


def rms(value):
    return lax.rsqrt(jnp.mean(value * value, axis=-1, keepdims=True) + EPS)


def norm_back(grad, value, factor, gain):
    scaled = grad * gain
    inner = jnp.mean(scaled * value, axis=-1, keepdims=True)
    return factor * scaled - value * (factor * factor * factor * inner)


def rotate(value, cosine, sine):
    return value * cosine + pltpu.roll(value, 64, axis=1) * sine


def rotate_back(value, cosine, sine):
    return value * cosine - pltpu.roll(value, 64, axis=1) * sine


def two_heads(fn, value, cosine, sine):
    return jnp.concatenate(
        [fn(value[:, :HEAD], cosine, sine), fn(value[:, HEAD:], cosine, sine)], axis=1
    )


def pair_of_sums(first, second):
    one, two = (jnp.sum(v, axis=1, keepdims=True) for v in (first, second))
    wide = jnp.concatenate([one] * 4 + [two] * 4, axis=1).T
    row = lax.broadcasted_iota(jnp.int32, (8, HEAD), 0)
    packed = wide[:, :HEAD]
    for i in range(1, 4):
        packed = jnp.where(row % 4 == i, wide[:, i * HEAD : (i + 1) * HEAD], packed)
    return packed


def as_columns(packed):
    tall = packed.T
    return [
        jnp.concatenate([tall[:, k + i : k + i + 1] for i in range(4)], axis=0) for k in (0, 4)
    ]


def folded(row):
    return jnp.concatenate([row[:, i * COLS : (i + 1) * COLS] for i in range(8)], axis=0)


def layer_body(
    tok_h, cot_h, pos, freqs, qgain, kgain, again, mgain,
    wq_h, wk_h, wv_h, wo_h, wg_h, wu_h, wd_h,
    out_h, ig_h, gdown_h, ggate_h, gup_h, gqkv_h, gout_h, gains_h,
    tok, cot, wqkv, wo, wg, wu, wd, hid, gate, up, mixed, dgate, dup, part_a, part_b,
    m_full, d_m, do_full, ra0, rb0, zs0, zr0, ra1, rb1, zs1, zr1, ochunk,
    qraw, kraw, sums_s, qrot, keys, vals, att, lse, m_s, acc, dq, cosine, sine, low, lowfar,
    stat, stat2, krow, qfar, efar, sfar, srow, dqkv, d_att, ga_s, gm_s, gy, gz, gzr, gc, gcr, gains,
    send, recv, local, credit, ready,
):
    me = Place()
    net = Net(send, recv, local)
    bufs = ((ra0, rb0, zs0, zr0), (ra1, rb1, zs1, zr1))
    me.announce()
    thirds = [
        net.local(w, wqkv.at[me.f, :, pl.ds(i * COLS, COLS)])
        for i, w in enumerate((wq_h, wk_h, wv_h))
    ]
    tok_copy = net.local(tok_h, tok)
    cot_copy = net.local(cot_h, cot)
    w_qk, w_v = (
        kind(net, me, wqkv.at[me.f, :, cols], wqkv.at[:, :, cols], net.take(count), thirds)
        for kind, cols, count in (
            (Weight, pl.ds(0, 2 * COLS), 9),
            (QuarterWeight, pl.ds(2 * COLS, COLS), 16),
        )
    )
    w_o, w_u = (Weight(net, me, w, full, net.take(9)) for w, full in ((wo_h, wo), (wu_h, wu)))
    w_g = QuarterWeight(net, me, wg_h, wg, net.take(16))
    w_d = Weight(net, me, wd_h, wd, w_qk.slots)
    sum_slots = [net.take(6) for _ in range(2)]
    all_slots = [net.take(6) for _ in range(2)]
    cross_slots = [[net.take(1) for _ in range(2)] for _ in range(2)]

    def reduces(part, turn):
        return [
            Reduce(net, me, part, bufs[turn], b, sum_slots[b] + cross_slots[turn][b])
            for b in range(2)
        ]

    def gathers(full):
        return [Gather(net, me, full, b, all_slots[b]) for b in range(2)]

    def block_rows(b):
        return slice(b * BLOCK, (b + 1) * BLOCK)

    here = pos[0:1, pl.ds(pl.multiple_of(me.c * ROWS, ROWS), ROWS)].astype(F32)
    places = jnp.broadcast_to(here, (HEAD, ROWS)).T
    angle = places * freqs[0:1, :]
    lane = lax.broadcasted_iota(jnp.int32, (ROWS, HEAD), 1)
    cosine[...] = jnp.cos(angle)
    sin = jnp.sin(angle)
    sine[...] = jnp.where(lane < HEAD // 2, -sin, sin)
    token = lax.broadcasted_iota(jnp.int32, (ROWS, HEAD), 0)
    low[...] = me.c * ROWS + token - places.astype(jnp.int32)
    for i in range(2):
        there = pos[0:1, (2 + i) * ROWS : (3 + i) * ROWS].astype(F32)
        there = jnp.broadcast_to(there, (HEAD, ROWS)).T
        lowfar[i] = (2 + i) * ROWS + token - there.astype(jnp.int32)
    for copy in thirds:
        copy.wait()
    me.barrier()
    w_v.start()
    tok_copy.wait()
    qk_cols, v_cols = slice(0, 2 * COLS), slice(2 * COLS, 3 * COLS)

    def project(k, cols):
        f = (me.f + k) % 4
        some = tok[:, pl.ds(pl.multiple_of(f * 512, 512), 512)]
        return mm(some, wqkv[f, :, cols])

    gate[:, v_cols] = project(0, v_cols)
    w_v.relay()
    w_qk.start()
    gate[:, qk_cols] = project(0, qk_cols)
    w_v.pass_sides()
    w_v.pass_opposite()
    w_v.pass_rest()
    w_qk.relay()
    w_o.start()
    w_g.begin()
    w_v.pass_far()
    w_qk.pass_sides()
    with jax.named_scope("wait_wv"):
        w_v.arrive()
    with jax.named_scope("values"):
        value = gate[:, v_cols] + project(1, v_cols) + project(2, v_cols) + project(3, v_cols)
        vals[me.c] = value.astype(BF)
    kv_slots = net.take(6)
    v_near = net.put(vals.at[me.c], vals.at[me.c], me.to_core(), kv_slots[0])
    v_far = net.make(vals.at[me.c], vals.at[me.c], me.to_zl(), kv_slots[1])
    pl.when(me.zl == 0)(v_far.start)
    w_qk.n0.wait_recv()
    w_qk.n1.wait_recv()
    gate[:, qk_cols] += project(3, qk_cols) + project(1, qk_cols)
    w_qk.pass_opposite()
    w_qk.n2.wait_recv()
    with jax.named_scope("queries"):
        qk = gate[:, qk_cols] + project(2, qk_cols)
        qraw[...] = qk[:, :COLS]
        kraw[...] = qk[:, COLS:]
        stat[me.t] = pair_of_sums(qraw[...] * qraw[...], kraw[...] * kraw[...])
    stat_slots = net.take(7)
    stats = [
        net.put(stat.at[me.t], stat.at[me.t], me.to_t(k), stat_slots[k - 1]) for k in range(1, 8)
    ]
    keys[me.c] = two_heads(rotate, kraw[...] * kgain[...], cosine[...], sine[...]).astype(BF)
    k_near = net.put(keys.at[me.c], keys.at[me.c], me.to_core(), kv_slots[2])
    k_far = net.make(keys.at[me.c], keys.at[me.c], me.to_zl(), kv_slots[3])
    pl.when(me.zl == 0)(k_far.start)
    w_o.relay()
    w_g.more()
    with jax.named_scope("wait_stats"):
        for copy in stats:
            copy.wait_recv()
    row_slots = net.take(3)
    with jax.named_scope("rotate"):
        packed = jnp.sum(stat[...], axis=0)
        krow[me.c] = packed
        rows_near = net.put(krow.at[me.c], krow.at[me.c], me.to_core(), row_slots[0])
        rows_far = [
            net.make(krow.at[me.c], krow.at[me.c], peer, slot)
            for peer, slot in ((me.to_zl(), row_slots[1]), (me.to_far(), row_slots[2]))
        ]

        @pl.when(me.zl == 0)
        def _():
            for copy in rows_far:
                copy.start()

        sum_q, sum_k = as_columns(packed)
        sums_s[:, 0:1] = sum_q
        sums_s[:, 4:5] = sum_k
        scale_q = lax.rsqrt(sum_q / WIDTH + EPS)
        q_norm = qraw[...] * (scale_q * (SCALE * LOG2E)) * qgain[...]
        qrot[...] = two_heads(rotate, q_norm, cosine[...], sine[...]).astype(BF)
    other = (1 - me.zl) * 2 + me.core

    m_s[...] = jnp.full(m_s.shape, 2 * BLOCKED, F32)
    acc[...] = jnp.zeros(acc.shape, F32)

    def allowed_keys(j, rows):
        k_index = j * ROWS + lax.broadcasted_iota(jnp.int32, (BLOCK, ROWS), 1)
        first = me.c * ROWS + rows.start
        q_index = first + lax.broadcasted_iota(jnp.int32, (BLOCK, ROWS), 0)
        return (k_index >= low[rows, 0:1]) & (k_index <= q_index)

    heads = [(h, slice(h * HEAD, (h + 1) * HEAD)) for h in range(2)]

    def key_scale(j):
        row = jnp.concatenate([krow[j, i : i + 1, :] for i in range(4, 8)], axis=1)
        return lax.rsqrt(row / WIDTH + EPS)

    def attend(b, start, stop):
        rows = block_rows(b)

        def step(i, _):
            j = me.c - i
            allowed = allowed_keys(j, rows)
            scale = key_scale(j)
            raw = [mm_nt(qrot[rows, cols], keys[j, :, cols]) * scale for _, cols in heads]
            probs, fades = [], []
            for h, _ in heads:
                s = jnp.where(allowed, raw[h], BLOCKED)
                m_old = m_s[h, rows]
                m_new = jnp.maximum(m_old, jnp.max(s, axis=1, keepdims=True))
                p = jnp.exp2(s - m_new)
                fade = jnp.exp2(m_old - m_new)
                m_s[h, rows] = m_new
                probs.append(p.astype(BF))
                fades.append(fade)
            ones = jnp.ones((ROWS, HEAD), BF)
            sums = [
                mm(probs[h], jnp.concatenate([vals[j, :, cols], ones], axis=1))
                for h, cols in heads
            ]
            for h, _ in heads:
                acc[h, rows] = acc[h, rows] * fades[h] + sums[h]
            return 0

        with jax.named_scope("attend"):
            lax.fori_loop(start, stop, step, 0)

    def attended(b):
        rows = block_rows(b)
        for h, cols in heads:
            att[rows, cols] = (acc[h, rows, :HEAD] / acc[h, rows, HEAD:]).astype(BF)
            lse[h, rows] = m_s[h, rows] + jnp.log2(acc[h, rows, HEAD : HEAD + 1])
        for f in range(4):
            part_a[rows, f * 512 : (f + 1) * 512] = mm(att[rows], wo[f]).astype(BF)

    w_g.relay()
    w_u.start()
    with jax.named_scope("wait_near"):
        v_near.wait_recv()
        k_near.wait_recv()
        rows_near.wait_recv()
        v_on = net.make(vals.at[other], vals.at[other], me.to_core(), kv_slots[4])
        k_on = net.make(keys.at[other], keys.at[other], me.to_core(), kv_slots[5])

        @pl.when(me.zl == 1)
        def _():
            v_far.wait_recv()
            v_on.start()

    attend(0, 0, 1 + me.core)
    w_g.pass_sides()

    @pl.when(me.zl == 1)
    def _():
        k_far.wait_recv()
        k_on.start()

    attend(1, 0, 1 + me.core)

    @pl.when(me.zl == 1)
    def _():
        for copy in (v_on, k_on, *rows_far):
            copy.wait_recv()

    o_sum = reduces(part_a, 0)
    to_hid = gathers(hid)
    w_o.pass_on()
    w_g.pass_opposite()
    attend(0, 1 + me.core, me.c + 1)
    w_o.wait()
    attended(0)
    o_sum[0].start()
    attend(1, 1 + me.core, me.c + 1)
    attended(1)
    o_sum[0].mid()
    o_sum[1].start()
    w_u.relay()
    w_v.left()
    w_qk.left()
    w_d.start()
    net.left(v_near, k_near, rows_near, *stats)

    @pl.when(me.zl == 0)
    def _():
        for copy in (v_far, k_far, *rows_far):
            copy.wait_send()

    @pl.when(me.zl == 1)
    def _():
        v_on.wait_send()
        k_on.wait_send()


    def hidden(b):
        value = o_sum[b].result()
        ochunk[b] = value
        own = tok[o_sum[b].at(0, size=CHUNK)].astype(F32)
        to_hid[b].start((own + value * rms(value) * again[...]).astype(BF))

    o_sum[0].cross()
    w_g.pass_rest()
    o_sum[1].mid()
    hidden(0)
    o_sum[1].cross()
    w_d.relay()
    w_g.pass_far()
    to_hid[0].mid()
    w_u.pass_on()
    hidden(1)
    q_far, q_on = net.take(2)
    q_far = net.make(qrot, qfar.at[me.core], me.to_zl(), q_far)
    q_on = net.make(qfar.at[me.core], qfar.at[me.core], me.to_core(), q_on)
    pl.when(me.zl == 1)(q_far.start)
    for k in (1, 3):
        GradSum.grant(credit.at[0], me.to_y(k))
    to_hid[0].end()

    m_sum = reduces(part_b, 1)
    to_m = gathers(m_full)

    def gates(b, tiles):
        rows = block_rows(b)
        for n in tiles:
            cols = slice(n * TILE, (n + 1) * TILE)
            g = mm(hid[rows], wg[:, :, cols].reshape(WIDTH, TILE))
            u = mm(hid[rows], wu[:, :, cols].reshape(WIDTH, TILE))
            gate[rows, cols] = g
            up[rows, cols] = u
            mixed[rows, cols] = (g * jax.nn.sigmoid(g) * u).astype(BF)

    def down(b):
        rows = block_rows(b)
        for f in range(4):
            part_b[rows, f * 512 : (f + 1) * 512] = mm(mixed[rows], wd[f]).astype(BF)

    w_d.pass_on()
    w_g.wait()
    w_u.wait()
    with jax.named_scope("gates"):
        gates(0, (0, 1))
    to_hid[1].mid()
    with jax.named_scope("gates"):
        gates(0, (2, 3))
    for s in o_sum:
        s.left()
    w_d.wait()
    down(0)
    m_sum[0].start()

    @pl.when(me.zl == 0)
    def _():
        q_far.wait_recv()
        q_on.start()

    to_hid[1].end()
    with jax.named_scope("gates"):
        gates(1, (0, 1, 2, 3))
    m_sum[0].mid()
    down(1)
    m_sum[1].start()
    m_sum[0].cross()
    m_sum[1].mid()
    cot_copy.wait()
    for g in to_hid:
        g.left()

    @pl.when(me.zl == 0)
    def _():
        q_on.wait_recv()
        q_on.wait_send()

    @pl.when(me.zl == 1)
    def _():
        q_far.wait_send()

    for w in (w_v, w_qk, w_o, w_g, w_u):
        net.give(w.slots)
    to_m[0].start(m_sum[0].result().astype(BF))
    m_sum[1].cross()
    to_m[0].mid()
    to_m[1].start(m_sum[1].result().astype(BF))
    for s in m_sum:
        s.left()
    gm_s[...] = jnp.zeros(gm_s.shape, F32)

    h_sum = reduces(part_a, 0)
    to_do = gathers(do_full)

    def norm_rows(b):
        def some_rows(i, _):
            some = rows_of(b * BLOCK + i * 64, 64, 64)
            m = m_full[some].astype(F32)
            g = cot[some].astype(F32)
            r = rms(m)
            mr = m * r
            part_b[some] = (hid[some].astype(F32) + mr * mgain[...]).astype(BF)
            d_m[some] = norm_back(g, m, r, mgain[...]).astype(BF)
            gm_s[...] += jnp.sum(g * mr, axis=0, keepdims=True)
            return 0

        with jax.named_scope("norm_rows"):
            lax.fori_loop(0, BLOCK // 64, some_rows, 0)
        return net.local(part_b.at[block_rows(b)], out_h.at[block_rows(b)])

    def gates_back(b):
        rows = block_rows(b)
        for n in range(4):
            cols = slice(n * TILE, (n + 1) * TILE)
            d_mixed = mm_nt(d_m[rows, 0:512], wd[0, cols])
            for f in range(1, 4):
                d_mixed += mm_nt(d_m[rows, f * 512 : (f + 1) * 512], wd[f, cols])
            g = gate[rows, cols]
            sigma = jax.nn.sigmoid(g)
            dgate[rows, cols] = (
                d_mixed * up[rows, cols] * sigma * (1.0 + g * (1.0 - sigma))
            ).astype(BF)
            dup[rows, cols] = (d_mixed * (g * sigma)).astype(BF)

    def hidden_back(b):
        rows = block_rows(b)
        for f in range(4):
            for n in range(0, 512, TILE):
                d = mm_nt(dgate[rows], wg[f, n : n + TILE])
                d += mm_nt(dup[rows], wu[f, n : n + TILE])
                part_a[rows, f * 512 + n : f * 512 + n + TILE] = d.astype(BF)

    stores = []
    to_m[0].end()
    stores.append(norm_rows(0))
    to_m[1].mid()
    with jax.named_scope("gates_back"):
        gates_back(0)
    with jax.named_scope("hidden_back"):
        hidden_back(0)
    h_sum[0].start()
    to_m[1].end()
    stores.append(norm_rows(1))
    for g in to_m:
        g.left()
    pl.semaphore_signal(ready, inc=1, device_id=me.to_core(), device_id_type=MESH)
    h_sum[0].mid()
    with jax.named_scope("gates_back"):
        gates_back(1)
    def columns(ref, f):
        return ref.at[:, pl.ds(f * 512, 512)]

    def quarter(ref, f, cols=1024):
        return ref.at[pl.ds(f // 2 * 256, 256), pl.ds(f % 2 * 1024, cols)]

    def half(pair, f):
        return pair[f // 2].at[pl.ds(f % 2 * 256, 256)]

    near_a, near_b, far_a, far_b, far_c = (net.take(n) for n in (4, 4, 6, 6, 6))

    def in_tok(slot, lower):
        return tok.at[pl.ds(lower * 256, 256), pl.ds(slot * 512, 512)]

    g_down = GradSum(
        net, me, wd, [columns(m_full, f) for f in range(4)],
        (credit.at[0], credit.at[5]), gdown_h, near_a, far_a, in_tok,
    )
    g_gate = GradSum(net, me, wg, [quarter(d_m, f) for f in range(4)], (credit.at[1], credit.at[6]),
        ggate_h, near_b, far_b,
    )
    g_up = GradSum(
        net, me, wu, [half((mixed, dgate), f) for f in range(4)], (credit.at[2], credit.at[7]),
        gup_h, near_a, far_a,
    )
    with jax.named_scope("grad_down"):
        for f in range(4):
            wd[f] = mm_tn(mixed[...], d_m[:, f * 512 : (f + 1) * 512]).astype(BF)
    pl.semaphore_wait(ready, 1)
    g_down.start()
    with jax.named_scope("hidden_back"):
        hidden_back(1)
    h_sum[1].start()

    h_sum[0].cross()
    g_down.add()
    g_down.spread()
    h_sum[1].mid()
    with jax.named_scope("grad_gate"):
        for f in range(4):
            wg[f] = mm_tn(hid[:, f * 512 : (f + 1) * 512], dgate[...]).astype(BF)
    g_down.release()

    def back_to_o(b):
        d_hidden = cot[h_sum[b].at(0, size=CHUNK)].astype(F32) + h_sum[b].result()
        value = ochunk[b]
        r = rms(value)
        to_do[b].start(norm_back(d_hidden, value, r, again[...]).astype(BF))
        ochunk[b] = d_hidden
        return jnp.sum(d_hidden * (value * r), axis=0, keepdims=True)

    ga = back_to_o(0)
    g_gate.start()
    h_sum[1].cross()
    g_down.relay()
    to_do[0].mid()
    with jax.named_scope("grad_up"):
        for f in range(4):
            wu[f] = mm_tn(hid[:, f * 512 : (f + 1) * 512], dup[...]).astype(BF)
    g_gate.add()
    g_up.start()
    ga = ga + back_to_o(1)
    ga_s[me.x] = folded(ga)
    ga_far = [net.put(ga_s.at[me.x], ga_s.at[me.x], me.to_x(k)) for k in (1, 3, 2)]
    g_gate.spread()
    to_do[0].end()

    dk, dv, deltas, dn = gate, up, m_s, acc
    dk[...] = jnp.zeros(dk.shape, F32)
    dv[...] = jnp.zeros(dv.shape, F32)
    dq[...] = jnp.zeros(dq.shape, F32)

    def attended_back(b):
        rows = block_rows(b)
        d = mm_nt(do_full[rows, 0:512], wo[0])
        for f in range(1, 4):
            d += mm_nt(do_full[rows, f * 512 : (f + 1) * 512], wo[f])
        d_att[rows] = d.astype(BF)

    def attend_back(b, start, stop, with_keys):
        rows = block_rows(b)
        q = [qrot[rows, cols] for _, cols in heads]
        e = [d_att[rows, cols] for _, cols in heads]
        delta = [deltas[h, rows] for h, _ in heads]

        def step(j, _):
            allowed = allowed_keys(j, rows)
            scale = key_scale(j)
            raw = [mm_nt(q[h], keys[j, :, cols]) * scale for h, cols in heads]
            d_probs = [mm_nt(e[h], vals[j, :, cols]) for h, cols in heads]
            probs, d_scores = [], []
            for h, _ in heads:
                s = jnp.where(allowed, raw[h] - lse[h, rows], BLOCKED)
                p = jnp.exp2(s)
                probs.append(p.astype(BF))
                d_scores.append((p * (d_probs[h] - delta[h]) * scale).astype(BF))
            for h, cols in heads:
                dq[rows, cols] += mm(d_scores[h], keys[j, :, cols])
                if with_keys:
                    there = pl.ds(pl.multiple_of((j - home) * COLS + h * HEAD, HEAD), HEAD)
                    dk[:, there] += mm_tn(d_scores[h], q[h])
                    dv[:, there] += mm_tn(probs[h], e[h])
            return 0

        with jax.named_scope("attend_back"):
            lax.fori_loop(start, stop, step, 0)

    def keys_back(b):
        rows = block_rows(b)

        def step(_, none, i):
            cols8 = sfar[i, b].T
            k_index = me.c * ROWS + lax.broadcasted_iota(jnp.int32, (BLOCK, ROWS), 1)
            allowed = k_index >= lowfar[i, rows, 0:1]
            scale = key_scale(me.c)
            q = [qfar[i, rows, cols] for _, cols in heads]
            e = [efar[i, rows, cols] for _, cols in heads]
            raw = [mm_nt(q[h], keys[me.c, :, cols]) * scale for h, cols in heads]
            d_probs = [mm_nt(e[h], vals[me.c, :, cols]) for h, cols in heads]
            probs, d_scores = [], []
            for h, _ in heads:
                s = jnp.where(allowed, raw[h] - cols8[:, h : h + 1], BLOCKED)
                p = jnp.exp2(s)
                probs.append(p.astype(BF))
                d = d_probs[h] - cols8[:, 2 + h : 3 + h]
                d_scores.append((p * d * scale).astype(BF))
            for h, cols in heads:
                there = pl.ds(pl.multiple_of(me.core * COLS + h * HEAD, HEAD), HEAD)
                dk[:, there] += mm_tn(d_scores[h], q[h])
                dv[:, there] += mm_tn(probs[h], e[h])
            return 0

        def from_queries(i):
            with jax.named_scope("keys_back"):
                lax.fori_loop(0, 1 - me.zl, functools.partial(step, i=i), 0)

        from_queries(me.core)

        @pl.when(me.zl == 0)
        def _():
            for copy in forward[b]:
                copy.wait_recv()

        from_queries(1 - me.core)

    home, away = me.zl * 2, (1 - me.zl) * 2
    cross, forward = {}, {}

    def send_far(b):
        rows = block_rows(b)
        for h, cols in heads:
            e, a = d_att[rows, cols].astype(F32), att[rows, cols].astype(F32)
            deltas[h, rows] = jnp.sum(e * a, axis=1, keepdims=True)
        cross[b] = [
            net.make(d_att.at[rows], efar.at[me.core, rows], me.to_zl(), cross_far[2 * b]),
            net.make(srow.at[b], sfar.at[me.core, b], me.to_zl(), cross_far[2 * b + 1]),
        ]

        @pl.when(me.zl == 1)
        def _():
            cross[b][0].start()
            four = [lse[0, rows], lse[1, rows], deltas[0, rows], deltas[1, rows]]
            srow[b] = jnp.concatenate(four + four, axis=1).T
            cross[b][1].start()

    def forward_far(b):
        e, s = efar.at[me.core, block_rows(b)], sfar.at[me.core, b]
        forward[b] = [
            net.make(e, e, me.to_core(), on_slots[2 * b]),
            net.make(s, s, me.to_core(), on_slots[2 * b + 1]),
        ]

        @pl.when(me.zl == 0)
        def _():
            for copy in cross[b]:
                copy.wait_recv()
            for copy in forward[b]:
                copy.start()

    def far_left():
        @pl.when(me.zl == 1)
        def _():
            for b in range(2):
                for copy in cross[b]:
                    copy.wait_send()

        @pl.when(me.zl == 0)
        def _():
            for b in range(2):
                for copy in forward[b]:
                    copy.wait_send()

    cross_far, on_slots = kv_slots[:4], kv_slots[4:] + row_slots[:2]
    attended_back(0)
    send_far(0)
    attend_back(0, away, away + 2 * me.zl, False)
    to_do[1].mid()
    g_down.cross()
    tok_copy = net.local(tok_h, tok)
    forward_far(0)
    attend_back(0, home, me.c + 1, True)
    keys_back(0)
    to_do[1].end()
    attended_back(1)
    send_far(1)
    g_down.cross_half()
    g_gate.relay()
    attend_back(1, away, away + 2 * me.zl, False)
    attend_back(1, home, me.c + 1, True)
    g_up.add()
    partner = pl.ds(pl.multiple_of((1 - me.core) * COLS, COLS), COLS)
    own = pl.ds(pl.multiple_of(me.core * COLS, COLS), COLS)

    def key_root(j):
        return jnp.sqrt(as_columns(krow[j])[1] / WIDTH + EPS) * (1.0 / LOG2E)

    d_m[:, :COLS] = (dk[:, partner] * key_root(home + 1 - me.core)).astype(BF)
    d_m[:, COLS : 2 * COLS] = dv[:, partner].astype(BF)
    from_core = dup.at[:, pl.ds(0, 2 * COLS)]
    swap = net.put(d_m.at[:, pl.ds(0, 2 * COLS)], from_core, me.to_core(), row_slots[2])
    with jax.named_scope("rotate_back"):
        dn[0] = two_heads(rotate_back, dq[...] * SCALE, cosine[...], sine[...])
    forward_far(1)
    g_up.spread()
    keys_back(1)
    with jax.named_scope("wait_swap"):
        swap.wait_recv()
    own_root = key_root(me.c)
    d_k = dk[:, own] * own_root + from_core[:, :COLS].astype(F32)
    d_v = dv[:, own] + from_core[:, COLS:].astype(F32)
    with jax.named_scope("rotate_back"):
        dn[1] = two_heads(rotate_back, d_k, cosine[...], sine[...])
        dqkv[:, 2 * COLS :] = d_v.astype(BF)
        scaled_q = dn[0] * qgain[...]
        scaled_k = dn[1] * kgain[...]
        stat2[me.t] = pair_of_sums(scaled_q * qraw[...], scaled_k * kraw[...])
    stats = [
        net.put(stat2.at[me.t], stat2.at[me.t], me.to_t(k), stat_slots[k - 1])
        for k in range(1, 8)
    ]
    scale_q = lax.rsqrt(sums_s[:, 0:1] / WIDTH + EPS)
    scale_k = lax.rsqrt(sums_s[:, 4:5] / WIDTH + EPS)
    for copy in ga_far:
        copy.wait_recv()
    gy[me.f] = jnp.zeros((8, 3 * COLS), F32)
    gy[me.f, :, :COLS] = jnp.sum(ga_s[...], axis=0)
    gy[me.f, :, COLS : 2 * COLS] = folded(gm_s[...])
    gy[me.f, 0:1, 2 * COLS :] = jnp.sum(dn[0] * (qraw[...] * scale_q), axis=0, keepdims=True)
    gy[me.f, 1:2, 2 * COLS :] = jnp.sum(dn[1] * (kraw[...] * scale_k), axis=0, keepdims=True)
    gain_y = [net.put(gy.at[me.f], gy.at[me.f], me.to_y(k)) for k in (1, 3, 2)]
    g_gate.cross()
    g_gate.cross_half()
    with jax.named_scope("grad_output"):
        for g in to_do:
            g.left()
        g_out = GradSum(
            net, me, wo, [mixed.at[pl.ds(f * 128, 128), pl.ds(0, 512)] for f in range(4)],
            (credit.at[3], credit.at[8]), gout_h, near_b, far_b,
        )
        for f in range(4):
            wo[f] = mm_tn(att[...], do_full[:, f * 512 : (f + 1) * 512]).astype(BF)
        g_out.start()
    with jax.named_scope("wait_stats"):
        for copy in stats:
            copy.wait_recv()
    dot_q, dot_k = (d / WIDTH for d in as_columns(jnp.sum(stat2[...], axis=0)))
    dqkv[:, :COLS] = (
        scale_q * scaled_q - qraw[...] * (scale_q * scale_q * scale_q * dot_q)
    ).astype(BF)
    dqkv[:, COLS : 2 * COLS] = (
        scale_k * scaled_k - kraw[...] * (scale_k * scale_k * scale_k * dot_k)
    ).astype(BF)

    for copy in stores:
        copy.wait()
    for s in h_sum:
        s.left()
    x_sum = reduces(part_b, 1)
    to_ig = gathers(m_full)

    def input_back(b):
        rows = block_rows(b)
        for f in range(4):
            for n in range(0, 512, TILE):
                d = mm_nt(dqkv[rows], wqkv[f, n : n + TILE])
                part_b[rows, f * 512 + n : f * 512 + n + TILE] = d.astype(BF)

    def input_grad(b):
        to_ig[b].start((ochunk[b] + x_sum[b].result()).astype(BF))

    with jax.named_scope("input_back"):
        input_back(0)
    x_sum[0].start()
    g_up.relay()
    g_out.add()
    with jax.named_scope("input_back"):
        input_back(1)
    g_qkv = GradSum(
        net, me, wqkv, [quarter(do_full, f, 3 * COLS) for f in range(4)], (credit.at[4], credit.at[9]),
        gqkv_h, near_a, far_c,
    )
    tok_copy.wait()
    with jax.named_scope("grad_qkv"):
        for f in range(4):
            wqkv[f] = mm_tn(tok[:, f * 512 : (f + 1) * 512], dqkv[...]).astype(BF)
    g_qkv.start()
    x_sum[0].mid()
    x_sum[1].start()
    g_out.spread()
    g_qkv.add()
    g_qkv.spread()
    for copy in gain_y:
        copy.wait_recv()
    gz[...] = gy[0] + gy[1] + gy[2] + gy[3]
    gain_z = net.put(gz, gzr, me.to_zl())
    x_sum[0].cross()
    x_sum[1].mid()
    g_up.cross()
    g_out.relay()
    input_grad(0)
    x_sum[1].cross()
    g_up.cross_half()
    g_qkv.relay()
    to_ig[0].mid()
    gain_z.wait_recv()
    gc[...] = gz[...] + gzr[...]
    gain_c = net.put(gc, gcr, me.to_core())
    g_down.finish()
    g_gate.finish()
    input_grad(1)
    g_qkv.cross()
    g_qkv.cross_half()
    g_out.cross()
    g_out.cross_half()
    to_ig[0].end()
    stores = [net.local(m_full.at[block_rows(0)], ig_h.at[block_rows(0)])]
    to_ig[1].mid()
    g_up.finish()
    gain_c.wait_recv()
    total = gc[...] + gcr[...]
    for i in range(8):
        cols = slice(i * COLS, (i + 1) * COLS)
        gains[0:1, cols] = total[i : i + 1, :COLS]
        gains[1:2, cols] = total[i : i + 1, COLS : 2 * COLS]
    for i in range(2):
        gains[2:3, i * COLS : (i + 1) * COLS] = total[i : i + 1, 2 * COLS :]
    stores.append(net.local(gains, gains_h))
    to_ig[1].end()
    stores.append(net.local(m_full.at[block_rows(1)], ig_h.at[block_rows(1)]))
    g_qkv.finish()
    g_out.finish()
    for g in (g_down, g_gate, g_up, g_out, g_qkv):
        g.end()
    for copy in stores:
        copy.wait()
    far_left()
    net.finish()


def sds(*shape, dtype=BF):
    return jax.ShapeDtypeStruct(shape, dtype)


VM = pl.BlockSpec(memory_space=pltpu.VMEM)
ANY = pl.BlockSpec(memory_space=pl.ANY)


def layer(*args):
    def buf(*shape, dtype=BF):
        return pltpu.VMEM(shape, dtype)

    def wide(*shape):
        return pltpu.VMEM(shape, F32)

    reduce_bufs = [
        buf(2, 2, HALF, WIDTH),
        buf(2, 2, CHUNK, WIDTH),
        buf(2, CHUNK, WIDTH),
        buf(2, CHUNK, WIDTH),
    ]
    return pl.pallas_call(
        layer_body,
        name="layer",
        out_shape=[
            sds(ROWS, WIDTH),
            sds(ROWS, WIDTH),
            sds(HIDDEN, 512),
            sds(512, HIDDEN),
            sds(512, HIDDEN),
            sds(512, 3 * COLS),
            sds(COLS, 512),
            sds(8, WIDTH, dtype=F32),
        ],
        out_specs=[ANY] * 8,
        in_specs=[ANY, ANY] + [VM] * 6 + [ANY] * 7,
        scratch_shapes=[
            buf(ROWS, WIDTH),
            buf(ROWS, WIDTH),
            buf(4, 512, 3 * COLS),
            buf(4, COLS, 512),
            buf(4, 512, HIDDEN),
            buf(4, 512, HIDDEN),
            buf(4, HIDDEN, 512),
            buf(ROWS, WIDTH),
            wide(ROWS, HIDDEN),
            wide(ROWS, HIDDEN),
            buf(ROWS, HIDDEN),
            buf(ROWS, HIDDEN),
            buf(ROWS, HIDDEN),
            buf(ROWS, WIDTH),
            buf(ROWS, WIDTH),
            buf(ROWS, WIDTH),
            buf(ROWS, WIDTH),
            buf(ROWS, WIDTH),
            *reduce_bufs,
            *reduce_bufs,
            wide(2, CHUNK, WIDTH),
            wide(ROWS, COLS),
            wide(ROWS, COLS),
            wide(ROWS, 8),
            buf(ROWS, COLS),
            buf(4, ROWS, COLS),
            buf(4, ROWS, COLS),
            buf(ROWS, COLS),
            wide(2, ROWS, 1),
            wide(2, ROWS, 1),
            wide(2, ROWS, 2 * HEAD),
            wide(ROWS, COLS),
            wide(ROWS, HEAD),
            wide(ROWS, HEAD),
            pltpu.VMEM((ROWS, HEAD), jnp.int32),
            pltpu.VMEM((2, ROWS, HEAD), jnp.int32),
            wide(8, 8, HEAD),
            wide(8, 8, HEAD),
            wide(4, 8, HEAD),
            buf(2, ROWS, COLS),
            buf(2, ROWS, COLS),
            wide(2, 2, 8, BLOCK),
            wide(2, 8, BLOCK),
            buf(ROWS, 3 * COLS),
            buf(ROWS, COLS),
            wide(4, 8, COLS),
            wide(1, WIDTH),
            wide(4, 8, 3 * COLS),
            *[wide(8, 3 * COLS) for _ in range(4)],
            wide(8, WIDTH),
            pltpu.SemaphoreType.DMA((SENDS,)),
            pltpu.SemaphoreType.DMA((SLOTS,)),
            pltpu.SemaphoreType.DMA((20,)),
            pltpu.SemaphoreType.REGULAR((10,)),
            pltpu.SemaphoreType.REGULAR,
        ],
        compiler_params=pltpu.CompilerParams(
            collective_id=1, has_side_effects=True, vmem_limit_bytes=63 * MIB
        ),
    )(*args)


ARRAYS = (
    (ROWS, WIDTH),
    (ROWS, WIDTH),
    (HIDDEN, 512),
    (512, HIDDEN),
    (512, HIDDEN),
    (COLS, 512),
    (512, 3 * COLS),
)


def finish_body(*refs):
    arrays, gains, outs, rest = refs[:7], refs[7], refs[8:21], refs[21:]
    ins, few, wides, (in_sem, out_sem) = rest[:7], rest[7], rest[8:15], rest[15:]
    order = (1, 2, 3, 4, 6, 5, 0)
    loads = {}
    for i in order:
        loads[i] = pltpu.make_async_copy(arrays[i], ins[i], in_sem.at[i])
        loads[i].start()
    few_load = pltpu.make_async_copy(gains, few, in_sem.at[7])
    few_load.start()
    stores = []

    def store(src, i):
        stores.append(pltpu.make_async_copy(src, outs[i], out_sem.at[i]))
        stores[-1].start()

    for i in order:
        loads[i].wait()
        if i == 0:
            store(ins[0], 0)
        elif i == 6:
            for k in range(3):
                wides[6][k] = ins[6][:, k * COLS : (k + 1) * COLS].astype(F32)
                store(wides[6].at[k], 6 + k)
        else:
            wides[i][...] = ins[i][...].astype(F32)
            store(wides[i], i)
    few_load.wait()
    for i in range(2):
        store(few.at[pl.ds(i, 1)], 9 + i)
        store(few.at[pl.ds(2, 1), pl.ds(i * COLS, COLS)], 11 + i)
    for copy in stores:
        copy.wait()


def finish(*args):
    outs = [sds(ROWS, WIDTH)] + [sds(*s, dtype=F32) for s in ARRAYS[1:6]]
    outs += [sds(512, COLS, dtype=F32)] * 3
    outs += [sds(1, n, dtype=F32) for n in (WIDTH, WIDTH, COLS, COLS)]
    wides = [(8, 128), *ARRAYS[1:6], (3, 512, COLS)]
    return pl.pallas_call(
        finish_body,
        name="to_float",
        out_shape=outs,
        out_specs=[ANY] * 13,
        in_specs=[ANY] * 8,
        scratch_shapes=[pltpu.VMEM(s, BF) for s in ARRAYS]
        + [pltpu.VMEM((8, WIDTH), F32)]
        + [pltpu.VMEM(s, F32) for s in wides]
        + [pltpu.SemaphoreType.DMA((8,)), pltpu.SemaphoreType.DMA((13,))],
        compiler_params=pltpu.CompilerParams(vmem_limit_bytes=62 * MIB),
    )(*args)


def body(
    tokens, segments, positions, cotangent,
    w_query, w_key, w_value, w_output, w_gate, w_up, w_down,
    query_gain, key_gain, attn_gain, mlp_gain,
):
    del segments
    inverse = ROPE_BASE ** (-np.arange(64, dtype=np.float64) * 2.0 / HEAD)
    freqs = jnp.asarray(np.concatenate([inverse, inverse])[None], F32)
    qgain, kgain, again, mgain = (
        g[None] for g in (query_gain, key_gain, attn_gain, mlp_gain)
    )
    out, d_in, g_down, g_gate, g_up, g_qkv, g_out, gains = layer(
        tokens[0], cotangent[0], positions, freqs, qgain, kgain, again, mgain,
        w_query, w_key, w_value, w_output, w_gate, w_up, w_down,
    )
    out, d_in, g_down, g_gate, g_up, g_out, g_q, g_k, g_v, ga, gm, gq, gk = finish(
        out, d_in, g_down, g_gate, g_up, g_out, g_qkv, gains
    )
    return (
        out[None], d_in[None], g_q, g_k, g_v, g_out, g_gate, g_up, g_down,
        gq[0], gk[0], ga[0], gm[0],
    )


def solution(mesh):
    in_specs = (
        P("fsdp", "context", None),
        P("fsdp", None),
        P("fsdp", None),
        P("fsdp", "context", None),
        P("fsdp", "tensor"),
        P("fsdp", "tensor"),
        P("fsdp", "tensor"),
        P("tensor", "fsdp"),
        P("fsdp", "tensor"),
        P("fsdp", "tensor"),
        P("tensor", "fsdp"),
        P("tensor"),
        P("tensor"),
        P(),
        P(),
    )
    out_specs = (
        P("fsdp", "context", None),
        P("fsdp", "context", None),
        P("fsdp", "tensor"),
        P("fsdp", "tensor"),
        P("fsdp", "tensor"),
        P("tensor", "fsdp"),
        P("fsdp", "tensor"),
        P("fsdp", "tensor"),
        P("tensor", "fsdp"),
        P("tensor"),
        P("tensor"),
        P(),
        P(),
    )
    return jax.shard_map(body, mesh=mesh, in_specs=in_specs, out_specs=out_specs, check_vma=False)
```
